32 devices in a mesh: dp: 16 (over z, x, core), blk: 2 (over y).
Axes of the slice: x: 2, y: 2, z: 4, core: 2. Of those that a mesh axis runs over, the one named last changes fastest.
Arguments:
- tokens: bfloat16 [2, 16, 1024, 768], P(None, 'dp', 'blk'), may hold values from -6 to 6
- segment_ids: int32 [2, 16, 1024], P(None, 'dp'), may hold values from 0 to 1022, as said below
- padding_mask: int32 [2, 16, 1024], P(None, 'dp'), may hold values from 0 to 1, as said below
- qkv_weight: bfloat16 [768, 2304], P('dp'), may hold values from -0.21875 to 0.21875
- proj_weight: bfloat16 [768, 768], P('dp'), may hold values from -0.875 to 0.875
- up_weight: bfloat16 [768, 3072], P('dp'), may hold values from -0.21875 to 0.21875
- down_weight: bfloat16 [3072, 768], P('dp'), may hold values from -0.109375 to 0.109375
- norm_gain: bfloat16 [2, 768], P(None, 'dp'), may hold values from 0.25 to 1.75
- norm_shift: bfloat16 [2, 768], P(None, 'dp'), may hold values from -4 to 4
- qv_bias: bfloat16 [2, 768], P(None, 'dp'), may hold values from -4 to 4
- out_bias: bfloat16 [2, 768], P(None, 'dp'), may hold values from -4 to 4
- up_bias: bfloat16 [3072], P('dp'), may hold values from -6 to 6
- cotangent: bfloat16 [2, 16, 1024, 768], P(None, 'dp', 'blk'), may hold values from -6 to 6
Outputs:
- layer_out: bfloat16 [2, 16, 1024, 768], P(None, 'dp', 'blk')
- grad_tokens: bfloat16 [2, 16, 1024, 768], P(None, 'dp', 'blk')
- grad_qkv: float32 [768, 2304], P('dp')
- grad_proj: float32 [768, 768], P('dp')
- grad_up: float32 [768, 3072], P('dp')
- grad_down: float32 [3072, 768], P('dp')
- grad_gain: float32 [2, 768], P(None, 'dp')
- grad_shift: float32 [2, 768], P(None, 'dp')
- grad_qv_bias: float32 [2, 768], P(None, 'dp')
- grad_out_bias: float32 [2, 768], P(None, 'dp')
- grad_up_bias: float32 [3072], P('dp')
The draws below stay inside these ranges and needn't reach their ends.
Inputs may be any that keep to these rules, and one draw needn't show every extreme that they name: `padding_mask`: in each row the ones form a prefix of at least 768 positions; the first row of the first micro-batch has no padding. `segment_ids`: the ids of a row are 0 at position 0 and rise by 0 or 1 from one position to the next; a rise happens only at a position whose padding_mask is 1 and never at position 512; padded positions keep the row's last id. In the first row of the first micro-batch the id rises at every position where a rise may happen.
All inputs are finite; a program needn't handle non-finite values.
Results may differ from the reference program's by a relative error of at most 0.012.
Values may be sent and summed in bfloat16 or wider, within the bound.
No kernel may reach another device: no remote copies, remote signals or barrier semaphores. Data moves between devices by JAX's collectives and lax.ppermute only.
A program may use at most 256 MiB of HBM per device.

```python
import math
import jax
import jax.numpy as jnp
from jax import lax

D = 768
HD = 64
FF = 3072
SEQ = 1024
MICRO = 2
SEQ_DEV = 512
ROWS = 16


def live_lengths(key):
    pad_count = jax.random.randint(key, (MICRO, ROWS), 0, SEQ // 4 + 1)
    pad_count = pad_count.at[0, 0].set(0)
    return SEQ - pad_count


def draw_padding_mask(key, part):
    live = live_lengths(key)
    positions = jnp.arange(SEQ, dtype=jnp.int32)
    return (positions[None, None, :] < live[:, :, None]).astype(jnp.int32)


def draw_segment_ids(key, part):
    live = live_lengths(key)
    key = jax.random.fold_in(key, 7)
    roll_key = jax.random.fold_in(key, 1)
    style_key = jax.random.fold_in(key, 2)
    rolls = jax.random.randint(roll_key, (MICRO, ROWS, SEQ), 0, 16)
    rolls = rolls.at[0, 0].set(0)
    style = jax.random.randint(style_key, (MICRO, ROWS), 0, 8)
    style = style.at[0, 0].set(7).at[0, 1].set(0).at[MICRO - 1, 1].set(1)
    positions = jnp.arange(SEQ, dtype=jnp.int32)
    usable = (positions[None, None, :] >= 1) & (positions[None, None, :] < live[:, :, None]) & (positions[None, None, :] != SEQ_DEV)
    window = (positions >= SEQ // 8) & (positions < SEQ - SEQ // 8)
    quiet = (style[:, :, None] == 0) | (style[:, :, None] == 1) & window[None, None, :]
    starts = jnp.where(usable & (rolls == 0) & jnp.logical_not(quiet), 1, 0).astype(jnp.int32)
    return jnp.cumsum(starts, axis=-1).astype(jnp.int32)


def with_spikes(drawn, own_key, source, target, shards_of, factor):
    owner, partner = [(jnp.arange(drawn.shape[axis_at]) // (drawn.shape[axis_at] // shards_of)).reshape([-1 if axis == axis_at else 1 for axis in range(drawn.ndim)]) for axis_at in (source, target)]
    chosen = jax.random.permutation(own_key, shards_of)[partner]
    strong = (owner == chosen) | (owner == (partner + shards_of // 2) % shards_of)
    return jnp.where(strong, factor * drawn, drawn)


def block_levels(own_key, shape, pieces, low, high):
    gain, own = 1.0, jax.random.fold_in(own_key, 6)
    for axis_at, parts in pieces:
        steps = jnp.exp(jax.random.uniform(jax.random.fold_in(own, axis_at), (parts,), jnp.float32, low / len(pieces), high / len(pieces)))
        gain = gain * jnp.repeat(steps, shape[axis_at] // parts).reshape([-1 if axis == axis_at else 1 for axis in range(len(shape))])
    return gain


def centred(stream_key, extent, scale, limit, shards=(), kind=jnp.bfloat16):
    factor_of = block_levels(stream_key, extent, shards, -0.22, 0.18) if shards else 1.0
    array = jax.random.normal(stream_key, extent, jnp.float32) * scale * factor_of
    return jnp.minimum(jnp.maximum(array, -limit), limit).astype(kind)


def noise_with(key, shape, deviation, limit, shards, heavy, kind=jnp.bfloat16):
    array = deviation * jax.random.normal(key, shape, jnp.float32)
    if shards:
        array = array * block_levels(key, shape, shards, -0.22, 0.18)
    return jnp.clip(with_spikes(array, jax.random.fold_in(key, 3), *heavy), -limit, limit).astype(kind)


def setup_inputs(seed: int = 0) -> dict:
    key_list = jax.random.split(jax.random.key(seed), 14)
    tokens = centred(key_list[0], (MICRO, ROWS, SEQ, D), 1.0, 6.0, ((1, 16), (2, 2)))
    segment_ids = draw_segment_ids(jax.random.fold_in(key_list[13], 71), 0)
    padding_mask = draw_padding_mask(jax.random.fold_in(key_list[13], 71), 0)
    qkv_weight = centred(key_list[3], (D, 3 * D), D ** -0.5, 0.21875, ((0, 16),))
    proj_weight = centred(key_list[4], (D, D), (D // 16) ** -0.5, 0.875, ((0, 16),))
    up_weight = centred(key_list[5], (D, FF), D ** -0.5, 0.21875, ((0, 16),))
    down_weight = centred(key_list[6], (FF, D), FF ** -0.5, 0.109375, ((0, 16),))
    norm_gain = jnp.clip(1.0 + 0.15 * jax.random.normal(key_list[7], (2, D), jnp.float32), 0.25, 1.75).astype(jnp.bfloat16)
    norm_shift = centred(key_list[8], (2, D), 0.3, 4.0, ((1, 16),))
    qv_bias = centred(key_list[9], (2, D), 0.3, 4.0, ((1, 16),))
    out_bias = centred(key_list[10], (2, D), 0.3, 4.0, ((1, 16),))
    up_bias = centred(key_list[11], (FF,), 0.5, 6.0, ((0, 16),))
    cotangent = noise_with(key_list[12], (MICRO, ROWS, SEQ, D), 1.0, 6.0, ((1, 16), (2, 2)), (1, 3, 16, 2.0))
    return dict(tokens=tokens, segment_ids=segment_ids, padding_mask=padding_mask, qkv_weight=qkv_weight, proj_weight=proj_weight, up_weight=up_weight, down_weight=down_weight, norm_gain=norm_gain, norm_shift=norm_shift, qv_bias=qv_bias, out_bias=out_bias, up_bias=up_bias, cotangent=cotangent)


highest = lax.Precision.HIGHEST

@jax.custom_vjp
def low(v):
    return lax.optimization_barrier(v.astype(jnp.bfloat16)).astype(jnp.float32)

@jax.custom_vjp
def low_back(v):
    return v

def low_keep(v):
    return (low(v), None)

def low_pass(kept, grad):
    return (grad,)

def back_keep(v):
    return (v, None)

def back_low(kept, grad):
    return (low(grad),)
low.defvjp(low_keep, low_pass)
low_back.defvjp(back_keep, back_low)

def layer_norm(source, gain_row, shift_row):
    center = source - lax.optimization_barrier(jnp.mean(source, axis=-1, keepdims=True))
    spread = lax.optimization_barrier(jnp.mean(center * center, axis=-1, keepdims=True))
    return center * lax.rsqrt(spread + 1e-05) * gain_row + shift_row

def gelu_exact(pre_act):
    return jax.nn.gelu(pre_act, approximate=False)

def forward(params, tok_block, seg_block, pad_block):
    qkv_w, proj_w, up_w, down_w, gains, shifts, qv_b, out_b, up_b = params
    row_count, seq_len, model_width = tok_block.shape
    head_count = model_width // HD
    norm_in = low(layer_norm(tok_block, gains[0], shifts[0]))
    joined = jnp.einsum('rsd,de->rse', norm_in, qkv_w, precision=highest)
    queries = low_back(low(joined[..., :model_width] + qv_b[0]))
    key_proj = low_back(low(joined[..., model_width:2 * model_width]))
    value_proj = low_back(low(joined[..., 2 * model_width:] + qv_b[1]))
    query_heads = queries.reshape(row_count, seq_len, head_count, HD)
    key_heads = key_proj.reshape(row_count, seq_len, head_count, HD)
    value_heads = value_proj.reshape(row_count, seq_len, head_count, HD)
    scores = jnp.einsum('rqhd,rkhd->rhqk', query_heads, key_heads, precision=highest) * 0.125
    allowed = (seg_block[:, :, None] == seg_block[:, None, :]) & (pad_block[:, None, :] == 1)
    scores = low_back(jnp.where(allowed[:, None], scores, -1e+30))
    row_top = lax.optimization_barrier(jnp.max(scores, axis=-1, keepdims=True))
    shifted_exp = jnp.exp(scores - row_top)
    attn_probs = shifted_exp / lax.optimization_barrier(jnp.sum(shifted_exp, axis=-1, keepdims=True))
    probs_low = low(attn_probs)
    attended = jnp.einsum('rhqk,rkhd->rqhd', probs_low, value_heads, precision=highest)
    attended = low_back(low(attended.reshape(row_count, seq_len, model_width)))
    branch = low_back(jnp.einsum('rsd,de->rse', attended, proj_w, precision=highest) + out_b[0])
    residual_mid = tok_block + branch
    norm_mid = low(layer_norm(residual_mid, gains[1], shifts[1]))
    pre_act = low_back(jnp.einsum('rsd,df->rsf', norm_mid, up_w, precision=highest) + up_b)
    act_low = low(gelu_exact(pre_act))
    ffn_out = low_back(jnp.einsum('rsf,fd->rsd', act_low, down_w, precision=highest) + out_b[1])
    return residual_mid + ffn_out

def reference(tokens, segment_ids, padding_mask, qkv_weight, proj_weight, up_weight, down_weight, norm_gain, norm_shift, qv_bias, out_bias, up_bias, cotangent):
    params = tuple((item.astype(jnp.float32) for item in (qkv_weight, proj_weight, up_weight, down_weight, norm_gain, norm_shift, qv_bias, out_bias, up_bias)))
    all_rows = MICRO * ROWS
    group_size = math.gcd(all_rows, max(1, 4096 // SEQ))
    group_count = all_rows // group_size
    tok_groups = tokens.astype(jnp.float32).reshape(group_count, group_size, SEQ, D)
    cot_groups = cotangent.astype(jnp.float32).reshape(group_count, group_size, SEQ, D)
    seg_groups = segment_ids.reshape(group_count, group_size, SEQ)
    pad_groups = padding_mask.reshape(group_count, group_size, SEQ)

    def step(running, slices):
        tok_block, seg_block, pad_block, cot_block = slices
        result, pull_back = jax.vjp(lambda prm, tok: forward(prm, tok, seg_block, pad_block), params, tok_block)
        gradients, d_tokens = pull_back(cot_block)
        running = jax.tree.map(lambda first_set, second_set: first_set + second_set, running, gradients)
        return (running, (result.astype(jnp.bfloat16), d_tokens.astype(jnp.bfloat16)))
    start_sums = jax.tree.map(jnp.zeros_like, params)
    sums, (out_groups, dtok_groups) = lax.scan(step, start_sums, (tok_groups, seg_groups, pad_groups, cot_groups))
    layer_out = out_groups.reshape(MICRO, ROWS, SEQ, D)
    grad_tokens = dtok_groups.reshape(MICRO, ROWS, SEQ, D)
    return (layer_out, grad_tokens, sums[0], sums[1], sums[2], sums[3], sums[4], sums[5], sums[6], sums[7], sums[8])
```

```python
import functools

import jax
import jax.numpy as jnp
import numpy as np
from jax import lax
from jax.experimental import pallas as pl
from jax.experimental.pallas import tpu as pltpu
from jax.sharding import PartitionSpec as P

HD = 64
BLOCKS = 16
NT = (((1,), (1,)), ((), ()))
TN = (((0,), (0,)), ((), ()))
F32 = jnp.float32
BF16 = jnp.bfloat16
ANY = pl.BlockSpec(memory_space=pl.ANY)
SMEM = pl.BlockSpec(memory_space=pltpu.SMEM)
VMEM_LIMIT = 60 << 20
MASKED = -1e30


def dot(a, b, dims=(((1,), (0,)), ((), ()))):
    return lax.dot_general(a, b, dims, preferred_element_type=F32)


def cost(us):
    return pl.CostEstimate(flops=int(us * 1.1e9), bytes_accessed=1 << 20, transcendentals=0)


def full(shape):
    return pl.BlockSpec(shape, lambda *_: (0,) * len(shape))


def params():
    return pltpu.CompilerParams(vmem_limit_bytes=VMEM_LIMIT)


def norm_stats(x):
    mean = jnp.mean(x, axis=1, keepdims=True)
    center = x - mean
    rstd = lax.rsqrt(jnp.mean(center * center, axis=1, keepdims=True) + 1e-05)
    return center * rstd, rstd


def norm_back(e, nhat, rstd):
    return (
        e - jnp.mean(e, axis=1, keepdims=True) - nhat * jnp.mean(e * nhat, axis=1, keepdims=True)
    ) * rstd


def row_sum(x):
    return jnp.sum(x, axis=0, keepdims=True)


def attn_forward_body(quad, block, idx, *refs):
    first = quad == 0
    if first:
        (own, sib, tok_own, tok_rx, sq, sk, q_o, k_o, v_o, att_o, li_o, e_o, w_o, nrm_o, small_o,
         w_s, s_s, kk, vv, aa, sem) = refs
    else:
        (own, sib, nrm_i, small_i, sq, sk, q_o, k_o, v_o, att_o, li_o, e_o, w_o,
         w_s, kk, vv, aa, sem) = refs
    seq = sq.shape[0]
    half = seq // 2
    n_part = own.shape[0]
    pair = pl.program_id(0)

    @pl.when(pair == 0)
    def _():
        copies = []
        for j, part in enumerate((own, sib)):
            for t in range(n_part):
                at = idx[j * n_part + t]
                copies.append(
                    pltpu.make_async_copy(
                        part.at[t, pl.ds(48 * quad, 48), :], w_s.at[at], sem.at[0, j * n_part + t]
                    )
                )
                if first:
                    copies.append(
                        pltpu.make_async_copy(
                            part.at[t, pl.ds(144, 16), :],
                            s_s.at[j * n_part + t],
                            sem.at[1, j * n_part + t],
                        )
                    )
        for c in copies:
            c.start()
        for c in copies:
            c.wait()
        weight = w_s[...].reshape(768, 768)
        w_o[...] = weight
        if first:
            small = jnp.zeros((16, 768), F32)
            for t in range(2 * n_part):
                small = small + s_s[t].astype(F32)
            small_o[...] = small
            gain, shift = small[0:1], small[2:3]
            for src, where in ((tok_own, idx[16]), (tok_rx, 1 - idx[16])):
                base = pl.multiple_of(where * half, half)
                for i in range(0, half, block):
                    nhat, _rstd = norm_stats(src[i : i + block, :].astype(F32))
                    nrm_o[pl.ds(base + i, block), :] = (nhat * gain + shift).astype(BF16)
            nrm = nrm_o
            bq, bv = small[4:5, 0:256], small[5:6, 0:256]
        else:
            nrm = nrm_i
            cols = slice(256 * quad, 256 * quad + 256)
            bq, bv = small_i[4:5, cols], small_i[5:6, cols]
        for i in range(0, seq, block):
            rows = slice(i, i + block)
            joined = dot(nrm[rows, :], weight)
            q_o[rows, :] = (joined[:, 0:256] + bq).astype(BF16)
            k_o[rows, :] = joined[:, 256:512].astype(BF16)
            v_o[rows, :] = (joined[:, 512:768] + bv).astype(BF16)

    lanes = pl.ds(pl.multiple_of(pair * 128, 128), 128)
    head = lax.broadcasted_iota(jnp.int32, (seq, 128), 1) // HD
    k_pair, v_pair = k_o[:, lanes], v_o[:, lanes]
    zero, one = jnp.zeros((seq, 128), BF16), jnp.ones((seq, 128), BF16)
    for h in range(2):
        mine = head == h
        kk[h, :, 0:128] = jnp.where(mine, k_pair, zero)
        kk[h, :, 128:256] = sk[...]
        vv[h, :, 0:128] = jnp.where(mine, v_pair, zero)
        vv[h, :, 128:256] = jnp.where(mine, one, zero)
    aa[:, 0:128] = q_o[:, lanes] * BF16(0.125)
    aa[:, 128:256] = sq[...]
    for i in range(0, seq, block):
        rows = slice(i, i + block)
        acc = None
        for h in range(2):
            s = dot(aa[rows, :], kk[h], NT)
            e = jnp.exp(s - jnp.max(s, axis=1, keepdims=True)).astype(BF16)
            e_o[h, rows, :] = e
            o = dot(e, vv[h])
            acc = o if acc is None else acc + o
        inverse = 1.0 / acc[:, 128:256]
        li_o[rows, :] = inverse
        att_o[rows, :] = (acc[:, 0:128] * inverse).astype(BF16)


def attn_forward(quad, idx, own, sib, rows_in, sq, sk):
    seq = sq.shape[0]
    sds = jax.ShapeDtypeStruct
    first = quad == 0
    pair_block = pl.BlockSpec((seq, 128), lambda p: (0, p))
    quad_block = full((seq, 256))
    out_shape = [
        sds((seq, 256), BF16),
        sds((seq, 256), BF16),
        sds((seq, 256), BF16),
        sds((seq, 256), BF16),
        sds((seq, 256), F32),
        sds((4, seq, seq), BF16),
        sds((768, 768), BF16),
    ]
    out_specs = [
        quad_block, quad_block, quad_block, pair_block, pair_block,
        pl.BlockSpec((2, seq, seq), lambda p: (p, 0, 0)), full((768, 768)),
    ]
    scratch = [pltpu.VMEM((BLOCKS, 48, 768), BF16)]
    if first:
        out_shape += [sds((seq, 768), BF16), sds((16, 768), F32)]
        out_specs += [full((seq, 768)), full((16, 768))]
        scratch += [pltpu.VMEM((BLOCKS, 16, 768), BF16)]
    scratch += [
        pltpu.VMEM((2, seq, 256), BF16),
        pltpu.VMEM((2, seq, 256), BF16),
        pltpu.VMEM((seq, 256), BF16),
        pltpu.SemaphoreType.DMA((2, BLOCKS)),
    ]
    return pl.pallas_call(
        functools.partial(attn_forward_body, quad, 256),
        grid=(2,),
        in_specs=[SMEM, ANY, ANY]
        + [full(r.shape) for r in rows_in]
        + [full(sq.shape), full(sk.shape)],
        out_specs=out_specs,
        out_shape=out_shape,
        scratch_shapes=scratch,
        compiler_params=params(),
        cost_estimate=cost(11),
    )(idx, own, sib, *rows_in, sq, sk)


def ffn_body(
    block, idx, gathered, att0, att1, att2, tok_own, tok_rx, cot_own, cot_rx, small,
    lo_mine, lo_theirs, dmid_o, datt_o, g_mine, g_theirs, sums_o,
    up_s, dn_s, proj_s, att_s, mid_s, nm_s, nmt_s, cot_s, act_s, dp_s, oacc, dacc, dbr_s, gbuf, gproj,
    wsem, psem, gsem, gpsem,
):
    c = pl.program_id(0)
    n_c = pl.num_programs(0)
    slot = lax.rem(c, 2)
    seq = mid_s.shape[0]
    half = seq // 2
    core = idx[17]

    def weight_copies(chunk, s):
        rows_up = pl.ds(pl.multiple_of(chunk * 96, 48), 48)
        rows_dn = pl.ds(pl.multiple_of(chunk * 96 + 48, 48), 48)
        return (
            pltpu.make_async_copy(gathered.at[:, rows_up, :], up_s.at[s], wsem.at[s, 0]),
            pltpu.make_async_copy(gathered.at[:, rows_dn, :], dn_s.at[s], wsem.at[s, 1]),
        )

    def grad_copies(chunk, s):
        rows = pl.ds(pl.multiple_of(chunk * 96, 96), 96)
        return (
            pltpu.make_async_copy(gbuf.at[s, :, core], g_mine.at[:, rows, :], gsem.at[s, 0]),
            pltpu.make_async_copy(gbuf.at[s, :, 1 - core], g_theirs.at[:, rows, :], gsem.at[s, 1]),
        )

    @pl.when(c == 0)
    def _():
        for copy in weight_copies(0, 0):
            copy.start()
        proj_copy = pltpu.make_async_copy(gathered.at[:, pl.ds(384, 48), :], proj_s, psem)
        proj_copy.start()
        for src, where in ((tok_own, idx[16]), (tok_rx, 1 - idx[16])):
            base = pl.multiple_of(where * half, half)
            mid_s[pl.ds(base, half), :] = src[...].astype(F32)
        for src, where in ((cot_own, idx[16]), (cot_rx, 1 - idx[16])):
            base = pl.multiple_of(where * half, half)
            cot_s[pl.ds(base, half), :] = src[...]
        for j, a in enumerate((att0, att1, att2)):
            att_s[:, 256 * j : 256 * j + 256] = a[...]
        proj_copy.wait()
        proj = proj_s[...].reshape(768, 768)
        for i in range(0, seq, block):
            rows = slice(i, i + block)
            mid = mid_s[rows, :] + (dot(att_s[rows, :], proj) + small[6:7])
            mid_s[rows, :] = mid
            nhat, _rstd = norm_stats(mid)
            nm_s[rows, :] = (nhat * small[1:2] + small[3:4]).astype(BF16)
        nmt_s[...] = nm_s[...].T
        oacc[...] = jnp.zeros_like(oacc)
        dacc[...] = jnp.zeros_like(dacc)

    for copy in weight_copies(c, slot):
        copy.wait()

    @pl.when(c + 1 < n_c)
    def _():
        for copy in weight_copies(c + 1, 1 - slot):
            copy.start()

    up = up_s[slot].reshape(768, 768)
    dn = dn_s[slot].reshape(768, 768)
    bias = small[pl.ds(8 + c, 1), :]
    bias_sum = None
    for i in range(0, seq, block):
        rows = slice(i, i + block)
        pre = dot(nm_s[rows, :], up) + bias
        cdf = 0.5 * (1.0 + lax.erf(pre * 0.7071067811865476))
        act = (pre * cdf).astype(BF16)
        act_s[rows, :] = act
        oacc[rows, :] += dot(act, dn)
        slope = cdf + pre * (jnp.exp(pre * pre * -0.5) * 0.3989422804014327)
        d_pre = (dot(cot_s[rows, :], dn, NT) * slope).astype(BF16)
        dp_s[rows, :] = d_pre
        part = row_sum(d_pre.astype(F32))
        bias_sum = part if bias_sum is None else bias_sum + part
        dacc[rows, :] += dot(d_pre, up, NT)
    sums_o[pl.ds(8 + c, 1), :] = bias_sum

    @pl.when(c >= 2)
    def _():
        for copy in grad_copies(c - 2, slot):
            copy.wait()

    g_up = dot(nmt_s[...], dp_s[...]).astype(BF16).reshape(BLOCKS // 2, 2, 48, 768)
    gbuf[slot, :, :, 0:48, :] = g_up
    g_dn = dot(act_s[...], cot_s[...], TN).astype(BF16).reshape(BLOCKS // 2, 2, 48, 768)
    gbuf[slot, :, :, 48:96, :] = g_dn
    for copy in grad_copies(c, slot):
        copy.start()

    @pl.when(c == n_c - 1)
    def _():
        proj = proj_s[...].reshape(768, 768)
        gain_sum = shift_sum = bout_sum = bdown_sum = None
        for i in range(0, seq, block):
            rows = slice(i, i + block)
            mid = mid_s[rows, :]
            cot = cot_s[rows, :].astype(F32)
            d_nm = dacc[rows, :]
            nhat, rstd = norm_stats(mid)
            d_mid = cot + norm_back(d_nm * small[1:2], nhat, rstd)
            dmid_o[rows, :] = d_mid
            d_branch = d_mid.astype(BF16)
            dbr_s[rows, :] = d_branch
            datt_o[rows, :] = dot(d_branch, proj, NT).astype(BF16)
            parts = [row_sum(d_nm * nhat), row_sum(d_nm), row_sum(d_branch.astype(F32)), row_sum(cot)]
            if gain_sum is None:
                gain_sum, shift_sum, bout_sum, bdown_sum = parts
            else:
                gain_sum, shift_sum = gain_sum + parts[0], shift_sum + parts[1]
                bout_sum, bdown_sum = bout_sum + parts[2], bdown_sum + parts[3]
        sums_o[0:8, :] = jnp.concatenate(
            [jnp.zeros_like(gain_sum), gain_sum, jnp.zeros_like(gain_sum), shift_sum,
             jnp.zeros_like(gain_sum), jnp.zeros_like(gain_sum), bout_sum, bdown_sum], axis=0)
        sums_o[12:16, :] = jnp.zeros((4, 768), F32)
        for dst, where in ((lo_mine, idx[16]), (lo_theirs, 1 - idx[16])):
            base = pl.multiple_of(where * half, half)
            for i in range(0, half, block):
                rows = pl.ds(base + i, block)
                dst[i : i + block, :] = (mid_s[rows, :] + (oacc[rows, :] + small[7:8])).astype(BF16)
        gproj[...] = dot(att_s[...], dbr_s[...], TN).astype(BF16).reshape(BLOCKS // 2, 2, 48, 768)
        last = [
            pltpu.make_async_copy(gproj.at[:, core], g_mine.at[:, pl.ds(384, 48), :], gpsem.at[0]),
            pltpu.make_async_copy(gproj.at[:, 1 - core], g_theirs.at[:, pl.ds(384, 48), :], gpsem.at[1]),
        ]
        for copy in last:
            copy.start()
        for copy in grad_copies(c - 1, 1 - slot):
            copy.wait()
        for copy in grad_copies(c, slot):
            copy.wait()
        for copy in last:
            copy.wait()


def ffn(idx, gathered, atts, tok_own, tok_rx, cot_own, cot_rx, small):
    seq = 2 * tok_own.shape[0]
    sds = jax.ShapeDtypeStruct
    v = pltpu.VMEM
    half = tok_own.shape
    rows, frows = v((seq, 768), BF16), v((seq, 768), F32)
    return pl.pallas_call(
        functools.partial(ffn_body, 256),
        grid=(4,),
        in_specs=[SMEM, ANY] + [full((seq, 256))] * 3 + [full(half)] * 4 + [full((16, 768))],
        out_specs=[full(half), full(half), full((seq, 768)), full((seq, 768)), ANY, ANY, full((16, 768))],
        out_shape=[
            sds(half, BF16), sds(half, BF16), sds((seq, 768), F32), sds((seq, 768), BF16),
            sds((BLOCKS // 2, 432, 768), BF16), sds((BLOCKS // 2, 432, 768), BF16), sds((16, 768), F32),
        ],
        scratch_shapes=[
            v((2, BLOCKS, 48, 768), BF16), v((2, BLOCKS, 48, 768), BF16), v((BLOCKS, 48, 768), BF16),
            rows, frows, rows, v((768, seq), BF16), rows, rows, rows, frows, frows, rows,
            v((2, BLOCKS // 2, 2, 96, 768), BF16), v((BLOCKS // 2, 2, 48, 768), BF16),
            pltpu.SemaphoreType.DMA((2, 2)), pltpu.SemaphoreType.DMA, pltpu.SemaphoreType.DMA((2, 2)),
            pltpu.SemaphoreType.DMA((2,)),
        ],
        compiler_params=params(),
        cost_estimate=cost(50),
    )(idx, gathered, *atts, tok_own, tok_rx, cot_own, cot_rx, small)


def attn_backward_body(quad, last, block, idx, *refs):
    (q_i, k_i, v_i, o_i, do_i, li_i, e_i, w_i, nrm_i) = refs[:9]
    refs = refs[9:]
    if quad > 0:
        dni_i, refs = refs[0], refs[1:]
    if quad == 1:
        refs = refs[2:]
    if last:
        (tok_own, tok_rx, dmid_i, small, sums_i, b0, b1, gt_mine, gt_theirs, g_mine, g_theirs) = refs[:11]
        refs = refs[11:]
    else:
        (dni_o, b_o, g_mine, g_theirs) = refs[:4]
        refs = refs[4:]
    (vv, kk, dd, qm, dm, dkt, dvt, dj, nt, gbuf, sem) = refs[:11]
    pair = pl.program_id(0)
    seq = q_i.shape[0]
    half = seq // 2
    core = idx[17]
    zero = jnp.zeros((seq, 128), BF16)
    lane = lax.broadcasted_iota(jnp.int32, (seq, 128), 1)

    @pl.when(pair == 0)
    def _():
        nt[...] = nrm_i[...].T

    d_out = do_i[...].astype(F32) * li_i[...]
    d_low = d_out.astype(BF16)
    prod = d_out * o_i[...].astype(F32)
    extra = jnp.zeros((seq, 128), F32)
    for h in range(2):
        mine = (lane // HD) == h
        delta = jnp.sum(jnp.where(mine, prod, 0.0), axis=1, keepdims=True)
        high = delta.astype(BF16).astype(F32)
        extra = jnp.where(lane == 2 * h, -high, extra)
        extra = jnp.where(lane == 2 * h + 1, high - delta, extra)
        vv[h, :, 0:128] = jnp.where(mine, v_i[...], zero)
        vv[h, :, 128:256] = jnp.where((lane // 2) == h, 1.0, 0.0).astype(BF16)
        kk[h] = jnp.where(mine, k_i[...], zero)
        qm[h] = jnp.where(mine, q_i[...], zero).astype(F32).T.astype(BF16)
        dm[h] = jnp.where(mine, d_low, zero).astype(F32).T.astype(BF16)
    dd[:, 0:128] = d_low
    dd[:, 128:256] = extra.astype(BF16)
    base = pl.multiple_of(pair * 128, 128)
    for i in range(0, seq, block):
        rows = slice(i, i + block)
        dq = None
        for h in range(2):
            dp = dot(dd[rows, :], vv[h], NT)
            e = e_i[h, rows, :]
            ds = dp.astype(BF16) * e
            t = dot(ds, kk[h])
            dq = t if dq is None else dq + t
            a, b = dot(qm[h, :, rows], ds), dot(dm[h, :, rows], e)
            if i == 0 and h == 0:
                dkt[...], dvt[...] = a, b
            else:
                dkt[...] += a
                dvt[...] += b
        dj[rows, pl.ds(base, 128)] = (dq * 0.125).astype(BF16)
    dj[:, pl.ds(base + 256, 128)] = (dkt[...] * 0.125).T.astype(BF16)
    dj[:, pl.ds(base + 512, 128)] = dvt[...].T.astype(BF16)

    @pl.when(pair == 1)
    def _():
        g_rows = 48 if last else 48
        gbuf[:, :, 0:48, :] = dot(nt[...], dj[...]).astype(BF16).reshape(BLOCKS // 2, 2, 48, 768)
        bq, bv = row_sum(dj[:, 0:256].astype(F32)), row_sum(dj[:, 512:768].astype(F32))
        dst_rows = pl.ds(48 * quad, g_rows) if not last else pl.ds(0, 48)
        copies = [
            pltpu.make_async_copy(gbuf.at[:, core], g_mine.at[:, dst_rows, :], sem.at[0]),
            pltpu.make_async_copy(gbuf.at[:, 1 - core], g_theirs.at[:, dst_rows, :], sem.at[1]),
        ]
        for copy in copies:
            copy.start()
        weight = w_i[...]
        if not last:
            b_o[...] = jnp.concatenate([bq, bv, jnp.zeros((6, 256), F32)], axis=0)
            for i in range(0, seq, block):
                rows = slice(i, i + block)
                d_ni = dot(dj[rows, :], weight, NT)
                dni_o[rows, :] = d_ni if quad == 0 else dni_i[rows, :] + d_ni
        else:
            sbuf = refs[11]
            gain = small[0:1]
            gain_sum = shift_sum = None
            for src, dst, where in ((tok_rx, gt_theirs, 1 - idx[16]), (tok_own, gt_mine, idx[16])):
                start = pl.multiple_of(where * half, half)
                for i in range(0, half, block):
                    rows = pl.ds(start + i, block)
                    d_ni = dni_i[rows, :] + dot(dj[rows, :], weight, NT)
                    nhat, rstd = norm_stats(src[i : i + block, :].astype(F32))
                    grad = dmid_i[rows, :] + norm_back(d_ni * gain, nhat, rstd)
                    dst[i : i + block, :] = grad.astype(BF16)
                    parts = [row_sum(d_ni * nhat), row_sum(d_ni)]
                    if gain_sum is None:
                        gain_sum, shift_sum = parts
                    else:
                        gain_sum, shift_sum = gain_sum + parts[0], shift_sum + parts[1]
            sums = sums_i[...]
            row = lax.broadcasted_iota(jnp.int32, (16, 768), 0)
            sums = jnp.where(row == 0, gain_sum, sums)
            sums = jnp.where(row == 2, shift_sum, sums)
            sums = jnp.where(row == 4, jnp.concatenate([b0[0:1, :], b1[0:1, :], bq], axis=1), sums)
            sums = jnp.where(row == 5, jnp.concatenate([b0[1:2, :], b1[1:2, :], bv], axis=1), sums)
            low = sums.astype(BF16)
            for t in range(BLOCKS // 2):
                sbuf[t] = low
            more = [
                pltpu.make_async_copy(sbuf, g_mine.at[:, pl.ds(48, 16), :], sem.at[2]),
                pltpu.make_async_copy(sbuf, g_theirs.at[:, pl.ds(48, 16), :], sem.at[3]),
            ]
            for copy in more:
                copy.start()
            for copy in more:
                copy.wait()
        for copy in copies:
            copy.wait()


def attn_backward(quad, idx, heads, d_att, nrm, d_ni=None, grads=None, tail=None):
    last = tail is not None
    q, k, v, att, li, e, w = heads
    seq = q.shape[0]
    half = (seq // 2, 768)
    sds = jax.ShapeDtypeStruct
    vm = pltpu.VMEM
    pair_block = pl.BlockSpec((seq, 128), lambda p: (0, p))
    args = [idx, q, k, v, att, d_att, li, e, w, nrm]
    in_specs = [SMEM] + [pair_block] * 4 + [pl.BlockSpec((seq, 128), lambda p: (0, 2 * quad + p)), pair_block]
    in_specs += [pl.BlockSpec((2, seq, seq), lambda p: (p, 0, 0)), full(w.shape), full(nrm.shape)]
    alias = {}
    if quad > 0:
        args.append(d_ni)
        in_specs.append(full(d_ni.shape))
        if not last:
            alias[len(args) - 1] = 0
    if quad == 1:
        for j, g in enumerate(grads):
            args.append(g)
            in_specs.append(ANY)
            alias[len(args) - 1] = 2 + j
    if last:
        args += list(tail)
        in_specs += [full(a.shape) for a in tail]
        g_rows = 64
        out_shape = [sds(half, BF16), sds(half, BF16)]
        out_specs = [full(half), full(half)]
    else:
        g_rows = 96
        out_shape = [sds((seq, 768), F32), sds((8, 256), F32)]
        out_specs = [full((seq, 768)), full((8, 256))]
    out_shape += [sds((BLOCKS // 2, g_rows, 768), BF16)] * 2
    out_specs += [ANY, ANY]
    scratch = [
        vm((2, seq, 256), BF16), vm((2, seq, 128), BF16), vm((seq, 256), BF16), vm((2, 128, seq), BF16),
        vm((2, 128, seq), BF16), vm((128, seq), F32), vm((128, seq), F32), vm((seq, 768), BF16),
        vm((768, seq), BF16), vm((BLOCKS // 2, 2, 48, 768), BF16), pltpu.SemaphoreType.DMA((4,)),
    ]
    if last:
        scratch.append(vm((BLOCKS // 2, 16, 768), BF16))
    return pl.pallas_call(
        functools.partial(attn_backward_body, quad, last, 256),
        grid=(2,),
        in_specs=in_specs,
        out_specs=out_specs,
        out_shape=out_shape,
        scratch_shapes=scratch,
        input_output_aliases=alias,
        compiler_params=params(),
        cost_estimate=cost(15),
    )(*args)


def chip_cycle(n_chips):
    rows = n_chips // 2
    return [2 * i for i in range(rows)] + [2 * i + 1 for i in reversed(range(rows))]


def chip_shift(n_chips, step):
    order = chip_cycle(n_chips)
    return [
        (2 * order[i] + core, 2 * order[(i + step) % n_chips] + core)
        for i in range(n_chips)
        for core in (0, 1)
    ]


def core_swap(n_dev):
    return [(i, i ^ 1) for i in range(n_dev)]


def ring_gather(x, n_chips):
    ahead, behind = [x], [x]
    for t in range(n_chips // 2):
        ahead.append(lax.ppermute(ahead[-1], "dp", chip_shift(n_chips, 1)))
        if t < n_chips - 1 - n_chips // 2:
            behind.append(lax.ppermute(behind[-1], "dp", chip_shift(n_chips, -1)))
    own = jnp.stack(ahead + behind[1:])
    return own, lax.ppermute(own, "dp", core_swap(2 * n_chips))


def ring_order(n_chips):
    order = chip_cycle(n_chips)
    table = np.zeros((2 * n_chips, 2 * n_chips), np.int32)
    steps = list(range(0, -(n_chips // 2) - 1, -1)) + list(range(1, n_chips - n_chips // 2))
    for chip in range(n_chips):
        pos = order.index(chip)
        chips = [order[(pos + s) % n_chips] for s in steps]
        for core in (0, 1):
            table[2 * chip + core] = [2 * q + core for q in chips] + [2 * q + 1 - core for q in chips]
    return table


def ring_reduce(mine, theirs, n_chips):
    order = np.array(chip_cycle(n_chips), np.int32)
    position = np.argsort(order).astype(np.int32)
    pos = jnp.asarray(position)[lax.axis_index("dp") // 2]
    sib = lax.ppermute(theirs, "dp", core_swap(2 * n_chips))

    def term(step):
        chip = jnp.asarray(order)[lax.rem(pos + step + n_chips, n_chips)]
        a = lax.dynamic_index_in_dim(mine, chip, 0, keepdims=False)
        b = lax.dynamic_index_in_dim(sib, chip, 0, keepdims=False)
        return a.astype(F32) + b.astype(F32)

    ahead_steps, behind_steps = n_chips // 2, n_chips - 1 - n_chips // 2
    ahead = term(ahead_steps).astype(BF16)
    behind = term(-behind_steps).astype(BF16)
    for t in range(ahead_steps - 1, -1, -1):
        ahead = lax.ppermute(ahead, "dp", chip_shift(n_chips, 1))
        if t > 0:
            ahead = (ahead.astype(F32) + term(t)).astype(BF16)
        if t < behind_steps:
            behind = lax.ppermute(behind, "dp", chip_shift(n_chips, -1))
            if t > 0:
                behind = (behind.astype(F32) + term(-t)).astype(BF16)
    return (term(0) + ahead.astype(F32) + behind.astype(F32)).astype(BF16)


def swap_rows(x):
    return lax.ppermute(x, "blk", [(0, 1), (1, 0)])


def pack_weights(qkv_w, proj_w, up_w, down_w, shares):
    r = qkv_w.shape[0] // shares
    qkv = qkv_w.reshape(shares, r, 3, 3, 256).transpose(0, 3, 1, 2, 4).reshape(shares, 3, r, 768)
    up = up_w.reshape(shares, r, BLOCKS, 4, 48).transpose(0, 3, 1, 2, 4).reshape(shares, 4, 1, r, 768)
    down = down_w.reshape(shares, 4, 1, r, 768)
    up_down = jnp.concatenate([up, down], axis=2).reshape(shares, 8, r, 768)
    proj = proj_w.reshape(shares, 1, r, 768)
    return qkv, jnp.concatenate([up_down, proj], axis=1)


def pack_small(gains, shifts, qv_b, out_b, up_b, at):
    width = gains.shape[1]
    flat = jnp.concatenate([gains, shifts, qv_b, out_b, up_b.reshape(4, width)], axis=0)
    return lax.dynamic_update_slice(jnp.zeros((16, 768), flat.dtype), flat, (0, at))


def unpack_qkv(blocks, rows):
    return blocks.reshape(3, rows, 3, 256).transpose(1, 2, 0, 3).reshape(rows, 2304)


def unpack_up(blocks, rows):
    return blocks.reshape(4, rows, BLOCKS, 48).transpose(1, 2, 0, 3).reshape(rows, 3072)


def shards(tokens, segment_ids, padding_mask, qkv_weight, proj_weight, up_weight, down_weight,
           norm_gain, norm_shift, qv_bias, out_bias, up_bias, cotangent):
    n_dev = lax.axis_size("dp")
    dp, blk = lax.axis_index("dp"), lax.axis_index("blk")
    ring = n_dev == BLOCKS
    n_chips = BLOCKS // 2

    def pick(pair, which):
        return lax.dynamic_index_in_dim(pair, which, 0, keepdims=False)

    tok_own, tok_rx = pick(tokens, blk)[0], swap_rows(pick(tokens, 1 - blk)[0])
    cot_own = pick(cotangent, blk)[0]
    seg, pad = pick(segment_ids, blk)[0], pick(padding_mask, blk)[0]
    lanes = jnp.arange(128, dtype=jnp.int32)[None, :]
    code = jnp.where(lanes < 32, seg[:, None] // 32 == lanes, seg[:, None] % 32 + 32 == lanes)
    seg_q = code.astype(BF16)
    allowed = code & (pad[:, None] == 1)
    seg_k = jnp.where(allowed | (lanes >= 64), 0.0, MASKED).astype(BF16)

    if ring:
        qkv_blocks, rest = pack_weights(qkv_weight, proj_weight, up_weight, down_weight, 1)
        small = pack_small(norm_gain, norm_shift, qv_bias, out_bias, up_bias, 48 * dp)
        first = jnp.concatenate([qkv_blocks.reshape(144, 768), small], axis=0)
        own, sib = ring_gather(first, n_chips)
        gathered = lax.all_gather(rest.reshape(432, 768), "dp", axis=0)
        order = jnp.asarray(ring_order(n_chips))[dp]
        core = lax.rem(dp, 2)
    else:
        whole = [lax.all_gather(w, "dp", axis=0, tiled=True)
                 for w in (qkv_weight, proj_weight, up_weight, down_weight)]
        qkv_blocks, rest = pack_weights(*whole, BLOCKS)
        vectors = [lax.all_gather(w, "dp", axis=1, tiled=True)
                   for w in (norm_gain, norm_shift, qv_bias, out_bias)]
        hidden = lax.all_gather(up_bias, "dp", axis=0, tiled=True)
        hidden = hidden.reshape(BLOCKS, 4, 48).transpose(1, 0, 2).reshape(-1)
        small = pack_small(*vectors, hidden, 0)
        small = jnp.concatenate([small[None], jnp.zeros((BLOCKS - 1, 16, 768), BF16)], axis=0)
        first = jnp.concatenate([qkv_blocks.reshape(BLOCKS, 144, 768), small], axis=1)
        own, sib = first[:n_chips], first[n_chips:]
        gathered = rest.reshape(BLOCKS, 432, 768)
        order = jnp.arange(BLOCKS, dtype=jnp.int32)
        core = jnp.int32(0)
    idx = jnp.concatenate([order, jnp.stack([blk, core]).astype(jnp.int32)])
    cot_rx = swap_rows(pick(cotangent, 1 - blk)[0])

    outs = attn_forward(0, idx, own, sib, (tok_own, tok_rx), seg_q, seg_k)
    heads, nrm, small_all = [outs[:7]], outs[7], outs[8]
    for quad in (1, 2):
        heads.append(attn_forward(quad, idx, own, sib, (nrm, small_all), seg_q, seg_k))
    lo_mine, lo_theirs, d_mid, d_att, g_mine, g_theirs, sums = ffn(
        idx, gathered, [h[3] for h in heads], tok_own, tok_rx, cot_own, cot_rx, small_all)
    lo_rx = swap_rows(lo_theirs)

    d_ni, b0, q_mine, q_theirs = attn_backward(0, idx, heads[0], d_att, nrm)
    d_ni, b1, q_mine, q_theirs = attn_backward(1, idx, heads[1], d_att, nrm, d_ni, (q_mine, q_theirs))
    gt_mine, gt_theirs, l_mine, l_theirs = attn_backward(
        2, idx, heads[2], d_att, nrm, d_ni, tail=(tok_own, tok_rx, d_mid, small_all, sums, b0, b1))
    gt_rx = swap_rows(gt_theirs)

    def together(own_half, other_half):
        swapped = blk == 1
        return jnp.stack([jnp.where(swapped, other_half, own_half),
                          jnp.where(swapped, own_half, other_half)])[:, None]

    layer_out, grad_tokens = together(lo_mine, lo_rx), together(gt_mine, gt_rx)

    if ring:
        done = [ring_reduce(a, b, n_chips) for a, b in ((g_mine, g_theirs), (q_mine, q_theirs), (l_mine, l_theirs))]
        done = [d.astype(F32) + swap_rows(d).astype(F32) for d in done]
        r = 48
        ffn_blocks = done[0][0:384].reshape(4, 2, r, 768)
        g_up, g_down, g_proj = ffn_blocks[:, 0], ffn_blocks[:, 1].reshape(4 * r, 768), done[0][384:432]
        g_qkv = jnp.stack([done[1][0:48], done[1][48:96], done[2][0:48]])
        g_small = lax.dynamic_slice_in_dim(done[2][48:64], 48 * dp, 48, 1)
        width = 48
        return (layer_out, grad_tokens, unpack_qkv(g_qkv, r), g_proj, unpack_up(g_up, r), g_down,
                g_small[0:2], g_small[2:4], g_small[4:6], g_small[6:8], g_small[8:12].reshape(4 * width))

    def whole_sum(a, b):
        return jnp.stack([a, b], axis=1).reshape(BLOCKS, a.shape[1], 768)

    def scatter(x, dim):
        part = lax.psum_scatter(x, "dp", scatter_dimension=dim, tiled=True)
        return lax.psum(part.astype(BF16), "blk").astype(F32)

    g_ffn, g_q, g_l = whole_sum(g_mine, g_theirs), whole_sum(q_mine, q_theirs), whole_sum(l_mine, l_theirs)
    ffn_blocks = g_ffn[:, 0:384].reshape(BLOCKS, 4, 2, 48, 768).transpose(1, 2, 0, 3, 4).reshape(4, 2, 768, 768)
    g_up = unpack_up(ffn_blocks[:, 0], 768)
    g_down = ffn_blocks[:, 1].reshape(4, BLOCKS, 48, 768).transpose(1, 0, 2, 3).reshape(3072, 768)
    g_proj = g_ffn[:, 384:432].reshape(768, 768)
    g_qkv = jnp.stack([g_q[:, 0:48].reshape(768, 768), g_q[:, 48:96].reshape(768, 768),
                       g_l[:, 0:48].reshape(768, 768)])
    g_small = l_mine[0, 48:64].astype(F32)
    g_bias = g_small[8:12].reshape(4, BLOCKS, 48).transpose(1, 0, 2).reshape(-1)
    big = [scatter(g.astype(F32), 0) for g in (unpack_qkv(g_qkv, 768), g_proj, g_up, g_down)]
    return (layer_out, grad_tokens, *big,
            *[scatter(g_small[2 * i : 2 * i + 2], 1) for i in range(4)], scatter(g_bias, 0))


def solution(mesh):
    rows = P(None, "dp", "blk", None)
    return jax.shard_map(
        shards,
        mesh=mesh,
        in_specs=(rows, P(None, "dp", None), P(None, "dp", None)) + (P("dp", None),) * 4
        + (P(None, "dp"),) * 4 + (P("dp"), rows),
        out_specs=(rows, rows) + (P("dp", None),) * 4 + (P(None, "dp"),) * 4 + (P("dp"),),
        check_vma=False,
    )
```

```python
import functools

import jax
import jax.numpy as jnp
import numpy as np
from jax import lax
from jax.experimental import pallas as pl
from jax.experimental.pallas import tpu as pltpu
from jax.sharding import PartitionSpec as P

HD = 64
BLOCKS = 16
NT = (((1,), (1,)), ((), ()))
TN = (((0,), (0,)), ((), ()))
F32 = jnp.float32
BF16 = jnp.bfloat16
ANY = pl.BlockSpec(memory_space=pl.ANY)
SMEM = pl.BlockSpec(memory_space=pltpu.SMEM)
VMEM_LIMIT = 60 << 20
MASKED = -1e30


def dot(a, b, dims=(((1,), (0,)), ((), ()))):
    return lax.dot_general(a, b, dims, preferred_element_type=F32)


def cost(us):
    return pl.CostEstimate(flops=int(us * 1.1e9), bytes_accessed=1 << 20, transcendentals=0)


def full(shape):
    return pl.BlockSpec(shape, lambda *_: (0,) * len(shape))


def params():
    return pltpu.CompilerParams(vmem_limit_bytes=VMEM_LIMIT)


def norm_stats(x):
    mean = jnp.mean(x, axis=1, keepdims=True)
    center = x - mean
    rstd = lax.rsqrt(jnp.mean(center * center, axis=1, keepdims=True) + 1e-05)
    return center * rstd, rstd


def norm_back(e, nhat, rstd):
    return (
        e - jnp.mean(e, axis=1, keepdims=True) - nhat * jnp.mean(e * nhat, axis=1, keepdims=True)
    ) * rstd


def row_sum(x):
    return jnp.sum(x, axis=0, keepdims=True)


def send_copies(idx, buf, rows, mine, near, far, sem):
    core = idx[17]
    copies = []
    for slot in range(BLOCKS // 2):
        chip = idx[18 + slot]
        theirs = near.at[slot] if slot < 2 else far.at[slot - 2]
        copies.append(pltpu.make_async_copy(buf.at[chip, core], mine.at[slot, rows, :], sem.at[0, slot]))
        copies.append(pltpu.make_async_copy(buf.at[chip, 1 - core], theirs.at[rows, :], sem.at[1, slot]))
    return copies


def send_shapes(rows):
    return [jax.ShapeDtypeStruct((n, rows, 768), BF16) for n in (BLOCKS // 2, 2, BLOCKS // 2 - 2)]


def attn_forward_body(quad, block, idx, *refs):
    first = quad == 0
    parts, refs = refs[:BLOCKS], refs[BLOCKS:]
    if first:
        (tok_own, tok_rx, sq, sk, q_o, k_o, v_o, att_o, li_o, e_o, w_o, nrm_o, small_o,
         w_s, s_s, kk, vv, aa, sem) = refs
    else:
        (nrm_i, small_i, sq, sk, q_o, k_o, v_o, att_o, li_o, e_o, w_o,
         w_s, kk, vv, aa, sem) = refs
    seq = sq.shape[0]
    half = seq // 2
    pair = pl.program_id(0)

    @pl.when(pair == 0)
    def _():
        copies = []
        for t, part in enumerate(parts):
            copies.append(
                pltpu.make_async_copy(part.at[pl.ds(48 * quad, 48), :], w_s.at[idx[t]], sem.at[0, t])
            )
            if first:
                copies.append(
                    pltpu.make_async_copy(part.at[pl.ds(144, 16), :], s_s.at[t], sem.at[1, t])
                )
        for c in copies:
            c.start()
        for c in copies:
            c.wait()
        weight = w_s[...].reshape(768, 768)
        w_o[...] = weight
        if first:
            small = jnp.zeros((16, 768), F32)
            for t in range(BLOCKS):
                small = small + s_s[t].astype(F32)
            small_o[...] = small
            gain, shift = small[0:1], small[2:3]
            for src, where in ((tok_own, idx[16]), (tok_rx, 1 - idx[16])):
                base = pl.multiple_of(where * half, half)
                for i in range(0, half, block):
                    nhat, _rstd = norm_stats(src[i : i + block, :].astype(F32))
                    nrm_o[pl.ds(base + i, block), :] = (nhat * gain + shift).astype(BF16)
            nrm = nrm_o
            bq, bv = small[4:5, 0:256], small[5:6, 0:256]
        else:
            nrm = nrm_i
            cols = slice(256 * quad, 256 * quad + 256)
            bq, bv = small_i[4:5, cols], small_i[5:6, cols]
        for i in range(0, seq, block):
            rows = slice(i, i + block)
            joined = dot(nrm[rows, :], weight)
            q_o[rows, :] = (joined[:, 0:256] + bq).astype(BF16)
            k_o[rows, :] = joined[:, 256:512].astype(BF16)
            v_o[rows, :] = (joined[:, 512:768] + bv).astype(BF16)

    lanes = pl.ds(pl.multiple_of(pair * 128, 128), 128)
    head = lax.broadcasted_iota(jnp.int32, (seq, 128), 1) // HD
    k_pair, v_pair = k_o[:, lanes], v_o[:, lanes]
    zero, one = jnp.zeros((seq, 128), BF16), jnp.ones((seq, 128), BF16)
    for h in range(2):
        mine = head == h
        kk[h, :, 0:128] = jnp.where(mine, k_pair, zero)
        kk[h, :, 128:256] = sk[...]
        vv[h, :, 0:128] = jnp.where(mine, v_pair, zero)
        vv[h, :, 128:256] = jnp.where(mine, one, zero)
    aa[:, 0:128] = q_o[:, lanes] * BF16(0.125)
    aa[:, 128:256] = sq[...]
    for i in range(0, seq, block):
        rows = slice(i, i + block)
        acc = None
        for h in range(2):
            s = dot(aa[rows, :], kk[h], NT)
            e = jnp.exp(s - jnp.max(s, axis=1, keepdims=True)).astype(BF16)
            e_o[h, rows, :] = e
            o = dot(e, vv[h])
            acc = o if acc is None else acc + o
        inverse = 1.0 / acc[:, 128:256]
        li_o[rows, :] = inverse
        att_o[rows, :] = (acc[:, 0:128] * inverse).astype(BF16)


def attn_forward(quad, idx, parts, rows_in, sq, sk):
    seq = sq.shape[0]
    sds = jax.ShapeDtypeStruct
    first = quad == 0
    pair_block = pl.BlockSpec((seq, 128), lambda p: (0, p))
    quad_block = full((seq, 256))
    out_shape = [
        sds((seq, 256), BF16),
        sds((seq, 256), BF16),
        sds((seq, 256), BF16),
        sds((seq, 256), BF16),
        sds((seq, 256), F32),
        sds((4, seq, seq), BF16),
        sds((768, 768), BF16),
    ]
    out_specs = [
        quad_block, quad_block, quad_block, pair_block, pair_block,
        pl.BlockSpec((2, seq, seq), lambda p: (p, 0, 0)), full((768, 768)),
    ]
    scratch = [pltpu.VMEM((BLOCKS, 48, 768), BF16)]
    if first:
        out_shape += [sds((seq, 768), BF16), sds((16, 768), F32)]
        out_specs += [full((seq, 768)), full((16, 768))]
        scratch += [pltpu.VMEM((BLOCKS, 16, 768), BF16)]
    scratch += [
        pltpu.VMEM((2, seq, 256), BF16),
        pltpu.VMEM((2, seq, 256), BF16),
        pltpu.VMEM((seq, 256), BF16),
        pltpu.SemaphoreType.DMA((2, BLOCKS)),
    ]
    return pl.pallas_call(
        functools.partial(attn_forward_body, quad, 256),
        grid=(2,),
        in_specs=[SMEM] + [ANY] * BLOCKS
        + [full(r.shape) for r in rows_in]
        + [full(sq.shape), full(sk.shape)],
        out_specs=out_specs,
        out_shape=out_shape,
        scratch_shapes=scratch,
        compiler_params=params(),
        cost_estimate=cost(11),
    )(idx, *parts, *rows_in, sq, sk)


def ffn_body(
    block, idx, *refs
):
    parts, refs = refs[:BLOCKS], refs[BLOCKS:]
    ffn_steps(block, idx, parts, *refs)


def ffn_steps(
    block, idx, parts, att0, att1, att2, tok_own, tok_rx, cot_own, cot_rx, small,
    lo_mine, lo_theirs, dmid_o, datt_o, g_mine, g_near, g_far, sums_o,
    up_s, dn_s, proj_s, att_s, mid_s, nm_s, nmt_s, cot_s, act_s, dp_s, oacc, dacc, dbr_s, gbuf, gproj,
    wsem, psem, gsem, gpsem,
):
    c = pl.program_id(0)
    n_c = pl.num_programs(0)
    slot = lax.rem(c, 2)
    seq = mid_s.shape[0]
    half = seq // 2

    def weight_copies(chunk, s):
        rows_up = pl.ds(pl.multiple_of(chunk * 96, 48), 48)
        rows_dn = pl.ds(pl.multiple_of(chunk * 96 + 48, 48), 48)
        return [
            pltpu.make_async_copy(part.at[rows, :], buf.at[s, idx[t]], wsem.at[s, j, t])
            for t, part in enumerate(parts)
            for j, (rows, buf) in enumerate(((rows_up, up_s), (rows_dn, dn_s)))
        ]

    def grad_copies(chunk, s):
        rows = pl.ds(pl.multiple_of(chunk * 96, 96), 96)
        return send_copies(idx, gbuf.at[s], rows, g_mine, g_near, g_far, gsem.at[s])

    @pl.when(c == 0)
    def _():
        for copy in weight_copies(0, 0):
            copy.start()
        proj_copies = [
            pltpu.make_async_copy(part.at[pl.ds(384, 48), :], proj_s.at[idx[t]], psem.at[t])
            for t, part in enumerate(parts)
        ]
        for copy in proj_copies:
            copy.start()
        for src, where in ((tok_own, idx[16]), (tok_rx, 1 - idx[16])):
            base = pl.multiple_of(where * half, half)
            mid_s[pl.ds(base, half), :] = src[...].astype(F32)
        for src, where in ((cot_own, idx[16]), (cot_rx, 1 - idx[16])):
            base = pl.multiple_of(where * half, half)
            cot_s[pl.ds(base, half), :] = src[...]
        for j, a in enumerate((att0, att1, att2)):
            att_s[:, 256 * j : 256 * j + 256] = a[...]
        for copy in proj_copies:
            copy.wait()
        proj = proj_s[...].reshape(768, 768)
        for i in range(0, seq, block):
            rows = slice(i, i + block)
            mid = mid_s[rows, :] + (dot(att_s[rows, :], proj) + small[6:7])
            mid_s[rows, :] = mid
            nhat, _rstd = norm_stats(mid)
            nm_s[rows, :] = (nhat * small[1:2] + small[3:4]).astype(BF16)
        nmt_s[...] = nm_s[...].T
        oacc[...] = jnp.zeros_like(oacc)
        dacc[...] = jnp.zeros_like(dacc)

    for copy in weight_copies(c, slot):
        copy.wait()

    @pl.when(c + 1 < n_c)
    def _():
        for copy in weight_copies(c + 1, 1 - slot):
            copy.start()

    up = up_s[slot].reshape(768, 768)
    dn = dn_s[slot].reshape(768, 768)
    bias = small[pl.ds(8 + c, 1), :]
    bias_sum = None
    for i in range(0, seq, block):
        rows = slice(i, i + block)
        pre = dot(nm_s[rows, :], up) + bias
        cdf = 0.5 * (1.0 + lax.erf(pre * 0.7071067811865476))
        act = (pre * cdf).astype(BF16)
        act_s[rows, :] = act
        oacc[rows, :] += dot(act, dn)
        slope = cdf + pre * (jnp.exp(pre * pre * -0.5) * 0.3989422804014327)
        d_pre = (dot(cot_s[rows, :], dn, NT) * slope).astype(BF16)
        dp_s[rows, :] = d_pre
        part = row_sum(d_pre.astype(F32))
        bias_sum = part if bias_sum is None else bias_sum + part
        dacc[rows, :] += dot(d_pre, up, NT)
    sums_o[pl.ds(8 + c, 1), :] = bias_sum

    @pl.when(c >= 2)
    def _():
        for copy in grad_copies(c - 2, slot):
            copy.wait()

    g_up = dot(nmt_s[...], dp_s[...]).astype(BF16).reshape(BLOCKS // 2, 2, 48, 768)
    gbuf[slot, :, :, 0:48, :] = g_up
    g_dn = dot(act_s[...], cot_s[...], TN).astype(BF16).reshape(BLOCKS // 2, 2, 48, 768)
    gbuf[slot, :, :, 48:96, :] = g_dn
    for copy in grad_copies(c, slot):
        copy.start()

    @pl.when(c == n_c - 1)
    def _():
        proj = proj_s[...].reshape(768, 768)
        gain_sum = shift_sum = bout_sum = bdown_sum = None
        for i in range(0, seq, block):
            rows = slice(i, i + block)
            mid = mid_s[rows, :]
            cot = cot_s[rows, :].astype(F32)
            d_nm = dacc[rows, :]
            nhat, rstd = norm_stats(mid)
            d_mid = cot + norm_back(d_nm * small[1:2], nhat, rstd)
            dmid_o[rows, :] = d_mid
            d_branch = d_mid.astype(BF16)
            dbr_s[rows, :] = d_branch
            datt_o[rows, :] = dot(d_branch, proj, NT).astype(BF16)
            parts = [row_sum(d_nm * nhat), row_sum(d_nm), row_sum(d_branch.astype(F32)), row_sum(cot)]
            if gain_sum is None:
                gain_sum, shift_sum, bout_sum, bdown_sum = parts
            else:
                gain_sum, shift_sum = gain_sum + parts[0], shift_sum + parts[1]
                bout_sum, bdown_sum = bout_sum + parts[2], bdown_sum + parts[3]
        sums_o[0:8, :] = jnp.concatenate(
            [jnp.zeros_like(gain_sum), gain_sum, jnp.zeros_like(gain_sum), shift_sum,
             jnp.zeros_like(gain_sum), jnp.zeros_like(gain_sum), bout_sum, bdown_sum], axis=0)
        sums_o[12:16, :] = jnp.zeros((4, 768), F32)
        for dst, where in ((lo_mine, idx[16]), (lo_theirs, 1 - idx[16])):
            base = pl.multiple_of(where * half, half)
            for i in range(0, half, block):
                rows = pl.ds(base + i, block)
                dst[i : i + block, :] = (mid_s[rows, :] + (oacc[rows, :] + small[7:8])).astype(BF16)
        gproj[...] = dot(att_s[...], dbr_s[...], TN).astype(BF16).reshape(BLOCKS // 2, 2, 48, 768)
        last = send_copies(idx, gproj, pl.ds(384, 48), g_mine, g_near, g_far, gpsem)
        for copy in last:
            copy.start()
        for copy in grad_copies(c - 1, 1 - slot):
            copy.wait()
        for copy in grad_copies(c, slot):
            copy.wait()
        for copy in last:
            copy.wait()


def ffn(idx, parts, atts, tok_own, tok_rx, cot_own, cot_rx, small):
    seq = 2 * tok_own.shape[0]
    sds = jax.ShapeDtypeStruct
    v = pltpu.VMEM
    half = tok_own.shape
    rows, frows = v((seq, 768), BF16), v((seq, 768), F32)
    return pl.pallas_call(
        functools.partial(ffn_body, 256),
        grid=(4,),
        in_specs=[SMEM] + [ANY] * BLOCKS + [full((seq, 256))] * 3 + [full(half)] * 4 + [full((16, 768))],
        out_specs=[full(half), full(half), full((seq, 768)), full((seq, 768)), ANY, ANY, ANY, full((16, 768))],
        out_shape=[
            sds(half, BF16), sds(half, BF16), sds((seq, 768), F32), sds((seq, 768), BF16),
            *send_shapes(432), sds((16, 768), F32),
        ],
        scratch_shapes=[
            v((2, BLOCKS, 48, 768), BF16), v((2, BLOCKS, 48, 768), BF16), v((BLOCKS, 48, 768), BF16),
            rows, frows, rows, v((768, seq), BF16), rows, rows, rows, frows, frows, rows,
            v((2, BLOCKS // 2, 2, 96, 768), BF16), v((BLOCKS // 2, 2, 48, 768), BF16),
            pltpu.SemaphoreType.DMA((2, 2, BLOCKS)), pltpu.SemaphoreType.DMA((BLOCKS,)),
            pltpu.SemaphoreType.DMA((2, 2, BLOCKS // 2)), pltpu.SemaphoreType.DMA((2, BLOCKS // 2)),
        ],
        compiler_params=params(),
        cost_estimate=cost(50),
    )(idx, *parts, *atts, tok_own, tok_rx, cot_own, cot_rx, small)


def attn_backward_body(quad, last, block, idx, *refs):
    (q_i, k_i, v_i, o_i, do_i, li_i, e_i, w_i, nrm_i) = refs[:9]
    refs = refs[9:]
    if quad > 0:
        dni_i, refs = refs[0], refs[1:]
        refs = refs[3:]
    if last:
        (tok_own, tok_rx, dmid_i, small, sums_i, b0, b1, gt_mine, gt_theirs, *sends) = refs[:12]
        refs = refs[12:]
    else:
        (dni_o, b_o, *sends) = refs[:5]
        refs = refs[5:]
    (vv, kk, dd, qm, dm, dkt, dvt, dj, nt, gbuf, sem) = refs[:11]
    pair = pl.program_id(0)
    seq = q_i.shape[0]
    half = seq // 2
    zero = jnp.zeros((seq, 128), BF16)
    lane = lax.broadcasted_iota(jnp.int32, (seq, 128), 1)

    @pl.when(pair == 0)
    def _():
        nt[...] = nrm_i[...].T

    d_out = do_i[...].astype(F32) * li_i[...]
    d_low = d_out.astype(BF16)
    prod = d_out * o_i[...].astype(F32)
    extra = jnp.zeros((seq, 128), F32)
    for h in range(2):
        mine = (lane // HD) == h
        delta = jnp.sum(jnp.where(mine, prod, 0.0), axis=1, keepdims=True)
        high = delta.astype(BF16).astype(F32)
        extra = jnp.where(lane == 2 * h, -high, extra)
        extra = jnp.where(lane == 2 * h + 1, high - delta, extra)
        vv[h, :, 0:128] = jnp.where(mine, v_i[...], zero)
        vv[h, :, 128:256] = jnp.where((lane // 2) == h, 1.0, 0.0).astype(BF16)
        kk[h] = jnp.where(mine, k_i[...], zero)
        qm[h] = jnp.where(mine, q_i[...], zero).astype(F32).T.astype(BF16)
        dm[h] = jnp.where(mine, d_low, zero).astype(F32).T.astype(BF16)
    dd[:, 0:128] = d_low
    dd[:, 128:256] = extra.astype(BF16)
    base = pl.multiple_of(pair * 128, 128)
    for i in range(0, seq, block):
        rows = slice(i, i + block)
        dq = None
        for h in range(2):
            dp = dot(dd[rows, :], vv[h], NT)
            e = e_i[h, rows, :]
            ds = dp.astype(BF16) * e
            t = dot(ds, kk[h])
            dq = t if dq is None else dq + t
            a, b = dot(qm[h, :, rows], ds), dot(dm[h, :, rows], e)
            if i == 0 and h == 0:
                dkt[...], dvt[...] = a, b
            else:
                dkt[...] += a
                dvt[...] += b
        dj[rows, pl.ds(base, 128)] = (dq * 0.125).astype(BF16)
    dj[:, pl.ds(base + 256, 128)] = (dkt[...] * 0.125).T.astype(BF16)
    dj[:, pl.ds(base + 512, 128)] = dvt[...].T.astype(BF16)

    @pl.when(pair == 1)
    def _():
        gbuf[...] = dot(nt[...], dj[...]).astype(BF16).reshape(BLOCKS // 2, 2, 48, 768)
        bq, bv = row_sum(dj[:, 0:256].astype(F32)), row_sum(dj[:, 512:768].astype(F32))
        copies = send_copies(idx, gbuf, pl.ds(48 * quad, 48), *sends, sem.at[0])
        for copy in copies:
            copy.start()
        weight = w_i[...]
        if not last:
            b_o[...] = jnp.concatenate([bq, bv, jnp.zeros((6, 256), F32)], axis=0)
            for i in range(0, seq, block):
                rows = slice(i, i + block)
                d_ni = dot(dj[rows, :], weight, NT)
                dni_o[rows, :] = d_ni if quad == 0 else dni_i[rows, :] + d_ni
        else:
            sbuf = refs[11]
            gain = small[0:1]
            gain_sum = shift_sum = None
            for src, dst, where in ((tok_rx, gt_theirs, 1 - idx[16]), (tok_own, gt_mine, idx[16])):
                start = pl.multiple_of(where * half, half)
                for i in range(0, half, block):
                    rows = pl.ds(start + i, block)
                    d_ni = dni_i[rows, :] + dot(dj[rows, :], weight, NT)
                    nhat, rstd = norm_stats(src[i : i + block, :].astype(F32))
                    grad = dmid_i[rows, :] + norm_back(d_ni * gain, nhat, rstd)
                    dst[i : i + block, :] = grad.astype(BF16)
                    parts = [row_sum(d_ni * nhat), row_sum(d_ni)]
                    if gain_sum is None:
                        gain_sum, shift_sum = parts
                    else:
                        gain_sum, shift_sum = gain_sum + parts[0], shift_sum + parts[1]
            sums = sums_i[...]
            row = lax.broadcasted_iota(jnp.int32, (16, 768), 0)
            sums = jnp.where(row == 0, gain_sum, sums)
            sums = jnp.where(row == 2, shift_sum, sums)
            sums = jnp.where(row == 4, jnp.concatenate([b0[0:1, :], b1[0:1, :], bq], axis=1), sums)
            sums = jnp.where(row == 5, jnp.concatenate([b0[1:2, :], b1[1:2, :], bv], axis=1), sums)
            low = sums.astype(BF16)
            for t in range(BLOCKS // 2):
                sbuf[t, 0], sbuf[t, 1] = low, low
            more = send_copies(idx, sbuf, pl.ds(144, 16), *sends, sem.at[1])
            for copy in more:
                copy.start()
            for copy in more:
                copy.wait()
        for copy in copies:
            copy.wait()


def attn_backward(quad, idx, heads, d_att, nrm, d_ni=None, grads=None, tail=None):
    last = tail is not None
    q, k, v, att, li, e, w = heads
    seq = q.shape[0]
    half = (seq // 2, 768)
    sds = jax.ShapeDtypeStruct
    vm = pltpu.VMEM
    pair_block = pl.BlockSpec((seq, 128), lambda p: (0, p))
    args = [idx, q, k, v, att, d_att, li, e, w, nrm]
    in_specs = [SMEM] + [pair_block] * 4 + [pl.BlockSpec((seq, 128), lambda p: (0, 2 * quad + p)), pair_block]
    in_specs += [pl.BlockSpec((2, seq, seq), lambda p: (p, 0, 0)), full(w.shape), full(nrm.shape)]
    alias = {}
    if quad > 0:
        args.append(d_ni)
        in_specs.append(full(d_ni.shape))
        if not last:
            alias[len(args) - 1] = 0
        for j, g in enumerate(grads):
            args.append(g)
            in_specs.append(ANY)
            alias[len(args) - 1] = 2 + j
    if last:
        args += list(tail)
        in_specs += [full(a.shape) for a in tail]
        out_shape = [sds(half, BF16), sds(half, BF16)]
        out_specs = [full(half), full(half)]
    else:
        out_shape = [sds((seq, 768), F32), sds((8, 256), F32)]
        out_specs = [full((seq, 768)), full((8, 256))]
    out_shape += send_shapes(160)
    out_specs += [ANY, ANY, ANY]
    scratch = [
        vm((2, seq, 256), BF16), vm((2, seq, 128), BF16), vm((seq, 256), BF16), vm((2, 128, seq), BF16),
        vm((2, 128, seq), BF16), vm((128, seq), F32), vm((128, seq), F32), vm((seq, 768), BF16),
        vm((768, seq), BF16), vm((BLOCKS // 2, 2, 48, 768), BF16), pltpu.SemaphoreType.DMA((2, 2, BLOCKS // 2)),
    ]
    if last:
        scratch.append(vm((BLOCKS // 2, 2, 16, 768), BF16))
    return pl.pallas_call(
        functools.partial(attn_backward_body, quad, last, 256),
        grid=(2,),
        in_specs=in_specs,
        out_specs=out_specs,
        out_shape=out_shape,
        scratch_shapes=scratch,
        input_output_aliases=alias,
        compiler_params=params(),
        cost_estimate=cost(15),
    )(*args)


def chip_cycle(n_chips):
    rows = n_chips // 2
    return [2 * i for i in range(rows)] + [2 * i + 1 for i in reversed(range(rows))]


def chip_shift(n_chips, step):
    order = chip_cycle(n_chips)
    return [
        (2 * order[i] + core, 2 * order[(i + step) % n_chips] + core)
        for i in range(n_chips)
        for core in (0, 1)
    ]


def core_swap(n_dev):
    return [(i, i ^ 1) for i in range(n_dev)]


def tie(*arrays):
    return lax.optimization_barrier(arrays)


class RingGather:
    def __init__(self, x, n_chips):
        self.n, self.ahead, self.behind = n_chips, [x], [x]

    def step(self):
        if len(self.ahead) <= self.n // 2:
            self.ahead.append(lax.ppermute(self.ahead[-1], "dp", chip_shift(self.n, 1)))
        if len(self.behind) <= self.n - 1 - self.n // 2:
            self.behind.append(lax.ppermute(self.behind[-1], "dp", chip_shift(self.n, -1)))

    def tie(self, *arrays):
        out = tie(self.ahead[-1], self.behind[-1], *arrays)
        self.ahead[-1], self.behind[-1] = out[:2]
        return out[2:]

    def parts(self):
        own = self.ahead + self.behind[1:]
        return own + [lax.ppermute(x, "dp", core_swap(2 * self.n)) for x in own]


def ring_order(n_chips):
    order = chip_cycle(n_chips)
    table = np.zeros((2 * n_chips, 2 * n_chips), np.int32)
    steps = list(range(0, -(n_chips // 2) - 1, -1)) + list(range(1, n_chips - n_chips // 2))
    for chip in range(n_chips):
        pos = order.index(chip)
        chips = [order[(pos + s) % n_chips] for s in steps]
        for core in (0, 1):
            table[2 * chip + core] = [2 * q + core for q in chips] + [2 * q + 1 - core for q in chips]
    return table


def send_order(n_chips):
    order = chip_cycle(n_chips)
    steps = []
    for t in range(n_chips // 2, 0, -1):
        steps += [t, 1 - t] if t > 1 else [t]
    steps.append(0)
    table = np.zeros((n_chips, n_chips), np.int32)
    for chip in range(n_chips):
        table[chip] = [order[(order.index(chip) + s) % n_chips] for s in steps]
    return table


class RingReduce:
    def __init__(self, mine, near, far, n_chips):
        self.n, self.mine, self.slot = n_chips, mine, 0
        self.near = lax.ppermute(near, "dp", core_swap(2 * n_chips))
        self.far = lax.ppermute(far, "dp", core_swap(2 * n_chips))
        self.ahead, self.behind = self.term(), self.term()
        self.left = n_chips // 2

    def term(self, *moved):
        other = self.near[self.slot] if self.slot < 2 else self.far[self.slot - 2]
        total = self.mine[self.slot].astype(F32) + other.astype(F32)
        for m in moved:
            total = total + m.astype(F32)
        self.slot += 1
        return total.astype(BF16)

    def send(self):
        self.ahead, self.behind = tie(self.ahead, self.behind)
        self.ahead = lax.ppermute(self.ahead, "dp", chip_shift(self.n, 1))
        if self.left > 1:
            self.behind = lax.ppermute(self.behind, "dp", chip_shift(self.n, -1))
        self.left -= 1

    def add(self):
        if self.left > 1:
            self.ahead = self.term(self.ahead)
            self.behind = self.term(self.behind)
        elif self.left == 1:
            self.ahead = self.term(self.ahead)
        else:
            self.ahead = self.term(self.ahead, self.behind)

    def tie(self, *arrays):
        out = tie(self.ahead, self.behind, *arrays)
        self.ahead, self.behind = out[:2]
        return out[2:]


def swap_rows(x):
    return lax.ppermute(x, "blk", [(0, 1), (1, 0)])


def pack_weights(qkv_w, proj_w, up_w, down_w, shares):
    r = qkv_w.shape[0] // shares
    qkv = qkv_w.reshape(shares, r, 3, 3, 256).transpose(0, 3, 1, 2, 4).reshape(shares, 3, r, 768)
    up = up_w.reshape(shares, r, BLOCKS, 4, 48).transpose(0, 3, 1, 2, 4).reshape(shares, 4, 1, r, 768)
    down = down_w.reshape(shares, 4, 1, r, 768)
    up_down = jnp.concatenate([up, down], axis=2).reshape(shares, 8, r, 768)
    proj = proj_w.reshape(shares, 1, r, 768)
    return qkv, jnp.concatenate([up_down, proj], axis=1)


def pack_small(gains, shifts, qv_b, out_b, up_b, at):
    width = gains.shape[1]
    flat = jnp.concatenate([gains, shifts, qv_b, out_b, up_b.reshape(4, width)], axis=0)
    return lax.dynamic_update_slice(jnp.zeros((16, 768), flat.dtype), flat, (0, at))


def unpack_qkv(blocks, rows):
    return blocks.reshape(3, rows, 3, 256).transpose(1, 2, 0, 3).reshape(rows, 2304)


def unpack_up(blocks, rows):
    return blocks.reshape(4, rows, BLOCKS, 48).transpose(1, 2, 0, 3).reshape(rows, 3072)


def shards(tokens, segment_ids, padding_mask, qkv_weight, proj_weight, up_weight, down_weight,
           norm_gain, norm_shift, qv_bias, out_bias, up_bias, cotangent):
    n_dev = lax.axis_size("dp")
    dp, blk = lax.axis_index("dp"), lax.axis_index("blk")
    ring = n_dev == BLOCKS
    n_chips = BLOCKS // 2

    def pick(pair, which):
        return lax.dynamic_index_in_dim(pair, which, 0, keepdims=False)

    tok_own, tok_rx = pick(tokens, blk)[0], swap_rows(pick(tokens, 1 - blk)[0])
    cot_own, cot_send = pick(cotangent, blk)[0], pick(cotangent, 1 - blk)[0]
    seg, pad = pick(segment_ids, blk)[0], pick(padding_mask, blk)[0]
    lanes = jnp.arange(128, dtype=jnp.int32)[None, :]
    code = jnp.where(lanes < 32, seg[:, None] // 32 == lanes, seg[:, None] % 32 + 32 == lanes)
    seg_q = code.astype(BF16)
    allowed = code & (pad[:, None] == 1)
    seg_k = jnp.where(allowed | (lanes >= 64), 0.0, MASKED).astype(BF16)

    if ring:
        qkv_blocks, rest = pack_weights(qkv_weight, proj_weight, up_weight, down_weight, 1)
        small = pack_small(norm_gain, norm_shift, qv_bias, out_bias, up_bias, 48 * dp)
        first = RingGather(jnp.concatenate([qkv_blocks.reshape(144, 768), small], axis=0), n_chips)
        rest = rest.reshape(432, 768)
        for _ in range(4):
            first.step()
        (rest,) = first.tie(rest)
        parts = first.parts()
        second = RingGather(rest, n_chips)
        order = jnp.asarray(ring_order(n_chips))[dp]
        core = lax.rem(dp, 2)
        chips = jnp.asarray(send_order(n_chips))[dp // 2]
    else:
        whole = [lax.all_gather(w, "dp", axis=0, tiled=True)
                 for w in (qkv_weight, proj_weight, up_weight, down_weight)]
        qkv_blocks, rest = pack_weights(*whole, BLOCKS)
        vectors = [lax.all_gather(w, "dp", axis=1, tiled=True)
                   for w in (norm_gain, norm_shift, qv_bias, out_bias)]
        hidden = lax.all_gather(up_bias, "dp", axis=0, tiled=True)
        hidden = hidden.reshape(BLOCKS, 4, 48).transpose(1, 0, 2).reshape(-1)
        small = pack_small(*vectors, hidden, 0)
        small = jnp.concatenate([small[None], jnp.zeros((BLOCKS - 1, 16, 768), BF16)], axis=0)
        parts = list(jnp.concatenate([qkv_blocks.reshape(BLOCKS, 144, 768), small], axis=1))
        rest_parts = list(rest.reshape(BLOCKS, 432, 768))
        order = jnp.arange(BLOCKS, dtype=jnp.int32)
        core = jnp.int32(0)
        chips = jnp.arange(n_chips, dtype=jnp.int32)
    idx = jnp.concatenate([order, jnp.stack([blk, core]).astype(jnp.int32), chips])
    cot_send, tok_rx = tie(cot_send, tok_rx)
    cot_rx = swap_rows(cot_send)

    if ring:
        second.step()
    outs = attn_forward(0, idx, parts, (tok_own, tok_rx), seg_q, seg_k)
    heads, nrm, small_all = [list(outs[:7])], outs[7], outs[8]
    for quad in (1, 2):
        if ring:
            nrm, small_all, cot_rx, heads[-1][3] = second.tie(nrm, small_all, cot_rx, heads[-1][3])
            second.step()
        heads.append(list(attn_forward(quad, idx, parts, (nrm, small_all), seg_q, seg_k)))
    atts = [h[3] for h in heads]
    if ring:
        atts[2], small_all = second.tie(atts[2], small_all)
        second.step()
        rest_parts = second.parts()
    lo_mine, lo_theirs, d_mid, d_att, *sends, sums = ffn(
        idx, rest_parts, atts, tok_own, tok_rx, cot_own, cot_rx, small_all)
    lo_rx = swap_rows(lo_theirs)

    if ring:
        ffn_sum = RingReduce(*sends, n_chips)
        (d_att,) = ffn_sum.tie(d_att)
        ffn_sum.send()
    d_ni, b0, *q_sends = attn_backward(0, idx, heads[0], d_att, nrm)
    if ring:
        d_ni, ffn_sum.far, lo_rx = ffn_sum.tie(d_ni, ffn_sum.far, lo_rx)
        ffn_sum.add()
        (d_ni,) = ffn_sum.tie(d_ni)
        ffn_sum.send()
    d_ni, b1, *q_sends = attn_backward(1, idx, heads[1], d_att, nrm, d_ni, q_sends)
    if ring:
        (d_ni,) = ffn_sum.tie(d_ni)
        ffn_sum.add()
        (d_ni,) = ffn_sum.tie(d_ni)
        ffn_sum.send()
    gt_mine, gt_theirs, *q_sends = attn_backward(
        2, idx, heads[2], d_att, nrm, d_ni, q_sends, tail=(tok_own, tok_rx, d_mid, small_all, sums, b0, b1))

    def together(own_half, other_half):
        swapped = blk == 1
        return jnp.stack([jnp.where(swapped, other_half, own_half),
                          jnp.where(swapped, own_half, other_half)])[:, None]

    if ring:
        gt_theirs, *q_sends = ffn_sum.tie(gt_theirs, *q_sends)
        ffn_sum.add()
        ffn_sum.send()
        qkv_sum = RingReduce(*q_sends, n_chips)
        gt_rx = swap_rows(gt_theirs)
        qkv_sum.send()
        ffn_sum.add()
        for _ in range(3):
            qkv_sum.add()
            qkv_sum.send()
        qkv_sum.add()
        done_ffn, done_qkv = [x.ahead.astype(F32) + swap_rows(x.ahead).astype(F32) for x in (ffn_sum, qkv_sum)]
        r = 48
        ffn_blocks = done_ffn[0:384].reshape(4, 2, r, 768)
        g_up, g_down, g_proj = ffn_blocks[:, 0], ffn_blocks[:, 1].reshape(4 * r, 768), done_ffn[384:432]
        g_small = lax.dynamic_slice_in_dim(done_qkv[144:160], 48 * dp, 48, 1)
        return (together(lo_mine, lo_rx), together(gt_mine, gt_rx),
                unpack_qkv(done_qkv[0:144], r), g_proj, unpack_up(g_up, r), g_down,
                g_small[0:2], g_small[2:4], g_small[4:6], g_small[6:8], g_small[8:12].reshape(-1))

    gt_rx = swap_rows(gt_theirs)

    def whole_sum(mine, near, far):
        return jnp.stack([mine, jnp.concatenate([near, far])], axis=1).reshape(BLOCKS, mine.shape[1], 768)

    def scatter(x, dim):
        part = lax.psum_scatter(x, "dp", scatter_dimension=dim, tiled=True)
        return lax.psum(part.astype(BF16), "blk").astype(F32)

    g_ffn, g_q = whole_sum(*sends), whole_sum(*q_sends)
    ffn_blocks = g_ffn[:, 0:384].reshape(BLOCKS, 4, 2, 48, 768).transpose(1, 2, 0, 3, 4).reshape(4, 2, 768, 768)
    g_up = unpack_up(ffn_blocks[:, 0], 768)
    g_down = ffn_blocks[:, 1].reshape(4, BLOCKS, 48, 768).transpose(1, 0, 2, 3).reshape(3072, 768)
    g_proj = g_ffn[:, 384:432].reshape(768, 768)
    g_qkv = jnp.stack([g_q[:, 48 * j : 48 * j + 48].reshape(768, 768) for j in range(3)])
    g_small = g_q[0, 144:160].astype(F32)
    g_bias = g_small[8:12].reshape(4, BLOCKS, 48).transpose(1, 0, 2).reshape(-1)
    big = [scatter(g.astype(F32), 0) for g in (unpack_qkv(g_qkv, 768), g_proj, g_up, g_down)]
    return (together(lo_mine, lo_rx), together(gt_mine, gt_rx), *big,
            *[scatter(g_small[2 * i : 2 * i + 2], 1) for i in range(4)], scatter(g_bias, 0))


def solution(mesh):
    rows = P(None, "dp", "blk", None)
    return jax.shard_map(
        shards,
        mesh=mesh,
        in_specs=(rows, P(None, "dp", None), P(None, "dp", None)) + (P("dp", None),) * 4
        + (P(None, "dp"),) * 4 + (P("dp"), rows),
        out_specs=(rows, rows) + (P("dp", None),) * 4 + (P(None, "dp"),) * 4 + (P("dp"),),
        check_vma=False,
    )
```

```python
import functools

import jax
import jax.numpy as jnp
import numpy as np
from jax import lax
from jax.experimental import pallas as pl
from jax.experimental.pallas import tpu as pltpu
from jax.sharding import PartitionSpec as P

HD = 64
BLOCKS = 16
N_PARTS = BLOCKS + 2
NT = (((1,), (1,)), ((), ()))
TN = (((0,), (0,)), ((), ()))
F32 = jnp.float32
BF16 = jnp.bfloat16
ANY = pl.BlockSpec(memory_space=pl.ANY)
SMEM = pl.BlockSpec(memory_space=pltpu.SMEM)
VMEM_LIMIT = 60 << 20
MASKED = -1e30


def dot(a, b, dims=(((1,), (0,)), ((), ()))):
    return lax.dot_general(a, b, dims, preferred_element_type=F32)


def cost(us):
    return pl.CostEstimate(flops=int(us * 1.1e9), bytes_accessed=1 << 20, transcendentals=0)


def full(shape):
    return pl.BlockSpec(shape, lambda *_: (0,) * len(shape))


def params():
    return pltpu.CompilerParams(vmem_limit_bytes=VMEM_LIMIT)


def norm_stats(x):
    mean = jnp.mean(x, axis=1, keepdims=True)
    center = x - mean
    rstd = lax.rsqrt(jnp.mean(center * center, axis=1, keepdims=True) + 1e-05)
    return center * rstd, rstd


def norm_back(e, nhat, rstd):
    return (
        e - jnp.mean(e, axis=1, keepdims=True) - nhat * jnp.mean(e * nhat, axis=1, keepdims=True)
    ) * rstd


def row_sum(x):
    return jnp.sum(x, axis=0, keepdims=True)


def send_copies(idx, buf, rows, mine, near, far, sem, lanes=slice(None)):
    core = idx[17]
    copies = []
    for slot in range(BLOCKS // 2):
        chip = idx[18 + slot]
        theirs = far.at[slot - 1] if slot else near.at[0]
        copies.append(pltpu.make_async_copy(buf.at[chip, core], mine.at[slot, rows, lanes], sem.at[0, slot]))
        copies.append(pltpu.make_async_copy(buf.at[chip, 1 - core], theirs.at[rows, lanes], sem.at[1, slot]))
    return copies


def part_copies(parts, split, start, size, place, sem, piece=None):
    copies = []
    n = BLOCKS // 2
    for t in range(BLOCKS):
        group = parts[(n + 1) * (t // n) : (n + 1) * (t // n + 1)]
        if t % n < n - 1:
            src, at = group[t % n], start
        elif piece == 0 or (piece is None and start < split):
            src, at = group[n - 1], start
        else:
            src, at = group[n], start - split
        copies.append(pltpu.make_async_copy(src.at[pl.ds(at, size), :], place(t), sem(t)))
    return copies


def send_shapes(rows):
    return [jax.ShapeDtypeStruct((n, rows, 768), BF16) for n in (BLOCKS // 2, 1, BLOCKS // 2 - 1)]


def attn_forward_body(quad, block, idx, *refs):
    first = quad == 0
    parts, refs = refs[:N_PARTS], refs[N_PARTS:]
    if first:
        (tok_own, tok_rx, sq, sk, q_o, k_o, v_o, att_o, li_o, e_o, w_o, nrm_o, small_o,
         w_s, s_s, kk, vv, aa, sem) = refs
    else:
        (nrm_i, small_i, sq, sk, q_o, k_o, v_o, att_o, li_o, e_o, w_o,
         w_s, kk, vv, aa, sem) = refs
    seq = sq.shape[0]
    half = seq // 2
    pair = pl.program_id(0)

    @pl.when(pair == 0)
    def _():
        copies = part_copies(parts, 96, 48 * quad, 48, lambda t: w_s.at[idx[t]], lambda t: sem.at[0, t])
        if first:
            copies += part_copies(parts, 96, 144, 16, lambda t: s_s.at[t], lambda t: sem.at[1, t])
        for c in copies:
            c.start()
        for c in copies:
            c.wait()
        weight = w_s[...].reshape(768, 768)
        w_o[...] = weight
        if first:
            small = jnp.zeros((16, 768), F32)
            for t in range(BLOCKS):
                small = small + s_s[t].astype(F32)
            small_o[...] = small
            gain, shift = small[0:1], small[2:3]
            for src, where in ((tok_own, idx[16]), (tok_rx, 1 - idx[16])):
                base = pl.multiple_of(where * half, half)
                for i in range(0, half, block):
                    nhat, _rstd = norm_stats(src[i : i + block, :].astype(F32))
                    nrm_o[pl.ds(base + i, block), :] = (nhat * gain + shift).astype(BF16)
            nrm = nrm_o
            bq, bv = small[4:5, 0:256], small[5:6, 0:256]
        else:
            nrm = nrm_i
            cols = slice(256 * quad, 256 * quad + 256)
            bq, bv = small_i[4:5, cols], small_i[5:6, cols]
        for i in range(0, seq, block):
            rows = slice(i, i + block)
            joined = dot(nrm[rows, :], weight)
            for p in range(2):
                c, to = 384 * p, slice(128 * p, 128 * p + 128)
                q_o[rows, to] = (joined[:, c : c + 128] + bq[:, to]).astype(BF16)
                k_o[rows, to] = joined[:, c + 128 : c + 256].astype(BF16)
                v_o[rows, to] = (joined[:, c + 256 : c + 384] + bv[:, to]).astype(BF16)

    lanes = pl.ds(pl.multiple_of(pair * 128, 128), 128)
    head = lax.broadcasted_iota(jnp.int32, (seq, 128), 1) // HD
    k_pair, v_pair = k_o[:, lanes], v_o[:, lanes]
    zero, one = jnp.zeros((seq, 128), BF16), jnp.ones((seq, 128), BF16)
    for h in range(2):
        mine = head == h
        kk[h, :, 0:128] = jnp.where(mine, k_pair, zero)
        kk[h, :, 128:256] = sk[...]
        vv[h, :, 0:128] = jnp.where(mine, v_pair, zero)
        vv[h, :, 128:256] = jnp.where(mine, one, zero)
    aa[:, 0:128] = q_o[:, lanes] * BF16(0.125)
    aa[:, 128:256] = sq[...]
    for i in range(0, seq, block):
        rows = slice(i, i + block)
        acc = None
        for h in range(2):
            s = dot(aa[rows, :], kk[h], NT)
            e = jnp.exp(s - jnp.max(s, axis=1, keepdims=True)).astype(BF16)
            e_o[h, rows, :] = e
            o = dot(e, vv[h])
            acc = o if acc is None else acc + o
        inverse = 1.0 / acc[:, 128:256]
        li_o[rows, :] = inverse
        att_o[rows, :] = (acc[:, 0:128] * inverse).astype(BF16)


def attn_forward(quad, idx, parts, rows_in, sq, sk):
    seq = sq.shape[0]
    sds = jax.ShapeDtypeStruct
    first = quad == 0
    pair_block = pl.BlockSpec((seq, 128), lambda p: (0, p))
    quad_block = full((seq, 256))
    out_shape = [
        sds((seq, 256), BF16),
        sds((seq, 256), BF16),
        sds((seq, 256), BF16),
        sds((seq, 256), BF16),
        sds((seq, 256), F32),
        sds((4, seq, seq), BF16),
        sds((768, 768), BF16),
    ]
    out_specs = [
        quad_block, quad_block, quad_block, pair_block, pair_block,
        pl.BlockSpec((2, seq, seq), lambda p: (p, 0, 0)), full((768, 768)),
    ]
    scratch = [pltpu.VMEM((BLOCKS, 48, 768), BF16)]
    if first:
        out_shape += [sds((seq, 768), BF16), sds((16, 768), F32)]
        out_specs += [full((seq, 768)), full((16, 768))]
        scratch += [pltpu.VMEM((BLOCKS, 16, 768), BF16)]
    scratch += [
        pltpu.VMEM((2, seq, 256), BF16),
        pltpu.VMEM((2, seq, 256), BF16),
        pltpu.VMEM((seq, 256), BF16),
        pltpu.SemaphoreType.DMA((2, BLOCKS)),
    ]
    return pl.pallas_call(
        functools.partial(attn_forward_body, quad, 256),
        grid=(2,),
        in_specs=[SMEM] + [ANY] * N_PARTS
        + [full(r.shape) for r in rows_in]
        + [full(sq.shape), full(sk.shape)],
        out_specs=out_specs,
        out_shape=out_shape,
        scratch_shapes=scratch,
        compiler_params=params(),
        cost_estimate=cost(11),
    )(idx, *parts, *rows_in, sq, sk)


def ffn_body(
    block, idx, *refs
):
    parts, refs = refs[:N_PARTS], refs[N_PARTS:]
    ffn_steps(block, idx, parts, *refs)


def ffn_steps(
    block, idx, parts, att0, att1, att2, tok_own, tok_rx, cot_own, cot_rx, small,
    lo_mine, lo_theirs, dmid_o, datt_o, g_mine, g_near, g_far, sums_o,
    up_s, dn_s, proj_s, att_s, mid_s, nm_s, nmt_s, cot_s, act_s, dp_s, oacc, dacc, dbr_s, gup_s, gdn_s, gproj,
    wsem, dsem, psem, gsem, gdsem, gpsem,
):
    c = pl.program_id(0)
    n_c = pl.num_programs(0)
    slot = lax.rem(c, 2)
    seq = mid_s.shape[0]
    half = seq // 2
    core = idx[17]

    def up_copies(chunk, s):
        rows = pl.multiple_of(chunk * 48, 48)
        return part_copies(parts, 0, rows, 48, lambda t: up_s.at[s, idx[t]], lambda t: wsem.at[s, t], piece=0)

    def down_copies():
        return part_copies(parts, 192, 192, 192, lambda t: dn_s.at[idx[t]], lambda t: dsem.at[idx[t]])

    def grad_copies(chunk, s, act):
        rows = pl.ds(pl.multiple_of(chunk * 48, 48), 48)
        for copy in send_copies(idx, gup_s.at[s], rows, g_mine, g_near, g_far, gsem.at[s]):
            act(copy)
        rows = pl.ds(192, 192)
        for j in range(2):
            slot_to = idx[26 + 2 * chunk + j]
            act(pltpu.make_async_copy(gdn_s.at[s, j, core], g_mine.at[slot_to, rows, :], gdsem.at[s, 0, j]))

            @pl.when(slot_to == 0)
            def _():
                act(pltpu.make_async_copy(gdn_s.at[s, j, 1 - core], g_near.at[0, rows, :], gdsem.at[s, 1, j]))

            @pl.when(slot_to > 0)
            def _():
                act(pltpu.make_async_copy(gdn_s.at[s, j, 1 - core], g_far.at[slot_to - 1, rows, :], gdsem.at[s, 1, j]))

    def start(copy):
        copy.start()

    def wait(copy):
        copy.wait()

    @pl.when(c == 0)
    def _():
        for copy in up_copies(c, 0) + down_copies():
            copy.start()
        proj_copies = part_copies(parts, 192, 384, 48, lambda t: proj_s.at[idx[t]], lambda t: psem.at[t])
        for copy in proj_copies:
            copy.start()
        for src, where in ((tok_own, idx[16]), (tok_rx, 1 - idx[16])):
            base = pl.multiple_of(where * half, half)
            mid_s[pl.ds(base, half), :] = src[...].astype(F32)
        for src, where in ((cot_own, idx[16]), (cot_rx, 1 - idx[16])):
            base = pl.multiple_of(where * half, half)
            cot_s[pl.ds(base, half), :] = src[...]
        for j, a in enumerate((att0, att1, att2)):
            att_s[:, 256 * j : 256 * j + 256] = a[...]
        for copy in proj_copies:
            copy.wait()
        proj = proj_s[...].reshape(768, 768)
        for i in range(0, seq, block):
            rows = slice(i, i + block)
            mid = mid_s[rows, :] + (dot(att_s[rows, :], proj) + small[6:7])
            mid_s[rows, :] = mid
            nhat, _rstd = norm_stats(mid)
            nm_s[rows, :] = (nhat * small[1:2] + small[3:4]).astype(BF16)
        nmt_s[...] = nm_s[...].T
        oacc[...] = jnp.zeros_like(oacc)
        dacc[...] = jnp.zeros_like(dacc)

    for copy in up_copies(c, slot):
        copy.wait()
    for j in range(4):
        owner = 4 * c + j
        pltpu.make_async_copy(parts[0].at[pl.ds(192, 192), :], dn_s.at[owner], dsem.at[owner]).wait()

    @pl.when(c + 1 < n_c)
    def _():
        for copy in up_copies(c + 1, 1 - slot):
            copy.start()

    up = up_s[slot].reshape(768, 768)
    dn = dn_s[pl.ds(4 * c, 4)].reshape(768, 768)
    bias = small[pl.ds(8 + c, 1), :]
    bias_sum = None
    for i in range(0, seq, block):
        rows = slice(i, i + block)
        pre = dot(nm_s[rows, :], up) + bias
        cdf = 0.5 * (1.0 + lax.erf(pre * 0.7071067811865476))
        act = (pre * cdf).astype(BF16)
        act_s[rows, :] = act
        oacc[rows, :] += dot(act, dn)
        slope = cdf + pre * (jnp.exp(pre * pre * -0.5) * 0.3989422804014327)
        d_pre = (dot(cot_s[rows, :], dn, NT) * slope).astype(BF16)
        dp_s[rows, :] = d_pre
        part = row_sum(d_pre.astype(F32))
        bias_sum = part if bias_sum is None else bias_sum + part
        dacc[rows, :] += dot(d_pre, up, NT)
    sums_o[pl.ds(8 + c, 1), :] = bias_sum

    @pl.when(c >= 2)
    def _():
        grad_copies(c - 2, slot, wait)

    gup_s[slot] = dot(nmt_s[...], dp_s[...]).astype(BF16).reshape(BLOCKS // 2, 2, 48, 768)
    gdn_s[slot] = dot(act_s[...], cot_s[...], TN).astype(BF16).reshape(2, 2, 192, 768)
    grad_copies(c, slot, start)

    @pl.when(c == n_c - 1)
    def _():
        proj = proj_s[...].reshape(768, 768)
        gain_sum = shift_sum = bout_sum = bdown_sum = None
        for i in range(0, seq, block):
            rows = slice(i, i + block)
            mid = mid_s[rows, :]
            cot = cot_s[rows, :].astype(F32)
            d_nm = dacc[rows, :]
            nhat, rstd = norm_stats(mid)
            d_mid = cot + norm_back(d_nm * small[1:2], nhat, rstd)
            dmid_o[rows, :] = d_mid
            d_branch = d_mid.astype(BF16)
            dbr_s[rows, :] = d_branch
            datt_o[rows, :] = dot(d_branch, proj, NT).astype(BF16)
            parts = [row_sum(d_nm * nhat), row_sum(d_nm), row_sum(d_branch.astype(F32)), row_sum(cot)]
            if gain_sum is None:
                gain_sum, shift_sum, bout_sum, bdown_sum = parts
            else:
                gain_sum, shift_sum = gain_sum + parts[0], shift_sum + parts[1]
                bout_sum, bdown_sum = bout_sum + parts[2], bdown_sum + parts[3]
        sums_o[0:8, :] = jnp.concatenate(
            [jnp.zeros_like(gain_sum), gain_sum, jnp.zeros_like(gain_sum), shift_sum,
             jnp.zeros_like(gain_sum), jnp.zeros_like(gain_sum), bout_sum, bdown_sum], axis=0)
        sums_o[12:16, :] = jnp.zeros((4, 768), F32)
        for dst, where in ((lo_mine, idx[16]), (lo_theirs, 1 - idx[16])):
            base = pl.multiple_of(where * half, half)
            for i in range(0, half, block):
                rows = pl.ds(base + i, block)
                dst[i : i + block, :] = (mid_s[rows, :] + (oacc[rows, :] + small[7:8])).astype(BF16)
        gproj[...] = dot(att_s[...], dbr_s[...], TN).astype(BF16).reshape(BLOCKS // 2, 2, 48, 768)
        last = send_copies(idx, gproj, pl.ds(384, 48), g_mine, g_near, g_far, gpsem)
        for copy in last:
            copy.start()
        grad_copies(c - 1, 1 - slot, wait)
        grad_copies(c, slot, wait)
        for copy in last:
            copy.wait()


def ffn(idx, parts, atts, tok_own, tok_rx, cot_own, cot_rx, small):
    seq = 2 * tok_own.shape[0]
    sds = jax.ShapeDtypeStruct
    v = pltpu.VMEM
    half = tok_own.shape
    rows, frows = v((seq, 768), BF16), v((seq, 768), F32)
    return pl.pallas_call(
        functools.partial(ffn_body, 256),
        grid=(4,),
        in_specs=[SMEM] + [ANY] * N_PARTS + [full((seq, 256))] * 3 + [full(half)] * 4 + [full((16, 768))],
        out_specs=[full(half), full(half), full((seq, 768)), full((seq, 768)), ANY, ANY, ANY, full((16, 768))],
        out_shape=[
            sds(half, BF16), sds(half, BF16), sds((seq, 768), F32), sds((seq, 768), BF16),
            *send_shapes(432), sds((16, 768), F32),
        ],
        scratch_shapes=[
            v((2, BLOCKS, 48, 768), BF16), v((BLOCKS, 192, 768), BF16), v((BLOCKS, 48, 768), BF16),
            rows, frows, rows, v((768, seq), BF16), rows, rows, rows, frows, frows, rows,
            v((2, BLOCKS // 2, 2, 48, 768), BF16), v((2, 2, 2, 192, 768), BF16), v((BLOCKS // 2, 2, 48, 768), BF16),
            pltpu.SemaphoreType.DMA((2, BLOCKS)), pltpu.SemaphoreType.DMA((BLOCKS,)), pltpu.SemaphoreType.DMA((BLOCKS,)),
            pltpu.SemaphoreType.DMA((2, 2, BLOCKS // 2)), pltpu.SemaphoreType.DMA((2, 2, 2)),
            pltpu.SemaphoreType.DMA((2, BLOCKS // 2)),
        ],
        compiler_params=params(),
        cost_estimate=cost(50),
    )(idx, *parts, *atts, tok_own, tok_rx, cot_own, cot_rx, small)


def attn_backward_body(pairs, block, idx, *refs):
    n = len(pairs)
    start_pair, last = pairs[0] == 0, pairs[-1] == 5
    heads, refs = [refs[7 * j : 7 * j + 7] for j in range(n)], refs[7 * n :]
    (do_h, nrm_h), refs = refs[:2], refs[2:]
    if not start_pair:
        dni_h, refs = refs[0], refs[4:]
    if last:
        (tok_own, tok_rx, dmid_h, small, sums_i, *b_in), refs = refs[:8], refs[8:]
        (gt_mine, gt_theirs, *sends), refs = refs[:5], refs[5:]
    else:
        (dni_o, b_o, *sends), refs = refs[:5], refs[5:]
    (q_s, k_s, v_s, o_s, do_s, li_s, e_s, w_s, nrm_s, dni_s, vv, kk, dd, qm, dm, dkt, dvt, dj, gbuf,
     isem, esem, wsem, gsem), refs = refs[:23], refs[23:]
    seq = q_s.shape[1]
    half = seq // 2
    n_block = seq // block
    copy = pltpu.make_async_copy
    lane = lax.broadcasted_iota(jnp.int32, (seq, 128), 1)
    side = lax.broadcasted_iota(jnp.int32, (128, seq), 0)

    heads_in, e_in, late = [], [], []
    for j, (q_h, k_h, v_h, o_h, li_h, e_h, w_h) in enumerate(heads):
        odd = pairs[j] % 2
        lanes = pl.ds(128 * odd, 128)
        lanes_do = pl.ds(128 * pairs[j], 128)
        heads_in.append([
            copy(src.at[:, ln], dst.at[j], isem.at[j, m])
            for m, (src, dst, ln) in enumerate((
                (v_h, v_s, lanes), (do_h, do_s, lanes_do), (li_h, li_s, lanes), (o_h, o_s, lanes),
                (k_h, k_s, lanes), (q_h, q_s, lanes)))
        ])
        e_in.append([
            copy(e_h.at[pl.ds(2 * odd, 2), pl.ds(i * block, block), :],
                 e_s.at[pl.ds(2 * j, 2), pl.ds(i * block, block), :], esem.at[j, i])
            for i in range(n_block)
        ])
        late.append(copy(w_h.at[:, pl.ds(384 * odd, 384)], w_s.at[:, pl.ds(384 * j, 384)], wsem.at[j]))
    late.append(copy(nrm_h, nrm_s, wsem.at[2]))
    if not start_pair:
        late.append(copy(dni_h, dni_s, wsem.at[3]))
    if last:
        dmid_s, sbuf = refs
        late.append(copy(dmid_h, dmid_s, wsem.at[4]))
    for c in heads_in[0] + e_in[0][:2]:
        c.start()
    queue = e_in[0][2:]
    for j in range(1, n):
        queue = queue + heads_in[j] + e_in[j]
    queue = queue + late
    per_block = -(-len(queue) // n_block)

    for pair in range(n):
        for c in heads_in[pair]:
            c.wait()
        d_out = do_s[pair].astype(F32) * li_s[pair]
        d_low = d_out.astype(BF16)
        prod = d_out * o_s[pair].astype(F32)
        extra = jnp.zeros((seq, 128), F32)
        q_t, d_t = q_s[pair].T, d_low.T
        zero = jnp.zeros((seq, 128), BF16)
        zero_t = jnp.zeros((128, seq), BF16)
        for h in range(2):
            mine = (lane // HD) == h
            delta = jnp.sum(jnp.where(mine, prod, 0.0), axis=1, keepdims=True)
            high = delta.astype(BF16).astype(F32)
            extra = jnp.where(lane == 2 * h, -high, extra)
            extra = jnp.where(lane == 2 * h + 1, high - delta, extra)
            vv[h, :, 0:128] = jnp.where(mine, v_s[pair], zero)
            vv[h, :, 128:256] = jnp.where((lane // 2) == h, 1.0, 0.0).astype(BF16)
            kk[h] = jnp.where(mine, k_s[pair], zero)
            mine_t = (side // HD) == h
            qm[h] = jnp.where(mine_t, q_t, zero_t)
            dm[h] = jnp.where(mine_t, d_t, zero_t)
        dd[:, 0:128] = d_low
        dd[:, 128:256] = extra.astype(BF16)
        base = 384 * pair
        for i in range(n_block):
            e_in[pair][i].wait()
            for c in queue[:per_block]:
                c.start()
            queue = queue[per_block:]
            rows = slice(i * block, i * block + block)
            dq = None
            for h in range(2):
                dp = dot(dd[rows, :], vv[h], NT)
                e = e_s[2 * pair + h, rows, :]
                ds = dp.astype(BF16) * e
                t = dot(ds, kk[h])
                dq = t if dq is None else dq + t
                a, b = dot(qm[h, :, rows], ds), dot(dm[h, :, rows], e)
                if i == 0 and h == 0:
                    dkt[...], dvt[...] = a, b
                else:
                    dkt[...] += a
                    dvt[...] += b
            dj[rows, base : base + 128] = (dq * 0.125).astype(BF16)
        dj[:, base + 128 : base + 256] = (dkt[...] * 0.125).astype(BF16).T
        dj[:, base + 256 : base + 384] = dvt[...].astype(BF16).T

    for c in late:
        c.wait()
    grads = dot(nrm_s[...], dj[...], TN).astype(BF16)
    copies, bq, bv = [], [], []
    for j, p in enumerate(pairs):
        c = 384 * j
        gbuf[j] = grads[:, c : c + 384].reshape(BLOCKS // 2, 2, 48, 384)
        copies += send_copies(idx, gbuf.at[j], pl.ds(48 * (p // 2), 48), *sends, gsem.at[j],
                              pl.ds(384 * (p % 2), 384))
        bq.append(row_sum(dj[:, c : c + 128].astype(F32)))
        bv.append(row_sum(dj[:, c + 256 : c + 384].astype(F32)))
    for c in copies:
        c.start()
    weight = w_s[...]
    if not last:
        both = jnp.concatenate(
            [jnp.concatenate(bq, axis=1), jnp.concatenate(bv, axis=1), jnp.zeros((6, 128 * n), F32)], axis=0)
        b_o[...] = both
        for i in range(n_block):
            rows = slice(i * block, i * block + block)
            d_ni = dot(dj[rows, :], weight, NT)
            dni_s[rows, :] = d_ni if start_pair else dni_s[rows, :] + d_ni
            out = copy(dni_s.at[pl.ds(i * block, block), :], dni_o.at[pl.ds(i * block, block), :], esem.at[0, i])
            out.start()
            copies.append(out)
    else:
        gain = small[0:1]
        gain_sum = shift_sum = None
        for src, dst, where in ((tok_rx, gt_theirs, 1 - idx[16]), (tok_own, gt_mine, idx[16])):
            start = pl.multiple_of(where * half, half)
            for i in range(0, half, block):
                rows = pl.ds(start + i, block)
                d_ni = dni_s[rows, :] + dot(dj[rows, :], weight, NT)
                nhat, rstd = norm_stats(src[i : i + block, :].astype(F32))
                grad = dmid_s[rows, :] + norm_back(d_ni * gain, nhat, rstd)
                dst[i : i + block, :] = grad.astype(BF16)
                parts = [row_sum(d_ni * nhat), row_sum(d_ni)]
                if gain_sum is None:
                    gain_sum, shift_sum = parts
                else:
                    gain_sum, shift_sum = gain_sum + parts[0], shift_sum + parts[1]
        sums = sums_i[...]
        row = lax.broadcasted_iota(jnp.int32, (16, 768), 0)
        sums = jnp.where(row == 0, gain_sum, sums)
        sums = jnp.where(row == 2, shift_sum, sums)
        sums = jnp.where(row == 4, jnp.concatenate([b[0:1, :] for b in b_in] + bq, axis=1), sums)
        sums = jnp.where(row == 5, jnp.concatenate([b[1:2, :] for b in b_in] + bv, axis=1), sums)
        low = sums.astype(BF16)
        for t in range(BLOCKS // 2):
            sbuf[t, 0], sbuf[t, 1] = low, low
        more = send_copies(idx, sbuf, pl.ds(144, 16), *sends, gsem.at[1])
        for c in more:
            c.start()
        copies += more
    for c in copies:
        c.wait()


def attn_backward(pairs, idx, heads, d_att, nrm, d_ni=None, grads=None, tail=None):
    n, first, last = len(pairs), pairs[0] == 0, tail is not None
    seq = nrm.shape[0]
    half = (seq // 2, 768)
    block = 256
    sds = jax.ShapeDtypeStruct
    vm = pltpu.VMEM
    whole = pl.BlockSpec(memory_space=pltpu.VMEM)
    args = [idx]
    for p in pairs:
        args += heads[p // 2]
    args += [d_att, nrm]
    in_specs = [SMEM] + [ANY] * (len(args) - 1)
    alias = {}
    if not first:
        args.append(d_ni)
        in_specs.append(ANY)
        if not last:
            alias[len(args) - 1] = 0
        for j, g in enumerate(grads):
            args.append(g)
            in_specs.append(ANY)
            alias[len(args) - 1] = 2 + j
    if last:
        args += list(tail)
        in_specs += [whole, whole, ANY] + [whole] * (len(tail) - 3)
        out_shape = [sds(half, BF16), sds(half, BF16)]
        out_specs = [whole, whole]
    else:
        out_shape = [sds((seq, 768), F32), sds((8, 128 * n), F32)]
        out_specs = [ANY, whole]
    out_shape += send_shapes(160)
    out_specs += [ANY, ANY, ANY]
    pair = vm((n, seq, 128), BF16)
    dma = pltpu.SemaphoreType.DMA
    scratch = [
        pair, pair, pair, pair, pair, vm((n, seq, 128), F32), vm((2 * n, seq, seq), BF16), vm((768, 384 * n), BF16),
        vm((seq, 768), BF16), vm((seq, 768), F32),
        vm((2, seq, 256), BF16), vm((2, seq, 128), BF16), vm((seq, 256), BF16), vm((2, 128, seq), BF16),
        vm((2, 128, seq), BF16), vm((128, seq), F32), vm((128, seq), F32), vm((seq, 384 * n), BF16),
        vm((n, BLOCKS // 2, 2, 48, 384), BF16), dma((n, 6)), dma((n, seq // block)), dma((5,)),
        dma((2, 2, BLOCKS // 2)),
    ]
    if last:
        scratch += [vm((seq, 768), F32), vm((BLOCKS // 2, 2, 16, 768), BF16)]
    return pl.pallas_call(
        functools.partial(attn_backward_body, pairs, block),
        in_specs=in_specs,
        out_specs=out_specs,
        out_shape=out_shape,
        scratch_shapes=scratch,
        input_output_aliases=alias,
        compiler_params=params(),
        cost_estimate=cost(8 * n),
    )(*args)


def chip_cycle(n_chips):
    rows = n_chips // 2
    return [2 * i for i in range(rows)] + [2 * i + 1 for i in reversed(range(rows))]


def chip_shift(n_chips, step):
    order = chip_cycle(n_chips)
    return [
        (2 * order[i] + core, 2 * order[(i + step) % n_chips] + core)
        for i in range(n_chips)
        for core in (0, 1)
    ]


def core_swap(n_dev):
    return [(i, i ^ 1) for i in range(n_dev)]


def tie(*arrays):
    return lax.optimization_barrier(arrays)


class RingGather:
    def __init__(self, x, split, n_chips):
        self.n, self.split, self.ahead, self.behind = n_chips, split, [x], [x]
        self.other = [self.swap(x)]
        self.waiting = []

    def swap(self, x):
        return lax.ppermute(x, "dp", core_swap(2 * self.n))

    def step(self):
        a, b = self.ahead[-1], self.behind[-1]
        if len(self.ahead) == self.n // 2:
            a, b = a[: self.split], b[self.split :]
        self.ahead.append(lax.ppermute(a, "dp", chip_shift(self.n, 1)))
        self.behind.append(lax.ppermute(b, "dp", chip_shift(self.n, -1)))

    def tie(self, *arrays):
        a, b, *rest = tie(self.ahead[-1], self.behind[-1], *self.other[-2:], *arrays)
        self.ahead[-1], self.behind[-1] = a, b
        n = len(self.other[-2:])
        self.other[-n:], rest = rest[:n], rest[n:]
        self.other += [self.swap(a), self.swap(b)]
        return rest

    def arrived(self):
        self.other += [self.swap(self.ahead[-1]), self.swap(self.behind[-1])]

    def parts(self):
        def in_order(ahead, behind):
            return [ahead[0]] + ahead[1:-1] + behind[1:-1] + [ahead[-1], behind[-1]]

        o = self.other
        return in_order(self.ahead, self.behind) + in_order(o[:1] + o[1::2], o[:1] + o[2::2])


def ring_order(n_chips):
    order = chip_cycle(n_chips)
    table = np.zeros((2 * n_chips, 2 * n_chips), np.int32)
    far = n_chips // 2
    steps = list(range(0, -far, -1)) + list(range(1, far)) + [far]
    for chip in range(n_chips):
        pos = order.index(chip)
        chips = [order[(pos + s) % n_chips] for s in steps]
        for core in (0, 1):
            table[2 * chip + core] = [2 * q + core for q in chips] + [2 * q + 1 - core for q in chips]
    return table


def send_order(n_chips):
    order = chip_cycle(n_chips)
    steps = [n_chips // 2]
    for t in range(n_chips // 2 - 1, 0, -1):
        steps += [t, -t]
    steps.append(0)
    table = np.zeros((n_chips, n_chips), np.int32)
    for chip in range(n_chips):
        table[chip] = [order[(order.index(chip) + s) % n_chips] for s in steps]
    return table


class RingReduce:
    def __init__(self, mine, near, far, split, n_chips):
        self.n, self.mine, self.split, self.slot = n_chips, mine, split, 1
        self.near = lax.ppermute(near, "dp", core_swap(2 * n_chips))
        far, self.near = tie(far, self.near)
        self.far = lax.ppermute(far, "dp", core_swap(2 * n_chips))
        whole = (mine[0].astype(F32) + self.near[0].astype(F32)).astype(BF16)
        self.ahead, self.behind = whole[:split], whole[split:]

    def term(self, *moved):
        total = self.mine[self.slot].astype(F32) + self.far[self.slot - 1].astype(F32)
        for m in moved:
            total = total + m.astype(F32)
        self.slot += 1
        return total.astype(BF16)

    def send(self):
        self.ahead, self.behind = tie(self.ahead, self.behind)
        self.ahead = lax.ppermute(self.ahead, "dp", chip_shift(self.n, 1))
        self.behind = lax.ppermute(self.behind, "dp", chip_shift(self.n, -1))

    def add(self):
        if self.slot == 1:
            ahead = jnp.pad(self.ahead, ((0, self.mine.shape[1] - self.split), (0, 0)))
            behind = jnp.pad(self.behind, ((self.split, 0), (0, 0)))
            self.ahead, self.behind = self.term(ahead), self.term(behind)
        elif self.slot < self.n - 1:
            self.ahead, self.behind = self.term(self.ahead), self.term(self.behind)
        else:
            self.total = self.term(self.ahead, self.behind)

    def tie(self, *arrays):
        out = tie(self.ahead, self.behind, *arrays)
        self.ahead, self.behind = out[:2]
        return out[2:]


def swap_rows(x):
    return lax.ppermute(x, "blk", [(0, 1), (1, 0)])


def pack_weights(qkv_w, proj_w, up_w, down_w, shares):
    r = qkv_w.shape[0] // shares
    qkv = qkv_w.reshape(shares, r, 3, 3, 2, 128).transpose(0, 3, 1, 4, 2, 5).reshape(shares, 3, r, 768)
    up = up_w.reshape(shares, r, 4, 768).transpose(0, 2, 1, 3)
    down = down_w.reshape(shares, 4, r, 768)
    proj = proj_w.reshape(shares, 1, r, 768)
    return qkv, jnp.concatenate([up, down, proj], axis=1)


def pack_small(gains, shifts, qv_b, out_b, up_b, at):
    flat = jnp.concatenate([gains, shifts, qv_b, out_b], axis=0)
    rows = lax.dynamic_update_slice(jnp.zeros((8, 768), flat.dtype), flat, (0, at))
    hidden = lax.dynamic_update_slice(jnp.zeros((3072,), flat.dtype), up_b, (4 * at,)).reshape(4, 768)
    return jnp.concatenate([rows, hidden, jnp.zeros((4, 768), flat.dtype)], axis=0)


def split_far(blocks, split):
    parts = []
    for t in range(BLOCKS):
        far = t % (BLOCKS // 2) == BLOCKS // 2 - 1
        parts += [blocks[t, :split], blocks[t, split:]] if far else [blocks[t]]
    return parts


def unpack_qkv(blocks, rows):
    return blocks.reshape(3, rows, 2, 3, 128).transpose(1, 3, 0, 2, 4).reshape(rows, 2304)


def unpack_up(blocks, rows):
    return blocks.reshape(4, rows, 768).transpose(1, 0, 2).reshape(rows, 3072)


def shards(tokens, segment_ids, padding_mask, qkv_weight, proj_weight, up_weight, down_weight,
           norm_gain, norm_shift, qv_bias, out_bias, up_bias, cotangent):
    n_dev = lax.axis_size("dp")
    dp, blk = lax.axis_index("dp"), lax.axis_index("blk")
    ring = n_dev == BLOCKS
    n_chips = BLOCKS // 2

    def pick(pair, which):
        return lax.dynamic_index_in_dim(pair, which, 0, keepdims=False)

    tok_own, tok_rx = pick(tokens, blk)[0], swap_rows(pick(tokens, 1 - blk)[0])
    cot_own, cot_send = pick(cotangent, blk)[0], pick(cotangent, 1 - blk)[0]
    seg, pad = pick(segment_ids, blk)[0], pick(padding_mask, blk)[0]
    lanes = jnp.arange(128, dtype=jnp.int32)[None, :]
    code = jnp.where(lanes < 32, seg[:, None] // 32 == lanes, seg[:, None] % 32 + 32 == lanes)
    seg_q = code.astype(BF16)
    allowed = code & (pad[:, None] == 1)
    seg_k = jnp.where(allowed | (lanes >= 64), 0.0, MASKED).astype(BF16)

    if ring:
        qkv_blocks, rest = pack_weights(qkv_weight, proj_weight, up_weight, down_weight, 1)
        small = pack_small(norm_gain, norm_shift, qv_bias, out_bias, up_bias, 48 * dp)
        first = RingGather(jnp.concatenate([qkv_blocks.reshape(144, 768), small], axis=0), 96, n_chips)
        rest = rest.reshape(432, 768)
        for _ in range(4):
            first.step()
            first.arrived()
        rest, _, _ = tie(rest, first.ahead[-1], first.behind[-1])
        parts = first.parts()
        second = RingGather(rest, 192, n_chips)
        order = jnp.asarray(ring_order(n_chips))[dp]
        core = lax.rem(dp, 2)
        chips = jnp.asarray(send_order(n_chips))[dp // 2]
        slots = jnp.asarray(np.argsort(send_order(n_chips), axis=1).astype(np.int32))[dp // 2]
    else:
        whole = [lax.all_gather(w, "dp", axis=0, tiled=True)
                 for w in (qkv_weight, proj_weight, up_weight, down_weight)]
        qkv_blocks, rest = pack_weights(*whole, BLOCKS)
        vectors = [lax.all_gather(w, "dp", axis=1, tiled=True)
                   for w in (norm_gain, norm_shift, qv_bias, out_bias)]
        hidden = lax.all_gather(up_bias, "dp", axis=0, tiled=True)
        small = pack_small(*vectors, hidden, 0)
        small = jnp.concatenate([small[None], jnp.zeros((BLOCKS - 1, 16, 768), BF16)], axis=0)
        parts = split_far(jnp.concatenate([qkv_blocks.reshape(BLOCKS, 144, 768), small], axis=1), 96)
        rest_parts = split_far(rest.reshape(BLOCKS, 432, 768), 192)
        order = jnp.arange(BLOCKS, dtype=jnp.int32)
        core = jnp.int32(0)
        chips = slots = jnp.arange(n_chips, dtype=jnp.int32)
    idx = jnp.concatenate([order, jnp.stack([blk, core]).astype(jnp.int32), chips, slots])
    if ring:
        second.step()
    outs = attn_forward(0, idx, parts, (tok_own, tok_rx), seg_q, seg_k)
    heads, nrm, small_all = [list(outs[:7])], outs[7], outs[8]
    for quad in (1, 2):
        if ring:
            nrm, small_all, cot_send, heads[-1][3] = second.tie(nrm, small_all, cot_send, heads[-1][3])
            second.step()
        if quad == 1:
            cot_rx = swap_rows(cot_send)
            cot_send = cot_rx
        heads.append(list(attn_forward(quad, idx, parts, (nrm, small_all), seg_q, seg_k)))
    cot_rx = cot_send
    atts = [h[3] for h in heads]
    if ring:
        atts[2], small_all = second.tie(atts[2], small_all)
        second.step()
        (atts[2],) = second.tie(atts[2])
        rest_parts = second.parts()
    lo_mine, lo_theirs, d_mid, d_att, *sends, sums = ffn(
        idx, rest_parts, atts, tok_own, tok_rx, cot_own, cot_rx, small_all)
    lo_rx = swap_rows(lo_theirs)

    groups = ((0,), (1, 2), (3, 4), (5,))
    heads = [[h[0], h[1], h[2], h[3], h[4], h[5], h[6]] for h in heads]
    if ring:
        ffn_sum = RingReduce(*sends, 224, n_chips)
        (d_att,) = ffn_sum.tie(d_att)
        ffn_sum.send()
    d_ni, b0, *q_sends = attn_backward(groups[0], idx, heads, d_att, nrm)
    biases = [b0]
    for group in groups[1:]:
        if ring:
            d_ni, ffn_sum.far, lo_rx = ffn_sum.tie(d_ni, ffn_sum.far, lo_rx)
            ffn_sum.add()
            (d_ni,) = ffn_sum.tie(d_ni)
            ffn_sum.send()
        if group is not groups[-1]:
            d_ni, b, *q_sends = attn_backward(group, idx, heads, d_att, nrm, d_ni, q_sends)
            biases.append(b)
    gt_mine, gt_theirs, *q_sends = attn_backward(
        groups[-1], idx, heads, d_att, nrm, d_ni, q_sends,
        tail=(tok_own, tok_rx, d_mid, small_all, sums, *biases))

    def together(own_half, other_half):
        swapped = blk == 1
        return jnp.stack([jnp.where(swapped, other_half, own_half),
                          jnp.where(swapped, own_half, other_half)])[:, None]

    if ring:
        gt_theirs, *q_sends = ffn_sum.tie(gt_theirs, *q_sends)
        gt_rx = swap_rows(gt_theirs)
        qkv_sum = RingReduce(*q_sends, 80, n_chips)
        qkv_sum.send()
        ffn_sum.add()
        qkv_sum.add()
        (ffn_sum.total,) = qkv_sum.tie(ffn_sum.total)
        qkv_sum.send()
        ffn_rx = swap_rows(ffn_sum.total)
        qkv_sum.add()
        qkv_sum.send()
        (gt_rx,) = qkv_sum.tie(gt_rx)
        qkv_sum.add()
        qkv_sum.send()
        qkv_sum.add()
        gt_rx, lo_rx, _ = tie(gt_rx, lo_rx, qkv_sum.total)
        ffn_rx, _ = tie(ffn_rx, qkv_sum.total)
        done_ffn = ffn_sum.total.astype(F32) + ffn_rx.astype(F32)
        done_qkv = qkv_sum.total.astype(F32) + swap_rows(qkv_sum.total).astype(F32)
        r = 48
        small = done_qkv[144:160]
        own = lax.dynamic_slice_in_dim(small[0:8], 48 * dp, 48, 1)
        g_bias = lax.dynamic_slice_in_dim(small[8:12].reshape(3072), 192 * dp, 192, 0)
        return (together(lo_mine, lo_rx), together(gt_mine, gt_rx),
                unpack_qkv(done_qkv[0:144], r), done_ffn[384:432], unpack_up(done_ffn[0:192], r), done_ffn[192:384],
                own[0:2], own[2:4], own[4:6], own[6:8], g_bias)

    gt_rx = swap_rows(gt_theirs)

    def whole_sum(mine, near, far):
        return jnp.stack([mine, jnp.concatenate([near, far])], axis=1).reshape(BLOCKS, mine.shape[1], 768)

    def scatter(x, dim):
        part = lax.psum_scatter(x, "dp", scatter_dimension=dim, tiled=True)
        return lax.psum(part.astype(BF16), "blk").astype(F32)

    g_ffn, g_q = whole_sum(*sends), whole_sum(*q_sends)
    g_up = g_ffn[:, 0:192].reshape(BLOCKS, 4, 48, 768).transpose(0, 2, 1, 3).reshape(768, 3072)
    g_down = g_ffn[:, 192:384].reshape(3072, 768)
    g_proj = g_ffn[:, 384:432].reshape(768, 768)
    g_qkv = jnp.stack([g_q[:, 48 * j : 48 * j + 48].reshape(768, 768) for j in range(3)])
    g_small = g_q[0, 144:160].astype(F32)
    g_bias = g_small[8:12].reshape(-1)
    big = [scatter(g.astype(F32), 0) for g in (unpack_qkv(g_qkv, 768), g_proj, g_up, g_down)]
    return (together(lo_mine, lo_rx), together(gt_mine, gt_rx), *big,
            *[scatter(g_small[2 * i : 2 * i + 2], 1) for i in range(4)], scatter(g_bias, 0))


def solution(mesh):
    rows = P(None, "dp", "blk", None)
    return jax.shard_map(
        shards,
        mesh=mesh,
        in_specs=(rows, P(None, "dp", None), P(None, "dp", None)) + (P("dp", None),) * 4
        + (P(None, "dp"),) * 4 + (P("dp"), rows),
        out_specs=(rows, rows) + (P("dp", None),) * 4 + (P(None, "dp"),) * 4 + (P("dp"),),
        check_vma=False,
    )
```

```python
import functools

import jax
import jax.numpy as jnp
import numpy as np
from jax import lax
from jax.experimental import pallas as pl
from jax.experimental.pallas import tpu as pltpu
from jax.sharding import PartitionSpec as P

HD = 64
BLOCKS = 16
N_PARTS = BLOCKS + 2
NT = (((1,), (1,)), ((), ()))
TN = (((0,), (0,)), ((), ()))
F32 = jnp.float32
BF16 = jnp.bfloat16
ANY = pl.BlockSpec(memory_space=pl.ANY)
SMEM = pl.BlockSpec(memory_space=pltpu.SMEM)
VMEM_LIMIT = 60 << 20
MASKED = -1e30


def dot(a, b, dims=(((1,), (0,)), ((), ()))):
    return lax.dot_general(a, b, dims, preferred_element_type=F32)


def cost(us):
    return pl.CostEstimate(flops=int(us * 1.1e9), bytes_accessed=1 << 20, transcendentals=0)


def full(shape):
    return pl.BlockSpec(shape, lambda *_: (0,) * len(shape))


def params():
    return pltpu.CompilerParams(vmem_limit_bytes=VMEM_LIMIT)


def norm_stats(x):
    mean = jnp.mean(x, axis=1, keepdims=True)
    center = x - mean
    rstd = lax.rsqrt(jnp.mean(center * center, axis=1, keepdims=True) + 1e-05)
    return center * rstd, rstd


def norm_back(e, nhat, rstd):
    return (
        e - jnp.mean(e, axis=1, keepdims=True) - nhat * jnp.mean(e * nhat, axis=1, keepdims=True)
    ) * rstd


def row_sum(x):
    return jnp.sum(x, axis=0, keepdims=True)


def send_copies(idx, buf, rows, sends, sem, lanes=slice(None)):
    core = idx[17]
    copies = []
    mine, *others = sends
    slots = [other.at[i] for other in others for i in range(other.shape[0])]
    for slot, theirs in enumerate(slots):
        chip = idx[18 + slot]
        copies.append(pltpu.make_async_copy(buf.at[chip, core], mine.at[slot, rows, lanes], sem.at[0, slot]))
        copies.append(pltpu.make_async_copy(buf.at[chip, 1 - core], theirs.at[rows, lanes], sem.at[1, slot]))
    return copies


def part_copies(parts, split, start, size, place, sem, piece=None):
    copies = []
    n = BLOCKS // 2
    for t in range(BLOCKS):
        group = parts[(n + 1) * (t // n) : (n + 1) * (t // n + 1)]
        if t % n < n - 1:
            src, at = group[t % n], start
        elif piece == 0 or (piece is None and start < split):
            src, at = group[n - 1], start
        else:
            src, at = group[n], start - split
        copies.append(pltpu.make_async_copy(src.at[pl.ds(at, size), :], place(t), sem(t)))
    return copies


def send_shapes(rows, cuts):
    return [jax.ShapeDtypeStruct((n, rows, 768), BF16) for n in (BLOCKS // 2, *cuts)]


def attn_forward_body(quad, block, idx, *refs):
    first = quad == 0
    parts, refs = refs[:N_PARTS], refs[N_PARTS:]
    if first:
        (tok_own, tok_rx, sq, sk, q_o, k_o, v_o, att_o, li_o, e_o, w_o, nrm_o, small_o,
         w_s, s_s, kk, vv, aa, sem) = refs
    else:
        (nrm_i, small_i, sq, sk, q_o, k_o, v_o, att_o, li_o, e_o, w_o,
         w_s, kk, vv, aa, sem) = refs
    seq = sq.shape[0]
    half = seq // 2
    pair = pl.program_id(0)

    @pl.when(pair == 0)
    def _():
        copies = part_copies(parts, 96, 48 * quad, 48, lambda t: w_s.at[idx[t]], lambda t: sem.at[0, t])
        if first:
            copies += part_copies(parts, 96, 144, 16, lambda t: s_s.at[t], lambda t: sem.at[1, t])
        for c in copies:
            c.start()
        for c in copies:
            c.wait()
        weight = w_s[...].reshape(768, 768)
        w_o[0], w_o[1] = weight[:, :384], weight[:, 384:]
        if first:
            small = jnp.zeros((16, 768), F32)
            for t in range(BLOCKS):
                small = small + s_s[t].astype(F32)
            small_o[...] = small
            gain, shift = small[0:1], small[2:3]
            for src, where in ((tok_own, idx[16]), (tok_rx, 1 - idx[16])):
                base = pl.multiple_of(where * half, half)
                for i in range(0, half, block):
                    nhat, _rstd = norm_stats(src[i : i + block, :].astype(F32))
                    nrm_o[pl.ds(base + i, block), :] = (nhat * gain + shift).astype(BF16)
            nrm = nrm_o
            bq, bv = small[4:5, 0:256], small[5:6, 0:256]
        else:
            nrm = nrm_i
            cols = slice(256 * quad, 256 * quad + 256)
            bq, bv = small_i[4:5, cols], small_i[5:6, cols]
        for i in range(0, seq, block):
            rows = slice(i, i + block)
            joined = dot(nrm[rows, :], weight)
            for p in range(2):
                c, to = 384 * p, slice(128 * p, 128 * p + 128)
                q_o[p, rows, :] = (joined[:, c : c + 128] + bq[:, to]).astype(BF16)
                k_o[p, rows, :] = joined[:, c + 128 : c + 256].astype(BF16)
                v_o[p, rows, :] = (joined[:, c + 256 : c + 384] + bv[:, to]).astype(BF16)

    head = lax.broadcasted_iota(jnp.int32, (seq, 128), 1) // HD
    k_pair, v_pair = k_o[pair], v_o[pair]
    zero, one = jnp.zeros((seq, 128), BF16), jnp.ones((seq, 128), BF16)
    for h in range(2):
        mine = head == h
        kk[h, :, 0:128] = jnp.where(mine, k_pair, zero)
        kk[h, :, 128:256] = sk[...]
        vv[h, :, 0:128] = jnp.where(mine, v_pair, zero)
        vv[h, :, 128:256] = jnp.where(mine, one, zero)
    aa[:, 0:128] = q_o[pair] * BF16(0.125)
    aa[:, 128:256] = sq[...]
    for i in range(0, seq, block):
        rows = slice(i, i + block)
        acc = None
        for h in range(2):
            s = dot(aa[rows, :], kk[h], NT)
            e = jnp.exp(s - jnp.max(s, axis=1, keepdims=True)).astype(BF16)
            e_o[h, rows, :] = e
            o = dot(e, vv[h])
            acc = o if acc is None else acc + o
        inverse = 1.0 / acc[:, 128:256]
        li_o[0, rows, :] = inverse
        att_o[0, rows, :] = (acc[:, 0:128] * inverse).astype(BF16)


def attn_forward(quad, idx, parts, rows_in, sq, sk):
    seq = sq.shape[0]
    sds = jax.ShapeDtypeStruct
    first = quad == 0
    pair_block = pl.BlockSpec((1, seq, 128), lambda p: (p, 0, 0))
    quad_block = full((2, seq, 128))
    out_shape = [
        sds((2, seq, 128), BF16),
        sds((2, seq, 128), BF16),
        sds((2, seq, 128), BF16),
        sds((2, seq, 128), BF16),
        sds((2, seq, 128), F32),
        sds((4, seq, seq), BF16),
        sds((2, 768, 384), BF16),
    ]
    out_specs = [
        quad_block, quad_block, quad_block, pair_block, pair_block,
        pl.BlockSpec((2, seq, seq), lambda p: (p, 0, 0)), full((2, 768, 384)),
    ]
    scratch = [pltpu.VMEM((BLOCKS, 48, 768), BF16)]
    if first:
        out_shape += [sds((seq, 768), BF16), sds((16, 768), F32)]
        out_specs += [full((seq, 768)), full((16, 768))]
        scratch += [pltpu.VMEM((BLOCKS, 16, 768), BF16)]
    scratch += [
        pltpu.VMEM((2, seq, 256), BF16),
        pltpu.VMEM((2, seq, 256), BF16),
        pltpu.VMEM((seq, 256), BF16),
        pltpu.SemaphoreType.DMA((2, BLOCKS)),
    ]
    return pl.pallas_call(
        functools.partial(attn_forward_body, quad, 256),
        grid=(2,),
        in_specs=[SMEM] + [ANY] * N_PARTS
        + [full(r.shape) for r in rows_in]
        + [full(sq.shape), full(sk.shape)],
        out_specs=out_specs,
        out_shape=out_shape,
        scratch_shapes=scratch,
        compiler_params=params(),
        cost_estimate=cost(11),
    )(idx, *parts, *rows_in, sq, sk)


def ffn_body(
    block, idx, *refs
):
    parts, refs = refs[:N_PARTS], refs[N_PARTS:]
    ffn_steps(block, idx, parts, *refs)


def ffn_steps(
    block, idx, parts, att0, att1, att2, tok_own, tok_rx, cot_own, cot_rx, small,
    lo_mine, lo_theirs, dmid_o, datt_o, g_mine, g_near, g_mid, g_far, sums_o,
    up_s, dn_s, proj_s, att_s, mid_s, nm_s, nmt_s, cot_s, act_s, dp_s, oacc, dacc, dbr_s, gup_s, gdn_s, gproj,
    lo_s, datt_s, wsem, dsem, psem, gsem, gdsem, gpsem, osem,
):
    c = pl.program_id(0)
    n_c = pl.num_programs(0)
    slot = lax.rem(c, 2)
    seq = mid_s.shape[0]
    half = seq // 2
    core = idx[17]

    def up_copies(chunk, s):
        rows = pl.multiple_of(chunk * 48, 48)
        return part_copies(parts, 0, rows, 48, lambda t: up_s.at[s, idx[t]], lambda t: wsem.at[s, t], piece=0)

    def down_copies():
        return part_copies(parts, 192, 192, 192, lambda t: dn_s.at[idx[t]], lambda t: dsem.at[idx[t]])

    def grad_copies(chunk, s, act):
        rows = pl.ds(pl.multiple_of(chunk * 48, 48), 48)
        for copy in send_copies(idx, gup_s.at[s], rows, (g_mine, g_near, g_mid, g_far), gsem.at[s]):
            act(copy)
        rows = pl.ds(192, 192)
        for j in range(2):
            slot_to = idx[26 + 2 * chunk + j]
            act(pltpu.make_async_copy(gdn_s.at[s, j, core], g_mine.at[slot_to, rows, :], gdsem.at[s, 0, j]))

            @pl.when(slot_to == 0)
            def _():
                act(pltpu.make_async_copy(gdn_s.at[s, j, 1 - core], g_near.at[0, rows, :], gdsem.at[s, 1, j]))

            @pl.when((slot_to > 0) & (slot_to < 3))
            def _():
                act(pltpu.make_async_copy(gdn_s.at[s, j, 1 - core], g_mid.at[slot_to - 1, rows, :], gdsem.at[s, 1, j]))

            @pl.when(slot_to >= 3)
            def _():
                act(pltpu.make_async_copy(gdn_s.at[s, j, 1 - core], g_far.at[slot_to - 3, rows, :], gdsem.at[s, 1, j]))

    def start(copy):
        copy.start()

    def wait(copy):
        copy.wait()

    @pl.when(c == 0)
    def _():
        proj_copies = part_copies(parts, 192, 384, 48, lambda t: proj_s.at[idx[t]], lambda t: psem.at[t])
        for copy in proj_copies + up_copies(c, 0) + down_copies():
            copy.start()
        for src, where in ((tok_own, idx[16]), (tok_rx, 1 - idx[16])):
            base = pl.multiple_of(where * half, half)
            mid_s[pl.ds(base, half), :] = src[...].astype(F32)
        for src, where in ((cot_own, idx[16]), (cot_rx, 1 - idx[16])):
            base = pl.multiple_of(where * half, half)
            cot_s[pl.ds(base, half), :] = src[...]
        for j, a in enumerate((att0, att1, att2)):
            for p in range(2):
                att_s[:, 256 * j + 128 * p : 256 * j + 128 * p + 128] = a[p]
        for copy in proj_copies:
            copy.wait()
        proj = proj_s[...].reshape(768, 768)
        for i in range(0, seq, block):
            rows = slice(i, i + block)
            mid = mid_s[rows, :] + (dot(att_s[rows, :], proj) + small[6:7])
            mid_s[rows, :] = mid
            oacc[rows, :] = mid + small[7:8]
            dacc[rows, :] = jnp.zeros((block, 768), F32)
            nhat, _rstd = norm_stats(mid)
            nm_s[rows, :] = (nhat * small[1:2] + small[3:4]).astype(BF16)
        nmt_s[...] = nm_s[...].T

    for copy in up_copies(c, slot):
        copy.wait()
    for j in range(4):
        owner = 4 * c + j
        pltpu.make_async_copy(parts[0].at[pl.ds(192, 192), :], dn_s.at[owner], dsem.at[owner]).wait()

    @pl.when(c + 1 < n_c)
    def _():
        for copy in up_copies(c + 1, 1 - slot):
            copy.start()

    up = up_s[slot].reshape(768, 768)
    dn = dn_s[pl.ds(4 * c, 4)].reshape(768, 768)
    bias = small[pl.ds(8 + c, 1), :]
    bias_sum = None
    for i in range(0, seq, block):
        rows = slice(i, i + block)
        pre = dot(nm_s[rows, :], up) + bias
        cdf = 0.5 * (1.0 + lax.erf(pre * 0.7071067811865476))
        act = (pre * cdf).astype(BF16)
        act_s[rows, :] = act
        oacc[rows, :] += dot(act, dn)
        slope = cdf + pre * (jnp.exp(pre * pre * -0.5) * 0.3989422804014327)
        d_pre = (dot(cot_s[rows, :], dn, NT) * slope).astype(BF16)
        dp_s[rows, :] = d_pre
        part = row_sum(d_pre.astype(F32))
        bias_sum = part if bias_sum is None else bias_sum + part
        dacc[rows, :] += dot(d_pre, up, NT)
    sums_o[pl.ds(8 + c, 1), :] = bias_sum

    @pl.when(c >= 2)
    def _():
        grad_copies(c - 2, slot, wait)

    gup_s[slot] = dot(nmt_s[...], dp_s[...]).astype(BF16).reshape(BLOCKS // 2, 2, 48, 768)
    gdn_s[slot] = dot(act_s[...], cot_s[...], TN).astype(BF16).reshape(2, 2, 192, 768)
    grad_copies(c, slot, start)

    @pl.when(c == n_c - 1)
    def _():
        proj = proj_s[...].reshape(768, 768)
        gain_sum = shift_sum = bout_sum = bdown_sum = None
        out_copies = []

        def send_out(src, dst, n):
            out_copies.append(pltpu.make_async_copy(src, dst, osem.at[n]))
            out_copies[-1].start()

        lo_s[...] = oacc[...].astype(BF16)
        for n, (dst, where) in enumerate(((lo_mine, idx[16]), (lo_theirs, 1 - idx[16]))):
            send_out(lo_s.at[pl.ds(pl.multiple_of(where * half, half), half), :], dst, n)
        for i in range(0, seq, block):
            rows = slice(i, i + block)
            mid = mid_s[rows, :]
            cot = cot_s[rows, :].astype(F32)
            d_nm = dacc[rows, :]
            nhat, rstd = norm_stats(mid)
            d_mid = cot + norm_back(d_nm * small[1:2], nhat, rstd)
            mid_s[rows, :] = d_mid
            send_out(mid_s.at[pl.ds(i, block), :], dmid_o.at[pl.ds(i, block), :], 2 + i // block)
            d_branch = d_mid.astype(BF16)
            dbr_s[rows, :] = d_branch
            d_att = dot(d_branch, proj, NT).astype(BF16)
            for p in range(6):
                datt_s[p, rows, :] = d_att[:, 128 * p : 128 * p + 128]
            send_out(datt_s.at[:, pl.ds(i, block), :], datt_o.at[:, pl.ds(i, block), :], 2 + (seq + i) // block)
            parts = [row_sum(d_nm * nhat), row_sum(d_nm), row_sum(d_branch.astype(F32)), row_sum(cot)]
            if gain_sum is None:
                gain_sum, shift_sum, bout_sum, bdown_sum = parts
            else:
                gain_sum, shift_sum = gain_sum + parts[0], shift_sum + parts[1]
                bout_sum, bdown_sum = bout_sum + parts[2], bdown_sum + parts[3]
        sums_o[0:8, :] = jnp.concatenate(
            [jnp.zeros_like(gain_sum), gain_sum, jnp.zeros_like(gain_sum), shift_sum,
             jnp.zeros_like(gain_sum), jnp.zeros_like(gain_sum), bout_sum, bdown_sum], axis=0)
        sums_o[12:16, :] = jnp.zeros((4, 768), F32)
        gproj[...] = dot(att_s[...], dbr_s[...], TN).astype(BF16).reshape(BLOCKS // 2, 2, 48, 768)
        last = send_copies(idx, gproj, pl.ds(384, 48), (g_mine, g_near, g_mid, g_far), gpsem)
        for copy in last:
            copy.start()
        grad_copies(c - 1, 1 - slot, wait)
        grad_copies(c, slot, wait)
        for copy in out_copies + last:
            copy.wait()


def ffn(idx, parts, atts, tok_own, tok_rx, cot_own, cot_rx, small):
    seq = 2 * tok_own.shape[0]
    sds = jax.ShapeDtypeStruct
    v = pltpu.VMEM
    half = tok_own.shape
    rows, frows = v((seq, 768), BF16), v((seq, 768), F32)
    return pl.pallas_call(
        functools.partial(ffn_body, 256),
        grid=(4,),
        in_specs=[SMEM] + [ANY] * N_PARTS + [full((2, seq, 128))] * 3 + [full(half)] * 4 + [full((16, 768))],
        out_specs=[ANY] * 8 + [full((16, 768))],
        out_shape=[
            sds(half, BF16), sds(half, BF16), sds((seq, 768), F32), sds((6, seq, 128), BF16),
            *send_shapes(432, (1, 2, 5)), sds((16, 768), F32),
        ],
        scratch_shapes=[
            v((2, BLOCKS, 48, 768), BF16), v((BLOCKS, 192, 768), BF16), v((BLOCKS, 48, 768), BF16),
            rows, frows, rows, v((768, seq), BF16), rows, rows, rows, frows, frows, rows,
            v((2, BLOCKS // 2, 2, 48, 768), BF16), v((2, 2, 2, 192, 768), BF16), v((BLOCKS // 2, 2, 48, 768), BF16),
            rows, v((6, seq, 128), BF16), pltpu.SemaphoreType.DMA((2, BLOCKS)), pltpu.SemaphoreType.DMA((BLOCKS,)), pltpu.SemaphoreType.DMA((BLOCKS,)),
            pltpu.SemaphoreType.DMA((2, 2, BLOCKS // 2)), pltpu.SemaphoreType.DMA((2, 2, 2)),
            pltpu.SemaphoreType.DMA((2, BLOCKS // 2)), pltpu.SemaphoreType.DMA((2 + 2 * seq // 256,)),
        ],
        compiler_params=params(),
        cost_estimate=cost(50),
    )(idx, *parts, *atts, tok_own, tok_rx, cot_own, cot_rx, small)


def attn_backward_body(pairs, block, idx, *refs):
    n = len(pairs)
    start_pair, last = pairs[0] == 0, pairs[-1] == 5
    heads, refs = [refs[7 * j : 7 * j + 7] for j in range(n)], refs[7 * n :]
    (do_h, nrm_h), refs = refs[:2], refs[2:]
    if not start_pair:
        dni_h, refs = refs[0], refs[4:]
    if last:
        (tok_own, tok_rx, dmid_h, small, sums_i, *b_in), refs = refs[:8], refs[8:]
        (gt_mine, gt_first, gt_second, *sends), refs = refs[:6], refs[6:]
    else:
        (dni_o, b_o, *sends), refs = refs[:5], refs[5:]
    (q_s, k_s, v_s, o_s, do_s, li_s, e_s, w_s, nrm_s, dni_s, vv, kk, dd, qm, dm, dkt, dvt, dj, gbuf,
     isem, esem, wsem, gsem), refs = refs[:23], refs[23:]
    seq = q_s.shape[1]
    half = seq // 2
    n_block = seq // block
    copy = pltpu.make_async_copy
    lane = lax.broadcasted_iota(jnp.int32, (seq, 128), 1)
    side = lax.broadcasted_iota(jnp.int32, (128, seq), 0)

    heads_in, e_in, late = [], [], []
    for j, (q_h, k_h, v_h, o_h, li_h, e_h, w_h) in enumerate(heads):
        odd = pairs[j] % 2
        heads_in.append([
            copy(src.at[at], dst.at[j], isem.at[j, m])
            for m, (src, dst, at) in enumerate((
                (v_h, v_s, odd), (do_h, do_s, pairs[j]), (li_h, li_s, odd), (o_h, o_s, odd),
                (k_h, k_s, odd), (q_h, q_s, odd)))
        ])
        e_in.append([
            copy(e_h.at[pl.ds(2 * odd, 2), pl.ds(i * block, block), :],
                 e_s.at[pl.ds(2 * j, 2), pl.ds(i * block, block), :], esem.at[j, i])
            for i in range(n_block)
        ])
        late.append(copy(w_h.at[odd], w_s.at[:, pl.ds(384 * j, 384)], wsem.at[j]))
    late.append(copy(nrm_h, nrm_s, wsem.at[2]))
    if not start_pair:
        late.append(copy(dni_h, dni_s, wsem.at[3]))
    if last:
        dmid_s, sbuf = refs
        late.append(copy(dmid_h, dmid_s, wsem.at[4]))
    for c in heads_in[0] + e_in[0][:2]:
        c.start()
    queue = e_in[0][2:]
    for j in range(1, n):
        queue = queue + heads_in[j] + e_in[j]
    queue = queue + late
    per_block = -(-len(queue) // n_block)

    for pair in range(n):
        for c in heads_in[pair]:
            c.wait()
        d_out = do_s[pair].astype(F32) * li_s[pair]
        d_low = d_out.astype(BF16)
        prod = d_out * o_s[pair].astype(F32)
        extra = jnp.zeros((seq, 128), F32)
        q_t, d_t = q_s[pair].T, d_low.T
        zero = jnp.zeros((seq, 128), BF16)
        zero_t = jnp.zeros((128, seq), BF16)
        for h in range(2):
            mine = (lane // HD) == h
            delta = jnp.sum(jnp.where(mine, prod, 0.0), axis=1, keepdims=True)
            high = delta.astype(BF16).astype(F32)
            extra = jnp.where(lane == 2 * h, -high, extra)
            extra = jnp.where(lane == 2 * h + 1, high - delta, extra)
            vv[h, :, 0:128] = jnp.where(mine, v_s[pair], zero)
            vv[h, :, 128:256] = jnp.where((lane // 2) == h, 1.0, 0.0).astype(BF16)
            kk[h] = jnp.where(mine, k_s[pair], zero)
            mine_t = (side // HD) == h
            qm[h] = jnp.where(mine_t, q_t, zero_t)
            dm[h] = jnp.where(mine_t, d_t, zero_t)
        dd[:, 0:128] = d_low
        dd[:, 128:256] = extra.astype(BF16)
        base = 384 * pair
        for i in range(n_block):
            e_in[pair][i].wait()
            for c in queue[:per_block]:
                c.start()
            queue = queue[per_block:]
            rows = slice(i * block, i * block + block)
            dq = None
            for h in range(2):
                dp = dot(dd[rows, :], vv[h], NT)
                e = e_s[2 * pair + h, rows, :]
                ds = dp.astype(BF16) * e
                t = dot(ds, kk[h])
                dq = t if dq is None else dq + t
                a, b = dot(qm[h, :, rows], ds), dot(dm[h, :, rows], e)
                if i == 0 and h == 0:
                    dkt[...], dvt[...] = a, b
                else:
                    dkt[...] += a
                    dvt[...] += b
            dj[rows, base : base + 128] = (dq * 0.125).astype(BF16)
        dj[:, base + 128 : base + 256] = (dkt[...] * 0.125).astype(BF16).T
        dj[:, base + 256 : base + 384] = dvt[...].astype(BF16).T

    for c in late:
        c.wait()
    grads = dot(nrm_s[...], dj[...], TN).astype(BF16)
    copies, bq, bv = [], [], []
    for j, p in enumerate(pairs):
        c = 384 * j
        gbuf[j] = grads[:, c : c + 384].reshape(BLOCKS // 2, 2, 48, 384)
        copies += send_copies(idx, gbuf.at[j], pl.ds(48 * (p // 2), 48), sends, gsem.at[j],
                              pl.ds(384 * (p % 2), 384))
        bq.append(row_sum(dj[:, c : c + 128].astype(F32)))
        bv.append(row_sum(dj[:, c + 256 : c + 384].astype(F32)))
    for c in copies:
        c.start()
    weight = w_s[...]
    if not last:
        both = jnp.concatenate(
            [jnp.concatenate(bq, axis=1), jnp.concatenate(bv, axis=1), jnp.zeros((6, 128 * n), F32)], axis=0)
        b_o[...] = both
        for i in range(n_block):
            rows = slice(i * block, i * block + block)
            d_ni = dot(dj[rows, :], weight, NT)
            dni_s[rows, :] = d_ni if start_pair else dni_s[rows, :] + d_ni
            out = copy(dni_s.at[pl.ds(i * block, block), :], dni_o.at[pl.ds(i * block, block), :], esem.at[0, i])
            out.start()
            copies.append(out)
    else:
        gain = small[0:1]
        gain_sum = shift_sum = None
        for src, dsts, where in ((tok_rx, (gt_first, gt_second), 1 - idx[16]), (tok_own, (gt_mine,), idx[16])):
            start = pl.multiple_of(where * half, half)
            for i in range(0, half, block):
                rows = pl.ds(start + i, block)
                d_ni = dni_s[rows, :] + dot(dj[rows, :], weight, NT)
                nhat, rstd = norm_stats(src[i : i + block, :].astype(F32))
                grad = dmid_s[rows, :] + norm_back(d_ni * gain, nhat, rstd)
                dst = dsts[i * len(dsts) // half]
                at = i % dst.shape[0]
                dst[at : at + block, :] = grad.astype(BF16)
                parts = [row_sum(d_ni * nhat), row_sum(d_ni)]
                if gain_sum is None:
                    gain_sum, shift_sum = parts
                else:
                    gain_sum, shift_sum = gain_sum + parts[0], shift_sum + parts[1]
        sums = sums_i[...]
        row = lax.broadcasted_iota(jnp.int32, (16, 768), 0)
        sums = jnp.where(row == 0, gain_sum, sums)
        sums = jnp.where(row == 2, shift_sum, sums)
        sums = jnp.where(row == 4, jnp.concatenate([b[0:1, :] for b in b_in] + bq, axis=1), sums)
        sums = jnp.where(row == 5, jnp.concatenate([b[1:2, :] for b in b_in] + bv, axis=1), sums)
        low = sums.astype(BF16)
        for t in range(BLOCKS // 2):
            sbuf[t, 0], sbuf[t, 1] = low, low
        more = send_copies(idx, sbuf, pl.ds(144, 16), sends, gsem.at[1])
        for c in more:
            c.start()
        copies += more
    for c in copies:
        c.wait()


def attn_backward(pairs, idx, heads, d_att, nrm, d_ni=None, grads=None, tail=None):
    n, first, last = len(pairs), pairs[0] == 0, tail is not None
    seq = nrm.shape[0]
    half = (seq // 2, 768)
    block = 256
    sds = jax.ShapeDtypeStruct
    vm = pltpu.VMEM
    whole = pl.BlockSpec(memory_space=pltpu.VMEM)
    args = [idx]
    for p in pairs:
        args += heads[p // 2]
    args += [d_att, nrm]
    in_specs = [SMEM] + [ANY] * (len(args) - 1)
    alias = {}
    if not first:
        args.append(d_ni)
        in_specs.append(ANY)
        if not last:
            alias[len(args) - 1] = 0
        for j, g in enumerate(grads):
            args.append(g)
            in_specs.append(ANY)
            alias[len(args) - 1] = 2 + j + last
    if last:
        args += list(tail)
        in_specs += [whole, whole, ANY] + [whole] * (len(tail) - 3)
        quarter = sds((seq // 4, 768), BF16)
        out_shape = [sds(half, BF16), quarter, quarter]
        out_specs = [whole, whole, whole]
    else:
        out_shape = [sds((seq, 768), F32), sds((8, 128 * n), F32)]
        out_specs = [ANY, whole]
    out_shape += send_shapes(160, (1, 7))
    out_specs += [ANY] * 3
    pair = vm((n, seq, 128), BF16)
    dma = pltpu.SemaphoreType.DMA
    scratch = [
        pair, pair, pair, pair, pair, vm((n, seq, 128), F32), vm((2 * n, seq, seq), BF16), vm((768, 384 * n), BF16),
        vm((seq, 768), BF16), vm((seq, 768), F32),
        vm((2, seq, 256), BF16), vm((2, seq, 128), BF16), vm((seq, 256), BF16), vm((2, 128, seq), BF16),
        vm((2, 128, seq), BF16), vm((128, seq), F32), vm((128, seq), F32), vm((seq, 384 * n), BF16),
        vm((n, BLOCKS // 2, 2, 48, 384), BF16), dma((n, 6)), dma((n, seq // block)), dma((5,)),
        dma((2, 2, BLOCKS // 2)),
    ]
    if last:
        scratch += [vm((seq, 768), F32), vm((BLOCKS // 2, 2, 16, 768), BF16)]
    return pl.pallas_call(
        functools.partial(attn_backward_body, pairs, block),
        in_specs=in_specs,
        out_specs=out_specs,
        out_shape=out_shape,
        scratch_shapes=scratch,
        input_output_aliases=alias,
        compiler_params=params(),
        cost_estimate=cost(8 * n),
    )(*args)


def chip_cycle(n_chips):
    rows = n_chips // 2
    return [2 * i for i in range(rows)] + [2 * i + 1 for i in reversed(range(rows))]


def chip_shift(n_chips, step):
    order = chip_cycle(n_chips)
    return [
        (2 * order[i] + core, 2 * order[(i + step) % n_chips] + core)
        for i in range(n_chips)
        for core in (0, 1)
    ]


def core_swap(n_dev):
    return [(i, i ^ 1) for i in range(n_dev)]


def tie(*arrays):
    return lax.optimization_barrier(arrays)


class RingGather:
    def __init__(self, x, split, n_chips):
        self.n, self.split, self.ahead, self.behind = n_chips, split, [x], [x]
        self.other = [self.swap(x)]
        self.waiting = []

    def swap(self, x):
        return lax.ppermute(x, "dp", core_swap(2 * self.n))

    def step(self):
        a, b = self.ahead[-1], self.behind[-1]
        if len(self.ahead) == self.n // 2:
            a, b = a[: self.split], b[self.split :]
        self.ahead.append(lax.ppermute(a, "dp", chip_shift(self.n, 1)))
        self.behind.append(lax.ppermute(b, "dp", chip_shift(self.n, -1)))

    def tie(self, *arrays):
        a, b, *rest = tie(self.ahead[-1], self.behind[-1], *self.other[-2:], *arrays)
        self.ahead[-1], self.behind[-1] = a, b
        n = len(self.other[-2:])
        self.other[-n:], rest = rest[:n], rest[n:]
        self.other += [self.swap(a), self.swap(b)]
        return rest

    def arrived(self):
        self.other += [self.swap(self.ahead[-1]), self.swap(self.behind[-1])]

    def parts(self):
        def in_order(ahead, behind):
            return [ahead[0]] + ahead[1:-1] + behind[1:-1] + [ahead[-1], behind[-1]]

        o = self.other
        return in_order(self.ahead, self.behind) + in_order(o[:1] + o[1::2], o[:1] + o[2::2])


def ring_order(n_chips):
    order = chip_cycle(n_chips)
    table = np.zeros((2 * n_chips, 2 * n_chips), np.int32)
    far = n_chips // 2
    steps = list(range(0, -far, -1)) + list(range(1, far)) + [far]
    for chip in range(n_chips):
        pos = order.index(chip)
        chips = [order[(pos + s) % n_chips] for s in steps]
        for core in (0, 1):
            table[2 * chip + core] = [2 * q + core for q in chips] + [2 * q + 1 - core for q in chips]
    return table


def send_order(n_chips):
    order = chip_cycle(n_chips)
    steps = [n_chips // 2]
    for t in range(n_chips // 2 - 1, 0, -1):
        steps += [t, -t]
    steps.append(0)
    table = np.zeros((n_chips, n_chips), np.int32)
    for chip in range(n_chips):
        table[chip] = [order[(order.index(chip) + s) % n_chips] for s in steps]
    return table


class RingReduce:
    def __init__(self, mine, near, mid, far, split, n_chips):
        self.n, self.mine, self.split, self.slot, self.far = n_chips, mine, split, 1, far
        self.near = self.swap(near)
        mid, self.near = tie(mid, self.near)
        self.mid = self.swap(mid)
        whole = (mine[0].astype(F32) + self.near[0].astype(F32)).astype(BF16)
        self.ahead, self.behind = whole[:split], whole[split:]

    def swap(self, x):
        return lax.ppermute(x, "dp", core_swap(2 * self.n))

    def arrived(self, *arrays):
        self.ahead, self.behind, self.mid, self.far, *rest = tie(
            self.ahead, self.behind, self.mid, self.far, *arrays)
        if self.slot == 1 and self.far is not None:
            self.far = self.swap(self.far)
        return rest

    def term(self, *moved):
        n = self.mid.shape[0]
        other = self.mid[self.slot - 1] if self.slot <= n else self.far[self.slot - 1 - n]
        total = self.mine[self.slot].astype(F32) + other.astype(F32)
        for m in moved:
            total = total + m.astype(F32)
        self.slot += 1
        return total.astype(BF16)

    def send(self):
        self.ahead, self.behind = tie(self.ahead, self.behind)
        self.ahead = lax.ppermute(self.ahead, "dp", chip_shift(self.n, 1))
        self.behind = lax.ppermute(self.behind, "dp", chip_shift(self.n, -1))

    def add(self):
        if self.slot == 1:
            ahead = jnp.pad(self.ahead, ((0, self.mine.shape[1] - self.split), (0, 0)))
            behind = jnp.pad(self.behind, ((self.split, 0), (0, 0)))
            self.ahead, self.behind = self.term(ahead), self.term(behind)
        elif self.slot < self.n - 1:
            self.ahead, self.behind = self.term(self.ahead), self.term(self.behind)
        else:
            self.total = self.term(self.ahead, self.behind)

    def tie(self, *arrays):
        out = tie(self.ahead, self.behind, *arrays)
        self.ahead, self.behind = out[:2]
        return out[2:]


def swap_rows(x):
    return lax.ppermute(x, "blk", [(0, 1), (1, 0)])


def pack_weights(qkv_w, proj_w, up_w, down_w, shares):
    r = qkv_w.shape[0] // shares
    qkv = qkv_w.reshape(shares, r, 3, 3, 2, 128).transpose(0, 3, 1, 4, 2, 5).reshape(shares, 3, r, 768)
    up = up_w.reshape(shares, r, 4, 768).transpose(0, 2, 1, 3)
    down = down_w.reshape(shares, 4, r, 768)
    proj = proj_w.reshape(shares, 1, r, 768)
    return qkv, jnp.concatenate([up, down, proj], axis=1)


def pack_small(gains, shifts, qv_b, out_b, up_b, at):
    flat = jnp.concatenate([gains, shifts, qv_b, out_b], axis=0)
    rows = lax.dynamic_update_slice(jnp.zeros((8, 768), flat.dtype), flat, (0, at))
    hidden = lax.dynamic_update_slice(jnp.zeros((3072,), flat.dtype), up_b, (4 * at,)).reshape(4, 768)
    return jnp.concatenate([rows, hidden, jnp.zeros((4, 768), flat.dtype)], axis=0)


def split_far(blocks, split):
    parts = []
    for t in range(BLOCKS):
        far = t % (BLOCKS // 2) == BLOCKS // 2 - 1
        parts += [blocks[t, :split], blocks[t, split:]] if far else [blocks[t]]
    return parts


def unpack_qkv(blocks, rows):
    return blocks.reshape(3, rows, 2, 3, 128).transpose(1, 3, 0, 2, 4).reshape(rows, 2304)


def unpack_up(blocks, rows):
    return blocks.reshape(4, rows, 768).transpose(1, 0, 2).reshape(rows, 3072)


def shards(tokens, segment_ids, padding_mask, qkv_weight, proj_weight, up_weight, down_weight,
           norm_gain, norm_shift, qv_bias, out_bias, up_bias, cotangent):
    n_dev = lax.axis_size("dp")
    dp, blk = lax.axis_index("dp"), lax.axis_index("blk")
    ring = n_dev == BLOCKS
    n_chips = BLOCKS // 2

    def pick(pair, which):
        return lax.dynamic_index_in_dim(pair, which, 0, keepdims=False)

    tok_own, tok_rx = pick(tokens, blk)[0], swap_rows(pick(tokens, 1 - blk)[0])
    cot_own, cot_send = pick(cotangent, blk)[0], pick(cotangent, 1 - blk)[0]
    seg, pad = pick(segment_ids, blk)[0], pick(padding_mask, blk)[0]
    lanes = jnp.arange(128, dtype=jnp.int32)[None, :]
    code = jnp.where(lanes < 32, seg[:, None] // 32 == lanes, seg[:, None] % 32 + 32 == lanes)
    seg_q = code.astype(BF16)
    allowed = code & (pad[:, None] == 1)
    seg_k = jnp.where(allowed | (lanes >= 64), 0.0, MASKED).astype(BF16)

    if ring:
        qkv_blocks, rest = pack_weights(qkv_weight, proj_weight, up_weight, down_weight, 1)
        small = pack_small(norm_gain, norm_shift, qv_bias, out_bias, up_bias, 48 * dp)
        first = RingGather(jnp.concatenate([qkv_blocks.reshape(144, 768), small], axis=0), 96, n_chips)
        rest = rest.reshape(432, 768)
        for _ in range(4):
            first.step()
            first.arrived()
        rest, _, _ = tie(rest, first.ahead[-1], first.behind[-1])
        parts = first.parts()
        second = RingGather(rest, 192, n_chips)
        order = jnp.asarray(ring_order(n_chips))[dp]
        core = lax.rem(dp, 2)
        chips = jnp.asarray(send_order(n_chips))[dp // 2]
        slots = jnp.asarray(np.argsort(send_order(n_chips), axis=1).astype(np.int32))[dp // 2]
    else:
        whole = [lax.all_gather(w, "dp", axis=0, tiled=True)
                 for w in (qkv_weight, proj_weight, up_weight, down_weight)]
        qkv_blocks, rest = pack_weights(*whole, BLOCKS)
        vectors = [lax.all_gather(w, "dp", axis=1, tiled=True)
                   for w in (norm_gain, norm_shift, qv_bias, out_bias)]
        hidden = lax.all_gather(up_bias, "dp", axis=0, tiled=True)
        small = pack_small(*vectors, hidden, 0)
        small = jnp.concatenate([small[None], jnp.zeros((BLOCKS - 1, 16, 768), BF16)], axis=0)
        parts = split_far(jnp.concatenate([qkv_blocks.reshape(BLOCKS, 144, 768), small], axis=1), 96)
        rest_parts = split_far(rest.reshape(BLOCKS, 432, 768), 192)
        order = jnp.arange(BLOCKS, dtype=jnp.int32)
        core = jnp.int32(0)
        chips = slots = jnp.arange(n_chips, dtype=jnp.int32)
    idx = jnp.concatenate([order, jnp.stack([blk, core]).astype(jnp.int32), chips, slots])
    if ring:
        second.step()
    outs = attn_forward(0, idx, parts, (tok_own, tok_rx), seg_q, seg_k)
    heads, nrm, small_all = [list(outs[:7])], outs[7], outs[8]
    for quad in (1, 2):
        if ring:
            nrm, small_all, heads[-1][3] = second.tie(nrm, small_all, heads[-1][3])
            second.step()
        if quad == 1:
            cot_send, nrm = tie(cot_send, nrm)
            cot_rx = swap_rows(cot_send)
        heads.append(list(attn_forward(quad, idx, parts, (nrm, small_all), seg_q, seg_k)))
    atts = [h[3] for h in heads]
    if ring:
        atts[2], small_all = second.tie(atts[2], small_all)
        second.step()
        atts[2], cot_rx = second.tie(atts[2], cot_rx)
        rest_parts = second.parts()
    lo_mine, lo_theirs, d_mid, d_att, *sends, sums = ffn(
        idx, rest_parts, atts, tok_own, tok_rx, cot_own, cot_rx, small_all)
    lo_rx = swap_rows(lo_theirs)

    groups = ((0,), (1, 2), (3, 4), (5,))
    heads = [[h[0], h[1], h[2], h[3], h[4], h[5], h[6]] for h in heads]
    if ring:
        ffn_sum = RingReduce(*sends, 224, n_chips)
        (d_att,) = ffn_sum.tie(d_att)
        ffn_sum.send()
    d_ni, b0, *q_sends = attn_backward(groups[0], idx, heads, d_att, nrm)
    biases = [b0]
    for group in groups[1:]:
        if ring:
            if group is groups[1]:
                (d_ni,) = ffn_sum.arrived(d_ni)
            else:
                d_ni, lo_rx = ffn_sum.arrived(d_ni, lo_rx)
            ffn_sum.add()
            (d_ni,) = ffn_sum.tie(d_ni)
            ffn_sum.send()
        if group is not groups[-1]:
            d_ni, b, *q_sends = attn_backward(group, idx, heads, d_att, nrm, d_ni, q_sends)
            biases.append(b)
    gt_mine, gt_first, gt_second, *q_sends = attn_backward(
        groups[-1], idx, heads, d_att, nrm, d_ni, q_sends,
        tail=(tok_own, tok_rx, d_mid, small_all, sums, *biases))

    def together(own_half, other_half):
        swapped = blk == 1
        return jnp.stack([jnp.where(swapped, other_half, own_half),
                          jnp.where(swapped, own_half, other_half)])[:, None]

    if ring:
        gt_first, gt_second, *q_sends = ffn_sum.arrived(gt_first, gt_second, *q_sends)
        qkv_sum = RingReduce(*q_sends, None, 80, n_chips)
        gt_first = swap_rows(gt_first)
        qkv_sum.send()
        ffn_sum.add()
        gt_second, ffn_sum.total = qkv_sum.arrived(gt_second, ffn_sum.total)
        gt_second = swap_rows(gt_second)
        qkv_sum.add()
        qkv_sum.send()
        gt_first, ffn_sum.total = qkv_sum.arrived(gt_first, ffn_sum.total)
        ffn_rx = swap_rows(ffn_sum.total)
        qkv_sum.add()
        qkv_sum.send()
        (gt_second,) = qkv_sum.arrived(gt_second)
        qkv_sum.add()
        qkv_sum.send()
        qkv_sum.add()
        gt_rx = jnp.concatenate([gt_first, gt_second])
        out, grad_tokens, ffn_rx, _ = tie(
            together(lo_mine, lo_rx), together(gt_mine, gt_rx), ffn_rx, qkv_sum.total)
        done_ffn = ffn_sum.total.astype(F32) + ffn_rx.astype(F32)
        done_qkv = qkv_sum.total.astype(F32) + swap_rows(qkv_sum.total).astype(F32)
        r = 48
        small = done_qkv[144:160]
        own = lax.dynamic_slice_in_dim(small[0:8], 48 * dp, 48, 1)
        g_bias = lax.dynamic_slice_in_dim(small[8:12].reshape(3072), 192 * dp, 192, 0)
        return (out, grad_tokens,
                unpack_qkv(done_qkv[0:144], r), done_ffn[384:432], unpack_up(done_ffn[0:192], r), done_ffn[192:384],
                own[0:2], own[2:4], own[4:6], own[6:8], g_bias)

    gt_rx = swap_rows(jnp.concatenate([gt_first, gt_second]))

    def whole_sum(mine, *others):
        return jnp.stack([mine, jnp.concatenate(others)], axis=1).reshape(BLOCKS, mine.shape[1], 768)

    def scatter(x, dim):
        part = lax.psum_scatter(x, "dp", scatter_dimension=dim, tiled=True)
        return lax.psum(part.astype(BF16), "blk").astype(F32)

    g_ffn, g_q = whole_sum(*sends), whole_sum(*q_sends)
    g_up = g_ffn[:, 0:192].reshape(BLOCKS, 4, 48, 768).transpose(0, 2, 1, 3).reshape(768, 3072)
    g_down = g_ffn[:, 192:384].reshape(3072, 768)
    g_proj = g_ffn[:, 384:432].reshape(768, 768)
    g_qkv = jnp.stack([g_q[:, 48 * j : 48 * j + 48].reshape(768, 768) for j in range(3)])
    g_small = g_q[0, 144:160].astype(F32)
    g_bias = g_small[8:12].reshape(-1)
    big = [scatter(g.astype(F32), 0) for g in (unpack_qkv(g_qkv, 768), g_proj, g_up, g_down)]
    return (together(lo_mine, lo_rx), together(gt_mine, gt_rx), *big,
            *[scatter(g_small[2 * i : 2 * i + 2], 1) for i in range(4)], scatter(g_bias, 0))


def solution(mesh):
    rows = P(None, "dp", "blk", None)
    return jax.shard_map(
        shards,
        mesh=mesh,
        in_specs=(rows, P(None, "dp", None), P(None, "dp", None)) + (P("dp", None),) * 4
        + (P(None, "dp"),) * 4 + (P("dp"), rows),
        out_specs=(rows, rows) + (P("dp", None),) * 4 + (P(None, "dp"),) * 4 + (P("dp"),),
        check_vma=False,
    )
```

```python
import functools

import jax
import jax.numpy as jnp
import numpy as np
from jax import lax
from jax.experimental import pallas as pl
from jax.experimental.pallas import tpu as pltpu
from jax.sharding import PartitionSpec as P

HD = 64
BLOCKS = 16
N_PARTS = BLOCKS + 2
NT = (((1,), (1,)), ((), ()))
TN = (((0,), (0,)), ((), ()))
F32 = jnp.float32
BF16 = jnp.bfloat16
ANY = pl.BlockSpec(memory_space=pl.ANY)
SMEM = pl.BlockSpec(memory_space=pltpu.SMEM)
VMEM_LIMIT = 60 << 20
MASKED = -1e30


def dot(a, b, dims=(((1,), (0,)), ((), ()))):
    return lax.dot_general(a, b, dims, preferred_element_type=F32)


def cost(us):
    return pl.CostEstimate(flops=int(us * 1.1e9), bytes_accessed=1 << 20, transcendentals=0)


def full(shape):
    return pl.BlockSpec(shape, lambda *_: (0,) * len(shape))


def params():
    return pltpu.CompilerParams(vmem_limit_bytes=VMEM_LIMIT)


def norm_stats(x):
    mean = jnp.mean(x, axis=1, keepdims=True)
    center = x - mean
    rstd = lax.rsqrt(jnp.mean(center * center, axis=1, keepdims=True) + 1e-05)
    return center * rstd, rstd


def norm_back(e, nhat, rstd):
    return (
        e - jnp.mean(e, axis=1, keepdims=True) - nhat * jnp.mean(e * nhat, axis=1, keepdims=True)
    ) * rstd


def row_sum(x):
    return jnp.sum(x, axis=0, keepdims=True)


def send_copies(idx, buf, rows, sends, sem, lanes=slice(None)):
    core = idx[17]
    copies = []
    mine, *others = sends
    slots = [other.at[i] for other in others for i in range(other.shape[0])]
    for slot, theirs in enumerate(slots):
        chip = idx[18 + slot]
        copies.append(pltpu.make_async_copy(buf.at[chip, core], mine.at[slot, rows, lanes], sem.at[0, slot]))
        copies.append(pltpu.make_async_copy(buf.at[chip, 1 - core], theirs.at[rows, lanes], sem.at[1, slot]))
    return copies


def part_copies(parts, split, start, size, place, sem, piece=None):
    copies = []
    n = BLOCKS // 2
    for t in range(BLOCKS):
        group = parts[(n + 1) * (t // n) : (n + 1) * (t // n + 1)]
        if t % n < n - 1:
            src, at = group[t % n], start
        elif piece == 0 or (piece is None and start < split):
            src, at = group[n - 1], start
        else:
            src, at = group[n], start - split
        copies.append(pltpu.make_async_copy(src.at[pl.ds(at, size), :], place(t), sem(t)))
    return copies


def send_shapes(rows, cuts):
    return [jax.ShapeDtypeStruct((n, rows, 768), BF16) for n in (BLOCKS // 2, *cuts)]


def attn_forward_body(quad, block, idx, *refs):
    first = quad == 0
    parts, refs = refs[:N_PARTS], refs[N_PARTS:]
    if first:
        (tok_own, tok_rx, sq, sk, q_o, k_o, v_o, att_o, li_o, e_o, w_o, nrm_o, small_o,
         w_s, s_s, kk, vv, aa, sem) = refs
    else:
        (nrm_i, small_i, sq, sk, q_o, k_o, v_o, att_o, li_o, e_o, w_o,
         w_s, kk, vv, aa, sem) = refs
    seq = sq.shape[0]
    half = seq // 2
    pair = pl.program_id(0)

    @pl.when(pair == 0)
    def _():
        copies = part_copies(parts, 96, 48 * quad, 48, lambda t: w_s.at[idx[t]], lambda t: sem.at[0, t])
        if first:
            copies += part_copies(parts, 96, 144, 16, lambda t: s_s.at[t], lambda t: sem.at[1, t])
        for c in copies:
            c.start()
        for c in copies:
            c.wait()
        weight = w_s[...].reshape(768, 768)
        w_o[0], w_o[1] = weight[:, :384], weight[:, 384:]
        if first:
            small = jnp.zeros((16, 768), F32)
            for t in range(BLOCKS):
                small = small + s_s[t].astype(F32)
            small_o[...] = small
            gain, shift = small[0:1], small[2:3]
            for src, where in ((tok_own, idx[16]), (tok_rx, 1 - idx[16])):
                base = pl.multiple_of(where * half, half)
                for i in range(0, half, block):
                    nhat, _rstd = norm_stats(src[i : i + block, :].astype(F32))
                    nrm_o[pl.ds(base + i, block), :] = (nhat * gain + shift).astype(BF16)
            nrm = nrm_o
            bq, bv = small[4:5, 0:256], small[5:6, 0:256]
        else:
            nrm = nrm_i
            cols = slice(256 * quad, 256 * quad + 256)
            bq, bv = small_i[4:5, cols], small_i[5:6, cols]
        for i in range(0, seq, block):
            rows = slice(i, i + block)
            joined = dot(nrm[rows, :], weight)
            for p in range(2):
                c, to = 384 * p, slice(128 * p, 128 * p + 128)
                q_o[p, rows, :] = (joined[:, c : c + 128] + bq[:, to]).astype(BF16)
                k_o[p, rows, :] = joined[:, c + 128 : c + 256].astype(BF16)
                v_o[p, rows, :] = (joined[:, c + 256 : c + 384] + bv[:, to]).astype(BF16)

    head = lax.broadcasted_iota(jnp.int32, (seq, 128), 1) // HD
    k_pair, v_pair = k_o[pair], v_o[pair]
    zero, one = jnp.zeros((seq, 128), BF16), jnp.ones((seq, 128), BF16)
    for h in range(2):
        mine = head == h
        kk[h, :, 0:128] = jnp.where(mine, k_pair, zero)
        kk[h, :, 128:256] = sk[...]
        vv[h, :, 0:128] = jnp.where(mine, v_pair, zero)
        vv[h, :, 128:256] = jnp.where(mine, one, zero)
    aa[:, 0:128] = q_o[pair] * BF16(0.125)
    aa[:, 128:256] = sq[...]
    for i in range(0, seq, block):
        rows = slice(i, i + block)
        acc = None
        for h in range(2):
            s = dot(aa[rows, :], kk[h], NT)
            e = jnp.exp(s - jnp.max(s, axis=1, keepdims=True)).astype(BF16)
            e_o[h, rows, :] = e
            o = dot(e, vv[h])
            acc = o if acc is None else acc + o
        inverse = 1.0 / acc[:, 128:256]
        li_o[0, rows, :] = inverse
        att_o[0, rows, :] = (acc[:, 0:128] * inverse).astype(BF16)


def attn_forward(quad, idx, parts, rows_in, sq, sk):
    seq = sq.shape[0]
    sds = jax.ShapeDtypeStruct
    first = quad == 0
    pair_block = pl.BlockSpec((1, seq, 128), lambda p: (p, 0, 0))
    quad_block = full((2, seq, 128))
    out_shape = [
        sds((2, seq, 128), BF16),
        sds((2, seq, 128), BF16),
        sds((2, seq, 128), BF16),
        sds((2, seq, 128), BF16),
        sds((2, seq, 128), F32),
        sds((4, seq, seq), BF16),
        sds((2, 768, 384), BF16),
    ]
    out_specs = [
        quad_block, quad_block, quad_block, pair_block, pair_block,
        pl.BlockSpec((2, seq, seq), lambda p: (p, 0, 0)), full((2, 768, 384)),
    ]
    scratch = [pltpu.VMEM((BLOCKS, 48, 768), BF16)]
    if first:
        out_shape += [sds((seq, 768), BF16), sds((16, 768), F32)]
        out_specs += [full((seq, 768)), full((16, 768))]
        scratch += [pltpu.VMEM((BLOCKS, 16, 768), BF16)]
    scratch += [
        pltpu.VMEM((2, seq, 256), BF16),
        pltpu.VMEM((2, seq, 256), BF16),
        pltpu.VMEM((seq, 256), BF16),
        pltpu.SemaphoreType.DMA((2, BLOCKS)),
    ]
    return pl.pallas_call(
        functools.partial(attn_forward_body, quad, 256),
        grid=(2,),
        in_specs=[SMEM] + [ANY] * N_PARTS
        + [full(r.shape) for r in rows_in]
        + [full(sq.shape), full(sk.shape)],
        out_specs=out_specs,
        out_shape=out_shape,
        scratch_shapes=scratch,
        compiler_params=params(),
        cost_estimate=cost(11),
    )(idx, *parts, *rows_in, sq, sk)


def ffn_body(
    block, idx, *refs
):
    parts, refs = refs[:N_PARTS], refs[N_PARTS:]
    ffn_steps(block, idx, parts, *refs)


def ffn_steps(
    block, idx, parts, att0, att1, att2, tok_own, tok_rx, cot_own, cot_rx, small,
    lo_mine, lo_theirs, dmid_o, datt_o, g_mine, g_near, g_mid, g_far, sums_o,
    up_s, dn_s, proj_s, att_s, mid_s, nm_s, nmt_s, cot_s, act_s, dp_s, oacc, dacc, dbr_s, gup_s, gdn_s, gproj,
    lo_s, datt_s, wsem, dsem, psem, gsem, gdsem, gpsem, osem,
):
    c = pl.program_id(0)
    n_c = pl.num_programs(0)
    slot = lax.rem(c, 2)
    seq = mid_s.shape[0]
    half = seq // 2
    core = idx[17]

    def up_copies(chunk, s):
        rows = pl.multiple_of(chunk * 48, 48)
        return part_copies(parts, 0, rows, 48, lambda t: up_s.at[s, idx[t]], lambda t: wsem.at[s, t], piece=0)

    def down_copies():
        return part_copies(parts, 192, 192, 192, lambda t: dn_s.at[idx[t]], lambda t: dsem.at[idx[t]])

    def grad_copies(chunk, s, act):
        rows = pl.ds(pl.multiple_of(chunk * 48, 48), 48)
        for copy in send_copies(idx, gup_s.at[s], rows, (g_mine, g_near, g_mid, g_far), gsem.at[s]):
            act(copy)
        rows = pl.ds(192, 192)
        for j in range(2):
            slot_to = idx[26 + 2 * chunk + j]
            act(pltpu.make_async_copy(gdn_s.at[s, j, core], g_mine.at[slot_to, rows, :], gdsem.at[s, 0, j]))

            @pl.when(slot_to == 0)
            def _():
                act(pltpu.make_async_copy(gdn_s.at[s, j, 1 - core], g_near.at[0, rows, :], gdsem.at[s, 1, j]))

            @pl.when((slot_to > 0) & (slot_to < 3))
            def _():
                act(pltpu.make_async_copy(gdn_s.at[s, j, 1 - core], g_mid.at[slot_to - 1, rows, :], gdsem.at[s, 1, j]))

            @pl.when(slot_to >= 3)
            def _():
                act(pltpu.make_async_copy(gdn_s.at[s, j, 1 - core], g_far.at[slot_to - 3, rows, :], gdsem.at[s, 1, j]))

    def start(copy):
        copy.start()

    def wait(copy):
        copy.wait()

    @pl.when(c == 0)
    def _():
        proj_copies = part_copies(parts, 192, 384, 48, lambda t: proj_s.at[idx[t]], lambda t: psem.at[t])
        for copy in proj_copies + up_copies(c, 0) + down_copies():
            copy.start()
        for src, where in ((tok_own, idx[16]), (tok_rx, 1 - idx[16])):
            base = pl.multiple_of(where * half, half)
            mid_s[pl.ds(base, half), :] = src[...].astype(F32)
        for src, where in ((cot_own, idx[16]), (cot_rx, 1 - idx[16])):
            base = pl.multiple_of(where * half, half)
            cot_s[pl.ds(base, half), :] = src[...]
        for j, a in enumerate((att0, att1, att2)):
            for p in range(2):
                att_s[:, 256 * j + 128 * p : 256 * j + 128 * p + 128] = a[p]
        for copy in proj_copies:
            copy.wait()
        proj = proj_s[...].reshape(768, 768)
        for i in range(0, seq, block):
            rows = slice(i, i + block)
            mid = mid_s[rows, :] + (dot(att_s[rows, :], proj) + small[6:7])
            mid_s[rows, :] = mid
            oacc[rows, :] = mid + small[7:8]
            dacc[rows, :] = jnp.zeros((block, 768), F32)
            nhat, _rstd = norm_stats(mid)
            nm_s[rows, :] = (nhat * small[1:2] + small[3:4]).astype(BF16)
        nmt_s[...] = nm_s[...].T

    for copy in up_copies(c, slot):
        copy.wait()
    for j in range(4):
        owner = 4 * c + j
        pltpu.make_async_copy(parts[0].at[pl.ds(192, 192), :], dn_s.at[owner], dsem.at[owner]).wait()

    @pl.when(c + 1 < n_c)
    def _():
        for copy in up_copies(c + 1, 1 - slot):
            copy.start()

    up = up_s[slot].reshape(768, 768)
    dn = dn_s[pl.ds(4 * c, 4)].reshape(768, 768)
    bias = small[pl.ds(8 + c, 1), :]
    bias_sum = None
    for i in range(0, seq, block):
        rows = slice(i, i + block)
        pre = dot(nm_s[rows, :], up) + bias
        cdf = 0.5 * (1.0 + lax.erf(pre * 0.7071067811865476))
        act = (pre * cdf).astype(BF16)
        act_s[rows, :] = act
        oacc[rows, :] += dot(act, dn)
        slope = cdf + pre * (jnp.exp(pre * pre * -0.5) * 0.3989422804014327)
        d_pre = (dot(cot_s[rows, :], dn, NT) * slope).astype(BF16)
        dp_s[rows, :] = d_pre
        part = row_sum(d_pre.astype(F32))
        bias_sum = part if bias_sum is None else bias_sum + part
        dacc[rows, :] += dot(d_pre, up, NT)
    sums_o[pl.ds(8 + c, 1), :] = bias_sum

    @pl.when(c >= 2)
    def _():
        grad_copies(c - 2, slot, wait)

    gup_s[slot] = dot(nmt_s[...], dp_s[...]).astype(BF16).reshape(BLOCKS // 2, 2, 48, 768)
    gdn_s[slot] = dot(act_s[...], cot_s[...], TN).astype(BF16).reshape(2, 2, 192, 768)
    grad_copies(c, slot, start)

    @pl.when(c == n_c - 1)
    def _():
        proj = proj_s[...].reshape(768, 768)
        gain_sum = shift_sum = bout_sum = bdown_sum = None
        out_copies = []

        def send_out(src, dst, n):
            out_copies.append(pltpu.make_async_copy(src, dst, osem.at[n]))
            out_copies[-1].start()

        lo_s[...] = oacc[...].astype(BF16)
        for n, (dst, where) in enumerate(((lo_mine, idx[16]), (lo_theirs, 1 - idx[16]))):
            send_out(lo_s.at[pl.ds(pl.multiple_of(where * half, half), half), :], dst, n)
        for i in range(0, seq, block):
            rows = slice(i, i + block)
            mid = mid_s[rows, :]
            cot = cot_s[rows, :].astype(F32)
            d_nm = dacc[rows, :]
            nhat, rstd = norm_stats(mid)
            d_mid = cot + norm_back(d_nm * small[1:2], nhat, rstd)
            mid_s[rows, :] = d_mid
            send_out(mid_s.at[pl.ds(i, block), :], dmid_o.at[pl.ds(i, block), :], 2 + i // block)
            d_branch = d_mid.astype(BF16)
            dbr_s[rows, :] = d_branch
            d_att = dot(d_branch, proj, NT).astype(BF16)
            for p in range(6):
                datt_s[p, rows, :] = d_att[:, 128 * p : 128 * p + 128]
            send_out(datt_s.at[:, pl.ds(i, block), :], datt_o.at[:, pl.ds(i, block), :], 2 + (seq + i) // block)
            parts = [row_sum(d_nm * nhat), row_sum(d_nm), row_sum(d_branch.astype(F32)), row_sum(cot)]
            if gain_sum is None:
                gain_sum, shift_sum, bout_sum, bdown_sum = parts
            else:
                gain_sum, shift_sum = gain_sum + parts[0], shift_sum + parts[1]
                bout_sum, bdown_sum = bout_sum + parts[2], bdown_sum + parts[3]
        sums_o[0:8, :] = jnp.concatenate(
            [jnp.zeros_like(gain_sum), gain_sum, jnp.zeros_like(gain_sum), shift_sum,
             jnp.zeros_like(gain_sum), jnp.zeros_like(gain_sum), bout_sum, bdown_sum], axis=0)
        sums_o[12:16, :] = jnp.zeros((4, 768), F32)
        gproj[...] = dot(att_s[...], dbr_s[...], TN).astype(BF16).reshape(BLOCKS // 2, 2, 48, 768)
        last = send_copies(idx, gproj, pl.ds(384, 48), (g_mine, g_near, g_mid, g_far), gpsem)
        for copy in last:
            copy.start()
        grad_copies(c - 1, 1 - slot, wait)
        grad_copies(c, slot, wait)
        for copy in out_copies + last:
            copy.wait()


def ffn(idx, parts, atts, tok_own, tok_rx, cot_own, cot_rx, small):
    seq = 2 * tok_own.shape[0]
    sds = jax.ShapeDtypeStruct
    v = pltpu.VMEM
    half = tok_own.shape
    rows, frows = v((seq, 768), BF16), v((seq, 768), F32)
    return pl.pallas_call(
        functools.partial(ffn_body, 256),
        grid=(4,),
        in_specs=[SMEM] + [ANY] * N_PARTS + [full((2, seq, 128))] * 3 + [full(half)] * 4 + [full((16, 768))],
        out_specs=[ANY] * 8 + [full((16, 768))],
        out_shape=[
            sds(half, BF16), sds(half, BF16), sds((seq, 768), F32), sds((6, seq, 128), BF16),
            *send_shapes(432, (1, 2, 5)), sds((16, 768), F32),
        ],
        scratch_shapes=[
            v((2, BLOCKS, 48, 768), BF16), v((BLOCKS, 192, 768), BF16), v((BLOCKS, 48, 768), BF16),
            rows, frows, rows, v((768, seq), BF16), rows, rows, rows, frows, frows, rows,
            v((2, BLOCKS // 2, 2, 48, 768), BF16), v((2, 2, 2, 192, 768), BF16), v((BLOCKS // 2, 2, 48, 768), BF16),
            rows, v((6, seq, 128), BF16), pltpu.SemaphoreType.DMA((2, BLOCKS)), pltpu.SemaphoreType.DMA((BLOCKS,)), pltpu.SemaphoreType.DMA((BLOCKS,)),
            pltpu.SemaphoreType.DMA((2, 2, BLOCKS // 2)), pltpu.SemaphoreType.DMA((2, 2, 2)),
            pltpu.SemaphoreType.DMA((2, BLOCKS // 2)), pltpu.SemaphoreType.DMA((2 + 2 * seq // 256,)),
        ],
        compiler_params=params(),
        cost_estimate=cost(50),
    )(idx, *parts, *atts, tok_own, tok_rx, cot_own, cot_rx, small)


def attn_backward_body(pairs, block, idx, *refs):
    n = len(pairs)
    start_pair, last = pairs[0] == 0, pairs[-1] == 5
    heads, refs = [refs[7 * j : 7 * j + 7] for j in range(n)], refs[7 * n :]
    (do_h, nrm_h), refs = refs[:2], refs[2:]
    if not start_pair:
        dni_h, refs = refs[0], refs[4:]
    if last:
        (tok_own, tok_rx, dmid_h, small, sums_i, *b_in), refs = refs[:8], refs[8:]
        (gt_mine, gt_first, gt_second, *sends), refs = refs[:6], refs[6:]
    else:
        (dni_o, b_o, *sends), refs = refs[:5], refs[5:]
    (q_s, k_s, v_s, o_s, do_s, li_s, e_s, w_s, nrm_s, dni_s, vv, kk, dd, qm, dm, dkt, dvt, dj, gbuf,
     isem, esem, wsem, gsem), refs = refs[:23], refs[23:]
    seq = q_s.shape[1]
    half = seq // 2
    n_block = seq // block
    copy = pltpu.make_async_copy
    lane = lax.broadcasted_iota(jnp.int32, (seq, 128), 1)
    side = lax.broadcasted_iota(jnp.int32, (128, seq), 0)

    heads_in, e_in, late = [], [], []
    for j, (q_h, k_h, v_h, o_h, li_h, e_h, w_h) in enumerate(heads):
        odd = pairs[j] % 2
        heads_in.append([
            copy(src.at[at], dst.at[j], isem.at[j, m])
            for m, (src, dst, at) in enumerate((
                (v_h, v_s, odd), (do_h, do_s, pairs[j]), (li_h, li_s, odd), (o_h, o_s, odd),
                (k_h, k_s, odd), (q_h, q_s, odd)))
        ])
        e_in.append([
            copy(e_h.at[pl.ds(2 * odd, 2), pl.ds(i * block, block), :],
                 e_s.at[pl.ds(2 * j, 2), pl.ds(i * block, block), :], esem.at[j, i])
            for i in range(n_block)
        ])
        late.append(copy(w_h.at[odd], w_s.at[:, pl.ds(384 * j, 384)], wsem.at[j]))
    late.append(copy(nrm_h, nrm_s, wsem.at[2]))
    if not start_pair:
        late.append(copy(dni_h, dni_s, wsem.at[3]))
    if last:
        dmid_s, sbuf, tok_s, gt_s = refs
        late.append(copy(dmid_h, dmid_s, wsem.at[4]))
        late.append(copy(tok_rx, tok_s.at[0], wsem.at[5]))
        late.append(copy(tok_own, tok_s.at[1], wsem.at[6]))
    for c in heads_in[0] + e_in[0][:2]:
        c.start()
    queue = e_in[0][2:]
    for j in range(1, n):
        queue = queue + heads_in[j] + e_in[j]
    queue = queue + late
    per_block = -(-len(queue) // n_block)

    for pair in range(n):
        for c in heads_in[pair]:
            c.wait()
        d_out = do_s[pair].astype(F32) * li_s[pair]
        d_low = d_out.astype(BF16)
        prod = d_out * o_s[pair].astype(F32)
        extra = jnp.zeros((seq, 128), F32)
        q_t, d_t = q_s[pair].T, d_low.T
        zero = jnp.zeros((seq, 128), BF16)
        zero_t = jnp.zeros((128, seq), BF16)
        for h in range(2):
            mine = (lane // HD) == h
            delta = jnp.sum(jnp.where(mine, prod, 0.0), axis=1, keepdims=True)
            high = delta.astype(BF16).astype(F32)
            extra = jnp.where(lane == 2 * h, -high, extra)
            extra = jnp.where(lane == 2 * h + 1, high - delta, extra)
            vv[h, :, 0:128] = jnp.where(mine, v_s[pair], zero)
            vv[h, :, 128:256] = jnp.where((lane // 2) == h, 1.0, 0.0).astype(BF16)
            kk[h] = jnp.where(mine, k_s[pair], zero)
            mine_t = (side // HD) == h
            qm[h] = jnp.where(mine_t, q_t, zero_t)
            dm[h] = jnp.where(mine_t, d_t, zero_t)
        dd[:, 0:128] = d_low
        dd[:, 128:256] = extra.astype(BF16)
        base = 384 * pair
        for i in range(n_block):
            e_in[pair][i].wait()
            for c in queue[:per_block]:
                c.start()
            queue = queue[per_block:]
            rows = slice(i * block, i * block + block)
            dq = None
            for h in range(2):
                dp = dot(dd[rows, :], vv[h], NT)
                e = e_s[2 * pair + h, rows, :]
                ds = dp.astype(BF16) * e
                t = dot(ds, kk[h])
                dq = t if dq is None else dq + t
                a, b = dot(qm[h, :, rows], ds), dot(dm[h, :, rows], e)
                if i == 0 and h == 0:
                    dkt[...], dvt[...] = a, b
                else:
                    dkt[...] += a
                    dvt[...] += b
            dj[rows, base : base + 128] = (dq * 0.125).astype(BF16)
        dj[:, base + 128 : base + 256] = (dkt[...] * 0.125).astype(BF16).T
        dj[:, base + 256 : base + 384] = dvt[...].astype(BF16).T

    for c in late:
        c.wait()
    grads = dot(nrm_s[...], dj[...], TN).astype(BF16)
    copies, bq, bv = [], [], []
    for j, p in enumerate(pairs):
        c = 384 * j
        gbuf[j] = grads[:, c : c + 384].reshape(BLOCKS // 2, 2, 48, 384)
        copies += send_copies(idx, gbuf.at[j], pl.ds(48 * (p // 2), 48), sends, gsem.at[j],
                              pl.ds(384 * (p % 2), 384))
        bq.append(row_sum(dj[:, c : c + 128].astype(F32)))
        bv.append(row_sum(dj[:, c + 256 : c + 384].astype(F32)))
    for c in copies:
        c.start()
    weight = w_s[...]
    if not last:
        both = jnp.concatenate(
            [jnp.concatenate(bq, axis=1), jnp.concatenate(bv, axis=1), jnp.zeros((6, 128 * n), F32)], axis=0)
        b_o[...] = both
        for i in range(n_block):
            rows = slice(i * block, i * block + block)
            d_ni = dot(dj[rows, :], weight, NT)
            dni_s[rows, :] = d_ni if start_pair else dni_s[rows, :] + d_ni
            out = copy(dni_s.at[pl.ds(i * block, block), :], dni_o.at[pl.ds(i * block, block), :], esem.at[0, i])
            out.start()
            copies.append(out)
    else:
        gain = small[0:1]
        gain_sum = shift_sum = None
        for m, dsts, where in ((0, (gt_first, gt_second), 1 - idx[16]), (1, (gt_mine,), idx[16])):
            start = pl.multiple_of(where * half, half)
            for i in range(0, half, block):
                rows = pl.ds(start + i, block)
                d_ni = dni_s[rows, :] + dot(dj[rows, :], weight, NT)
                nhat, rstd = norm_stats(tok_s[m, i : i + block, :].astype(F32))
                grad = dmid_s[rows, :] + norm_back(d_ni * gain, nhat, rstd)
                dst = dsts[i * len(dsts) // half]
                at = i % dst.shape[0]
                gt_s[m, i : i + block, :] = grad.astype(BF16)
                out = copy(gt_s.at[m, pl.ds(i, block), :], dst.at[pl.ds(at, block), :],
                           esem.at[0, (m * half + i) // block])
                out.start()
                copies.append(out)
                parts = [row_sum(d_ni * nhat), row_sum(d_ni)]
                if gain_sum is None:
                    gain_sum, shift_sum = parts
                else:
                    gain_sum, shift_sum = gain_sum + parts[0], shift_sum + parts[1]
        sums = sums_i[...]
        row = lax.broadcasted_iota(jnp.int32, (16, 768), 0)
        sums = jnp.where(row == 0, gain_sum, sums)
        sums = jnp.where(row == 2, shift_sum, sums)
        sums = jnp.where(row == 4, jnp.concatenate([b[0:1, :] for b in b_in] + bq, axis=1), sums)
        sums = jnp.where(row == 5, jnp.concatenate([b[1:2, :] for b in b_in] + bv, axis=1), sums)
        low = sums.astype(BF16)
        for t in range(BLOCKS // 2):
            sbuf[t, 0], sbuf[t, 1] = low, low
        more = send_copies(idx, sbuf, pl.ds(144, 16), sends, gsem.at[1])
        for c in more:
            c.start()
        copies += more
    for c in copies:
        c.wait()


def attn_backward(pairs, idx, heads, d_att, nrm, d_ni=None, grads=None, tail=None):
    n, first, last = len(pairs), pairs[0] == 0, tail is not None
    seq = nrm.shape[0]
    half = (seq // 2, 768)
    block = 256
    sds = jax.ShapeDtypeStruct
    vm = pltpu.VMEM
    whole = pl.BlockSpec(memory_space=pltpu.VMEM)
    args = [idx]
    for p in pairs:
        args += heads[p // 2]
    args += [d_att, nrm]
    in_specs = [SMEM] + [ANY] * (len(args) - 1)
    alias = {}
    if not first:
        args.append(d_ni)
        in_specs.append(ANY)
        if not last:
            alias[len(args) - 1] = 0
        for j, g in enumerate(grads):
            args.append(g)
            in_specs.append(ANY)
            alias[len(args) - 1] = 2 + j + last
    if last:
        args += list(tail)
        in_specs += [ANY, ANY, ANY] + [whole] * (len(tail) - 3)
        quarter = sds((seq // 4, 768), BF16)
        out_shape = [sds(half, BF16), quarter, quarter]
        out_specs = [ANY, ANY, ANY]
    else:
        out_shape = [sds((seq, 768), F32), sds((8, 128 * n), F32)]
        out_specs = [ANY, whole]
    out_shape += send_shapes(160, (1, 7))
    out_specs += [ANY] * 3
    pair = vm((n, seq, 128), BF16)
    dma = pltpu.SemaphoreType.DMA
    scratch = [
        pair, pair, pair, pair, pair, vm((n, seq, 128), F32), vm((2 * n, seq, seq), BF16), vm((768, 384 * n), BF16),
        vm((seq, 768), BF16), vm((seq, 768), F32),
        vm((2, seq, 256), BF16), vm((2, seq, 128), BF16), vm((seq, 256), BF16), vm((2, 128, seq), BF16),
        vm((2, 128, seq), BF16), vm((128, seq), F32), vm((128, seq), F32), vm((seq, 384 * n), BF16),
        vm((n, BLOCKS // 2, 2, 48, 384), BF16), dma((n, 6)), dma((n, seq // block)), dma((7,)),
        dma((2, 2, BLOCKS // 2)),
    ]
    if last:
        scratch += [vm((seq, 768), F32), vm((BLOCKS // 2, 2, 16, 768), BF16), vm((2, seq // 2, 768), BF16),
                    vm((2, seq // 2, 768), BF16)]
    return pl.pallas_call(
        functools.partial(attn_backward_body, pairs, block),
        in_specs=in_specs,
        out_specs=out_specs,
        out_shape=out_shape,
        scratch_shapes=scratch,
        input_output_aliases=alias,
        compiler_params=params(),
        cost_estimate=cost(8 * n),
    )(*args)


def chip_cycle(n_chips):
    rows = n_chips // 2
    return [2 * i for i in range(rows)] + [2 * i + 1 for i in reversed(range(rows))]


def chip_shift(n_chips, step):
    order = chip_cycle(n_chips)
    return [
        (2 * order[i] + core, 2 * order[(i + step) % n_chips] + core)
        for i in range(n_chips)
        for core in (0, 1)
    ]


def core_swap(n_dev):
    return [(i, i ^ 1) for i in range(n_dev)]


def tie(*arrays):
    return lax.optimization_barrier(arrays)


class RingGather:
    def __init__(self, x, split, n_chips):
        self.n, self.split, self.ahead, self.behind = n_chips, split, [x], [x]
        self.other = [self.swap(x)]
        self.waiting = []

    def swap(self, x):
        return lax.ppermute(x, "dp", core_swap(2 * self.n))

    def step(self):
        a, b = self.ahead[-1], self.behind[-1]
        if len(self.ahead) == self.n // 2:
            a, b = a[: self.split], b[self.split :]
        self.ahead.append(lax.ppermute(a, "dp", chip_shift(self.n, 1)))
        self.behind.append(lax.ppermute(b, "dp", chip_shift(self.n, -1)))

    def tie(self, *arrays):
        a, b, *rest = tie(self.ahead[-1], self.behind[-1], *self.other[-2:], *arrays)
        self.ahead[-1], self.behind[-1] = a, b
        n = len(self.other[-2:])
        self.other[-n:], rest = rest[:n], rest[n:]
        self.other += [self.swap(a), self.swap(b)]
        return rest

    def arrived(self):
        self.other += [self.swap(self.ahead[-1]), self.swap(self.behind[-1])]

    def parts(self):
        def in_order(ahead, behind):
            return [ahead[0]] + ahead[1:-1] + behind[1:-1] + [ahead[-1], behind[-1]]

        o = self.other
        return in_order(self.ahead, self.behind) + in_order(o[:1] + o[1::2], o[:1] + o[2::2])


def ring_order(n_chips):
    order = chip_cycle(n_chips)
    table = np.zeros((2 * n_chips, 2 * n_chips), np.int32)
    far = n_chips // 2
    steps = list(range(0, -far, -1)) + list(range(1, far)) + [far]
    for chip in range(n_chips):
        pos = order.index(chip)
        chips = [order[(pos + s) % n_chips] for s in steps]
        for core in (0, 1):
            table[2 * chip + core] = [2 * q + core for q in chips] + [2 * q + 1 - core for q in chips]
    return table


def send_order(n_chips):
    order = chip_cycle(n_chips)
    steps = [n_chips // 2]
    for t in range(n_chips // 2 - 1, 0, -1):
        steps += [t, -t]
    steps.append(0)
    table = np.zeros((n_chips, n_chips), np.int32)
    for chip in range(n_chips):
        table[chip] = [order[(order.index(chip) + s) % n_chips] for s in steps]
    return table


class RingReduce:
    def __init__(self, mine, near, mid, far, split, n_chips):
        self.n, self.mine, self.split, self.slot, self.far = n_chips, mine, split, 1, far
        self.near = self.swap(near)
        mid, self.near = tie(mid, self.near)
        self.mid = self.swap(mid)
        whole = (mine[0].astype(F32) + self.near[0].astype(F32)).astype(BF16)
        self.ahead, self.behind = whole[:split], whole[split:]

    def swap(self, x):
        return lax.ppermute(x, "dp", core_swap(2 * self.n))

    def arrived(self, *arrays):
        self.ahead, self.behind, self.mid, self.far, *rest = tie(
            self.ahead, self.behind, self.mid, self.far, *arrays)
        if self.slot == 1 and self.far is not None:
            self.far = self.swap(self.far)
        return rest

    def term(self, *moved):
        n = self.mid.shape[0]
        other = self.mid[self.slot - 1] if self.slot <= n else self.far[self.slot - 1 - n]
        total = self.mine[self.slot].astype(F32) + other.astype(F32)
        for m in moved:
            total = total + m.astype(F32)
        self.slot += 1
        return total.astype(BF16)

    def send(self):
        self.ahead, self.behind = tie(self.ahead, self.behind)
        self.ahead = lax.ppermute(self.ahead, "dp", chip_shift(self.n, 1))
        self.behind = lax.ppermute(self.behind, "dp", chip_shift(self.n, -1))

    def add(self):
        if self.slot == 1:
            ahead = jnp.pad(self.ahead, ((0, self.mine.shape[1] - self.split), (0, 0)))
            behind = jnp.pad(self.behind, ((self.split, 0), (0, 0)))
            self.ahead, self.behind = self.term(ahead), self.term(behind)
        elif self.slot < self.n - 1:
            self.ahead, self.behind = self.term(self.ahead), self.term(self.behind)
        else:
            self.total = self.term(self.ahead, self.behind)

    def tie(self, *arrays):
        out = tie(self.ahead, self.behind, *arrays)
        self.ahead, self.behind = out[:2]
        return out[2:]


def swap_rows(x):
    return lax.ppermute(x, "blk", [(0, 1), (1, 0)])


def pack_weights(qkv_w, proj_w, up_w, down_w, shares):
    r = qkv_w.shape[0] // shares
    qkv = qkv_w.reshape(shares, r, 3, 3, 2, 128).transpose(0, 3, 1, 4, 2, 5).reshape(shares, 3, r, 768)
    up = up_w.reshape(shares, r, 4, 768).transpose(0, 2, 1, 3)
    down = down_w.reshape(shares, 4, r, 768)
    proj = proj_w.reshape(shares, 1, r, 768)
    return qkv, jnp.concatenate([up, down, proj], axis=1)


def pack_small(gains, shifts, qv_b, out_b, up_b, at):
    flat = jnp.concatenate([gains, shifts, qv_b, out_b], axis=0)
    rows = lax.dynamic_update_slice(jnp.zeros((8, 768), flat.dtype), flat, (0, at))
    hidden = lax.dynamic_update_slice(jnp.zeros((3072,), flat.dtype), up_b, (4 * at,)).reshape(4, 768)
    return jnp.concatenate([rows, hidden, jnp.zeros((4, 768), flat.dtype)], axis=0)


def split_far(blocks, split):
    parts = []
    for t in range(BLOCKS):
        far = t % (BLOCKS // 2) == BLOCKS // 2 - 1
        parts += [blocks[t, :split], blocks[t, split:]] if far else [blocks[t]]
    return parts


def unpack_qkv(blocks, rows):
    return blocks.reshape(3, rows, 2, 3, 128).transpose(1, 3, 0, 2, 4).reshape(rows, 2304)


def unpack_up(blocks, rows):
    return blocks.reshape(4, rows, 768).transpose(1, 0, 2).reshape(rows, 3072)


def shards(tokens, segment_ids, padding_mask, qkv_weight, proj_weight, up_weight, down_weight,
           norm_gain, norm_shift, qv_bias, out_bias, up_bias, cotangent):
    n_dev = lax.axis_size("dp")
    dp, blk = lax.axis_index("dp"), lax.axis_index("blk")
    ring = n_dev == BLOCKS
    n_chips = BLOCKS // 2

    def pick(pair, which):
        return lax.dynamic_index_in_dim(pair, which, 0, keepdims=False)

    tok_own, tok_rx = pick(tokens, blk)[0], swap_rows(pick(tokens, 1 - blk)[0])
    cot_own, cot_send = pick(cotangent, blk)[0], pick(cotangent, 1 - blk)[0]
    seg, pad = pick(segment_ids, blk)[0], pick(padding_mask, blk)[0]
    lanes = jnp.arange(128, dtype=jnp.int32)[None, :]
    code = jnp.where(lanes < 32, seg[:, None] // 32 == lanes, seg[:, None] % 32 + 32 == lanes)
    seg_q = code.astype(BF16)
    allowed = code & (pad[:, None] == 1)
    seg_k = jnp.where(allowed | (lanes >= 64), 0.0, MASKED).astype(BF16)

    if ring:
        qkv_blocks, rest = pack_weights(qkv_weight, proj_weight, up_weight, down_weight, 1)
        small = pack_small(norm_gain, norm_shift, qv_bias, out_bias, up_bias, 48 * dp)
        first = RingGather(jnp.concatenate([qkv_blocks.reshape(144, 768), small], axis=0), 96, n_chips)
        rest = rest.reshape(432, 768)
        for _ in range(4):
            first.step()
            first.arrived()
        rest, _, _ = tie(rest, first.ahead[-1], first.behind[-1])
        parts = first.parts()
        second = RingGather(rest, 192, n_chips)
        order = jnp.asarray(ring_order(n_chips))[dp]
        core = lax.rem(dp, 2)
        chips = jnp.asarray(send_order(n_chips))[dp // 2]
        slots = jnp.asarray(np.argsort(send_order(n_chips), axis=1).astype(np.int32))[dp // 2]
    else:
        whole = [lax.all_gather(w, "dp", axis=0, tiled=True)
                 for w in (qkv_weight, proj_weight, up_weight, down_weight)]
        qkv_blocks, rest = pack_weights(*whole, BLOCKS)
        vectors = [lax.all_gather(w, "dp", axis=1, tiled=True)
                   for w in (norm_gain, norm_shift, qv_bias, out_bias)]
        hidden = lax.all_gather(up_bias, "dp", axis=0, tiled=True)
        small = pack_small(*vectors, hidden, 0)
        small = jnp.concatenate([small[None], jnp.zeros((BLOCKS - 1, 16, 768), BF16)], axis=0)
        parts = split_far(jnp.concatenate([qkv_blocks.reshape(BLOCKS, 144, 768), small], axis=1), 96)
        rest_parts = split_far(rest.reshape(BLOCKS, 432, 768), 192)
        order = jnp.arange(BLOCKS, dtype=jnp.int32)
        core = jnp.int32(0)
        chips = slots = jnp.arange(n_chips, dtype=jnp.int32)
    idx = jnp.concatenate([order, jnp.stack([blk, core]).astype(jnp.int32), chips, slots])
    if ring:
        second.step()
    outs = attn_forward(0, idx, parts, (tok_own, tok_rx), seg_q, seg_k)
    heads, nrm, small_all = [list(outs[:7])], outs[7], outs[8]
    for quad in (1, 2):
        if ring:
            nrm, small_all, heads[-1][3] = second.tie(nrm, small_all, heads[-1][3])
            second.step()
        if quad == 1:
            cot_send, nrm = tie(cot_send, nrm)
            cot_rx = swap_rows(cot_send)
        heads.append(list(attn_forward(quad, idx, parts, (nrm, small_all), seg_q, seg_k)))
    atts = [h[3] for h in heads]
    if ring:
        atts[2], small_all = second.tie(atts[2], small_all)
        second.step()
        atts[2], cot_rx = second.tie(atts[2], cot_rx)
        rest_parts = second.parts()
    lo_mine, lo_theirs, d_mid, d_att, *sends, sums = ffn(
        idx, rest_parts, atts, tok_own, tok_rx, cot_own, cot_rx, small_all)
    lo_rx = swap_rows(lo_theirs)

    groups = ((0,), (1, 2), (3, 4), (5,))
    heads = [[h[0], h[1], h[2], h[3], h[4], h[5], h[6]] for h in heads]
    if ring:
        ffn_sum = RingReduce(*sends, 224, n_chips)
        (d_att,) = ffn_sum.tie(d_att)
        ffn_sum.send()
    d_ni, b0, *q_sends = attn_backward(groups[0], idx, heads, d_att, nrm)
    biases = [b0]
    for group in groups[1:]:
        if ring:
            if group is groups[1]:
                (d_ni,) = ffn_sum.arrived(d_ni)
            else:
                d_ni, lo_rx = ffn_sum.arrived(d_ni, lo_rx)
            ffn_sum.add()
            (d_ni,) = ffn_sum.tie(d_ni)
            ffn_sum.send()
        if group is not groups[-1]:
            d_ni, b, *q_sends = attn_backward(group, idx, heads, d_att, nrm, d_ni, q_sends)
            biases.append(b)
    gt_mine, gt_first, gt_second, *q_sends = attn_backward(
        groups[-1], idx, heads, d_att, nrm, d_ni, q_sends,
        tail=(tok_own, tok_rx, d_mid, small_all, sums, *biases))

    def together(own_half, other_half):
        swapped = blk == 1
        return jnp.stack([jnp.where(swapped, other_half, own_half),
                          jnp.where(swapped, own_half, other_half)])[:, None]

    if ring:
        gt_first, gt_second, *q_sends = ffn_sum.arrived(gt_first, gt_second, *q_sends)
        qkv_sum = RingReduce(*q_sends, None, 80, n_chips)
        gt_first = swap_rows(gt_first)
        qkv_sum.send()
        ffn_sum.add()
        gt_second, ffn_sum.total = qkv_sum.arrived(gt_second, ffn_sum.total)
        gt_second = swap_rows(gt_second)
        qkv_sum.add()
        qkv_sum.send()
        gt_first, ffn_sum.total = qkv_sum.arrived(gt_first, ffn_sum.total)
        ffn_rx = swap_rows(ffn_sum.total)
        qkv_sum.add()
        qkv_sum.send()
        (gt_second,) = qkv_sum.arrived(gt_second)
        qkv_sum.add()
        qkv_sum.send()
        qkv_sum.add()
        gt_rx = jnp.concatenate([gt_first, gt_second])
        out, grad_tokens, ffn_rx, _ = tie(
            together(lo_mine, lo_rx), together(gt_mine, gt_rx), ffn_rx, qkv_sum.total)
        done_ffn = ffn_sum.total.astype(F32) + ffn_rx.astype(F32)
        done_qkv = qkv_sum.total.astype(F32) + swap_rows(qkv_sum.total).astype(F32)
        r = 48
        small = done_qkv[144:160]
        own = lax.dynamic_slice_in_dim(small[0:8], 48 * dp, 48, 1)
        g_bias = lax.dynamic_slice_in_dim(small[8:12].reshape(3072), 192 * dp, 192, 0)
        return (out, grad_tokens,
                unpack_qkv(done_qkv[0:144], r), done_ffn[384:432], unpack_up(done_ffn[0:192], r), done_ffn[192:384],
                own[0:2], own[2:4], own[4:6], own[6:8], g_bias)

    gt_rx = swap_rows(jnp.concatenate([gt_first, gt_second]))

    def whole_sum(mine, *others):
        return jnp.stack([mine, jnp.concatenate(others)], axis=1).reshape(BLOCKS, mine.shape[1], 768)

    def scatter(x, dim):
        part = lax.psum_scatter(x, "dp", scatter_dimension=dim, tiled=True)
        return lax.psum(part.astype(BF16), "blk").astype(F32)

    g_ffn, g_q = whole_sum(*sends), whole_sum(*q_sends)
    g_up = g_ffn[:, 0:192].reshape(BLOCKS, 4, 48, 768).transpose(0, 2, 1, 3).reshape(768, 3072)
    g_down = g_ffn[:, 192:384].reshape(3072, 768)
    g_proj = g_ffn[:, 384:432].reshape(768, 768)
    g_qkv = jnp.stack([g_q[:, 48 * j : 48 * j + 48].reshape(768, 768) for j in range(3)])
    g_small = g_q[0, 144:160].astype(F32)
    g_bias = g_small[8:12].reshape(-1)
    big = [scatter(g.astype(F32), 0) for g in (unpack_qkv(g_qkv, 768), g_proj, g_up, g_down)]
    return (together(lo_mine, lo_rx), together(gt_mine, gt_rx), *big,
            *[scatter(g_small[2 * i : 2 * i + 2], 1) for i in range(4)], scatter(g_bias, 0))


def solution(mesh):
    rows = P(None, "dp", "blk", None)
    return jax.shard_map(
        shards,
        mesh=mesh,
        in_specs=(rows, P(None, "dp", None), P(None, "dp", None)) + (P("dp", None),) * 4
        + (P(None, "dp"),) * 4 + (P("dp"), rows),
        out_specs=(rows, rows) + (P("dp", None),) * 4 + (P(None, "dp"),) * 4 + (P("dp"),),
        check_vma=False,
    )
```
